128 devices in a mesh: ctx: 32 (over x, z, core), head: 4 (over y).
Axes of the slice: x: 4, y: 4, z: 4, core: 2. Of those that a mesh axis runs over, the one named last changes fastest.
Arguments:
- queries: float32 [32768, 2048], P('ctx', 'head'), may hold values from -6 to 6
- keys: float32 [32768, 2048], P('ctx', 'head'), may hold values from -6 to 6
- values: float32 [32768, 2048], P('ctx', 'head'), may hold values from -6 to 6
- gate_logit: float32 [16], P('head'), may hold values from -2 to 2
- out_weight: float32 [2048, 4096], P('head'), may hold values from -0.125 to 0.125
- out_grad: float32 [32768, 4096], P('ctx', 'head'), may hold values from -6 to 6
Outputs:
- query_grad: float32 [32768, 2048], P('ctx', 'head')
- key_grad: float32 [32768, 2048], P('ctx', 'head')
- value_grad: float32 [32768, 2048], P('ctx', 'head')
- weight_grad: float32 [4096, 2048], P('ctx', 'head')
- gate_grad: float32 [16], P('head')
The draws below stay inside these ranges and needn't reach their ends.
All inputs are finite; a program needn't handle non-finite values.
Results may differ from the reference program's by a relative error of at most 0.0003.
Values sent between devices are 32-bit elements; how exact they have to be, the bound alone decides.
No kernel may reach another device: no remote copies, remote signals or barrier semaphores. Data moves between devices by JAX's collectives and lax.ppermute only.
A program may use at most 192 MiB of HBM per device.

```python
import math
import jax
import jax.numpy as jnp
from jax import lax

D = 4096
HEADS = 16
DH = 128
SEG = 1024
TOKENS = 32768


def drawn_rows(key, offset):
    key = jax.random.fold_in(key, 11 + offset)
    return jnp.clip(jax.random.normal(key, (TOKENS, HEADS * DH)), -6.0, 6.0)


def draw_queries(key, part):
    return drawn_rows(key, 0)


def draw_keys(key, part):
    return drawn_rows(key, 1)


def raised(values, own_key, source, target, blocks, factor):
    def block_of(dim):
        return (jnp.arange(values.shape[dim]) // (values.shape[dim] // blocks)).reshape((-1,) + (1,) * (values.ndim - 1 - dim))

    one_side = jax.random.permutation(own_key, blocks)[block_of(target)]
    other_side = (block_of(target) + blocks // 2) % blocks
    return jnp.where((block_of(source) == one_side) | (block_of(source) == other_side), factor * values, values)


def block_levels(own_key, extent, cuts, smallest, largest):
    def one(axis_at, shards_of):
        steps = jax.random.uniform(jax.random.fold_in(jax.random.fold_in(own_key, 6), axis_at), (shards_of,), jnp.float32, smallest / len(cuts), largest / len(cuts))
        return jnp.repeat(jnp.exp(steps), extent[axis_at] // shards_of).reshape((-1,) + (1,) * (len(extent) - axis_at - 1))

    factor_of = one(*cuts[0])
    for cut in cuts[1:]:
        factor_of = factor_of * one(*cut)
    return factor_of


def centred(stream_key, extent, spread, bound, cuts=(), dtype=jnp.bfloat16):
    entries = jax.random.normal(stream_key, extent, jnp.float32) * spread
    if len(cuts) > 0:
        entries = block_levels(stream_key, extent, cuts, -0.22, 0.18) * entries
    return jnp.clip(entries, min=-bound, max=bound).astype(dtype)


def gaussian_with(own_key, shape, spread, bound, pieces, heavy, kind=jnp.bfloat16):
    values = spread * jax.random.normal(own_key, shape, jnp.float32)
    if pieces:
        values = values * block_levels(own_key, shape, pieces, -0.22, 0.18)
    return jnp.clip(raised(values, jax.random.fold_in(own_key, 3), *heavy), -bound, bound).astype(kind)


def setup_inputs(seed: int = 0) -> dict:
    seeds = jax.random.split(jax.random.key(seed), 7)
    queries = draw_queries(jax.random.fold_in(seeds[6], 71), 0)
    keys = draw_keys(jax.random.fold_in(seeds[6], 71), 0)
    values = centred(seeds[2], (TOKENS, HEADS * DH), 1.0, 6.0, ((0, 32), (1, 4)), jnp.float32)
    gate_logit = jnp.clip(jax.random.uniform(seeds[3], (HEADS,), jnp.float32, -2.0, 2.0) * block_levels(seeds[3], (HEADS,), ((0, 4),), -0.4, 0.0), -2.0, 2.0)
    out_weight = centred(seeds[4], (HEADS * DH, D), (HEADS * DH) ** -0.5, 0.125, ((0, 4),), jnp.float32)
    out_grad = gaussian_with(seeds[5], (TOKENS, D), 1.0, 6.0, ((0, 32), (1, 4)), (0, 1, 32, 2.75), jnp.float32)
    return dict(queries=queries, keys=keys, values=values, gate_logit=gate_logit, out_weight=out_weight, out_grad=out_grad)


highest = lax.Precision.HIGHEST

def lifted(inputs):
    return jnp.where(inputs > 0, inputs + 1.0, jnp.exp(jnp.minimum(inputs, 0.0)))

def lifted_slope(inputs):
    return jnp.where(inputs > 0, 1.0, jnp.exp(jnp.minimum(inputs, 0.0)))

def split_heads(flat, segments, heads):
    return flat.reshape(segments, -1, heads, flat.shape[1] // heads).transpose(0, 2, 1, 3)

def join_heads(blocks):
    return blocks.transpose(0, 2, 1, 3).reshape(blocks.shape[0] * blocks.shape[2], blocks.shape[1] * blocks.shape[3])

def earlier_sum(update):
    return jnp.concatenate([jnp.zeros_like(update[:1]), jnp.cumsum(update, axis=0)[:-1]], axis=0)

def later_sum(update):
    flipped = jnp.cumsum(update[::-1], axis=0)[::-1]
    return jnp.concatenate([flipped[1:], jnp.zeros_like(update[:1])], axis=0)

def forward_local(query_block, key_block, value_block, mem_prev, norm_prev):
    lifted_query = lifted(query_block)
    numer = jnp.einsum('nhse,nhef->nhsf', lifted_query, mem_prev, precision=highest)
    denom = jnp.einsum('nhse,nhe->nhs', lifted_query, norm_prev, precision=highest) + 1.0
    memory_out = numer / denom[..., None]
    temper = 1.0 / math.sqrt(query_block.shape[-1])
    scores = jnp.einsum('nhse,nhte->nhst', query_block, key_block, precision=highest) * temper
    length = scores.shape[-1]
    causal = jnp.arange(length)[:, None] >= jnp.arange(length)[None, :]
    scores = jnp.where(causal, scores, -1e+30)
    weights = jnp.exp(scores - lax.optimization_barrier(jnp.max(scores, axis=-1, keepdims=True)))
    weights = weights / lax.optimization_barrier(jnp.sum(weights, axis=-1, keepdims=True))
    local_out = jnp.einsum('nhst,nhtf->nhsf', weights, value_block, precision=highest)
    return (memory_out, denom, weights, local_out)

def backward_local(query_block, key_block, value_block, mem_prev, norm_prev, gating, grad_out, memory_out, denom, weights):
    grad_memory = gating * grad_out
    grad_local = (1.0 - gating) * grad_out
    temper = 1.0 / math.sqrt(query_block.shape[-1])
    grad_weights = jnp.einsum('nhsf,nhtf->nhst', grad_local, value_block, precision=highest)
    grad_value = jnp.einsum('nhst,nhsf->nhtf', weights, grad_local, precision=highest)
    grad_scores = weights * (grad_weights - lax.optimization_barrier(jnp.sum(grad_weights * weights, axis=-1, keepdims=True)))
    grad_query = jnp.einsum('nhst,nhte->nhse', grad_scores, key_block, precision=highest) * temper
    grad_key = jnp.einsum('nhst,nhse->nhte', grad_scores, query_block, precision=highest) * temper
    grad_numer = grad_memory / denom[..., None]
    grad_denom = -lax.optimization_barrier(jnp.sum(grad_memory * memory_out, axis=-1)) / denom
    grad_lift = jnp.einsum('nhsf,nhef->nhse', grad_numer, mem_prev, precision=highest) + grad_denom[..., None] * norm_prev[:, :, None, :]
    grad_query = grad_query + grad_lift * lifted_slope(query_block)
    lifted_query = lifted(query_block)
    grad_mem = jnp.einsum('nhse,nhsf->nhef', lifted_query, grad_numer, precision=highest)
    grad_norm = jnp.einsum('nhse,nhs->nhe', lifted_query, grad_denom, precision=highest)
    return (grad_query, grad_key, grad_value, grad_mem, grad_norm)

def finish_keys(key_block, value_block, grad_key, grad_value, mem_after, norm_after):
    lifted_key = lifted(key_block)
    grad_lift = jnp.einsum('nhsf,nhef->nhse', value_block, mem_after, precision=highest) + norm_after[:, :, None, :]
    grad_key = grad_key + grad_lift * lifted_slope(key_block)
    grad_value = grad_value + jnp.einsum('nhse,nhef->nhsf', lifted_key, mem_after, precision=highest)
    return (grad_key, grad_value)

def per_segment(function, arrays):

    def single(items):
        results = function(*[item[None] for item in items])
        return tuple((result[0] for result in results))
    return lax.map(single, arrays)

def reference(queries, keys, values, gate_logit, out_weight, out_grad):
    segments = TOKENS // SEG
    query_block = split_heads(queries, segments, HEADS)
    key_block = split_heads(keys, segments, HEADS)
    value_block = split_heads(values, segments, HEADS)
    lifted_key = lifted(key_block)
    update = jnp.einsum('nhse,nhsf->nhef', lifted_key, value_block, precision=highest)
    update_norm = lax.optimization_barrier(jnp.sum(lifted_key, axis=2))
    mem_prev = earlier_sum(update)
    norm_prev = earlier_sum(update_norm)

    def forward_parts(query_one, key_one, value_one, mem_one, norm_one):
        memory_out, denom, weights, local_out = forward_local(query_one, key_one, value_one, mem_one, norm_one)
        return (memory_out, denom, local_out)
    memory_out, denom, local_out = per_segment(forward_parts, (query_block, key_block, value_block, mem_prev, norm_prev))
    gating = jax.nn.sigmoid(gate_logit)[None, :, None, None]
    mixed = join_heads(gating * memory_out + (1.0 - gating) * local_out)
    mixed_grad = jnp.dot(out_grad, out_weight.T, precision=highest)
    weight_grad = jnp.dot(out_grad.T, mixed, precision=highest)
    grad_out = split_heads(mixed_grad, segments, HEADS)
    gate_grad = lax.optimization_barrier(jnp.sum(grad_out * (memory_out - local_out), axis=(0, 2, 3))) * jax.nn.sigmoid(gate_logit) * (1.0 - jax.nn.sigmoid(gate_logit))

    def backward_parts(query_one, key_one, value_one, mem_one, norm_one, grad_one, memout_one, denom_one):
        weights = forward_local(query_one, key_one, value_one, mem_one, norm_one)[2]
        return backward_local(query_one, key_one, value_one, mem_one, norm_one, gating, grad_one, memout_one, denom_one, weights)
    grad_query, grad_key, grad_value, grad_mem, grad_norm = per_segment(backward_parts, (query_block, key_block, value_block, mem_prev, norm_prev, grad_out, memory_out, denom))
    mem_after = later_sum(grad_mem)
    norm_after = later_sum(grad_norm)
    grad_key, grad_value = finish_keys(key_block, value_block, grad_key, grad_value, mem_after, norm_after)
    return (join_heads(grad_query), join_heads(grad_key), join_heads(grad_value), weight_grad, gate_grad)
```

```python
import functools
import math

import jax
import jax.numpy as jnp
from jax import lax
from jax.experimental import pallas as pl
from jax.experimental.pallas import tpu as pltpu
from jax.sharding import PartitionSpec as P

SEG = 1024
HEAD = 128
ROWS = 136
FORWARD_QB = 512
BACKWARD_QB = 256
STEP = 256
LIGHT = 2**16
VMEM_LIMIT = 60 * 2**20
MICROSECOND = 3_600_000

f32 = jnp.float32
bf16 = jnp.bfloat16
HIGH = lax.Precision.HIGH


def lifted(x):
    return jnp.where(x > 0, x + 1.0, jnp.exp(jnp.minimum(x, 0.0)))


def lifted_slope(x):
    return jnp.where(x > 0, 1.0, jnp.exp(jnp.minimum(x, 0.0)))


def halves(x):
    hi = x.astype(bf16)
    return hi, (x - hi.astype(f32)).astype(bf16)


def mm(a, b, contract):
    dims = ((contract[:1], contract[1:]), ((), ()))

    def one(x, y):
        return lax.dot_general(x, y, dims, preferred_element_type=f32)

    return one(a[0], b[0]) + (one(a[0], b[1]) + one(a[1], b[0]))


NN = (1, 0)
NT = (1, 1)
TN = (0, 0)


def dot(a, b, contract):
    return lax.dot_general(
        a, b, ((contract[:1], contract[1:]), ((), ())), preferred_element_type=f32
    )


def wide(pair):
    return jnp.concatenate(pair, axis=1)


def doubled(x):
    return jnp.concatenate([x, x], axis=1)


def scores_of(a_wide, b_hi_twice, b_lo):
    return dot(a_wide, b_hi_twice, NT) + dot(a_wide[:, :HEAD], b_lo, NT)


def times_wide(a, b_wide):
    both = dot(a[0], b_wide, NN)
    return both[:, :HEAD] + (both[:, HEAD:] + dot(a[1], b_wide[:, :HEAD], NN))


def tall_times(a_tall, b):
    both = dot(a_tall, b[0], NN)
    return both[:HEAD] + (both[HEAD:] + dot(a_tall[:HEAD], b[1], NN))


def update_kernel(k_ref, v_ref, out_ref):
    lk = lifted(k_ref[...])
    out_ref[0, :HEAD, :] = mm(halves(lk.T), halves(v_ref[...]), NN)
    out_ref[0, HEAD : HEAD + 1, :] = jnp.sum(lk, axis=0, keepdims=True)
    out_ref[0, HEAD + 1 :, :] = jnp.zeros((ROWS - HEAD - 1, HEAD), f32)


LOG2E = math.log2(math.e)
TEMPER = 1.0 / math.sqrt(HEAD)


def parts_of(qb, size):
    return ([(0, qb * size, False)] if qb else []) + [(qb * size, (qb + 1) * size, True)]


def causal(size):
    t = lax.broadcasted_iota(jnp.int32, (size, size), 0)
    return t <= lax.broadcasted_iota(jnp.int32, (size, size), 1)


def forward_kernel(q_ref, k_ref, v_ref, *refs):
    out_ref, lse_ref = refs[-2:]
    key = wide(halves(k_ref[...]))
    value_t = jnp.concatenate(halves(v_ref[...].T), axis=0)
    q_hi, q_lo = halves(q_ref[...] * (TEMPER * LOG2E))
    q_twice = doubled(q_hi)
    seen = causal(FORWARD_QB)
    for qb in range(SEG // FORWARD_QB):
        at = slice(qb * FORWARD_QB, (qb + 1) * FORWARD_QB)
        scores = []
        for low, high, own in parts_of(qb, FORWARD_QB):
            part = scores_of(key[low:high], q_twice[at], q_lo[at])
            scores.append(jnp.where(seen, part, -1e30) if own else part)
        top = functools.reduce(
            jnp.maximum, [jnp.max(part, axis=0, keepdims=True) for part in scores]
        )
        total, out_t = 0.0, 0.0
        for (low, high, _), part in zip(parts_of(qb, FORWARD_QB), scores):
            weights = jnp.exp2(part - top)
            total = total + jnp.sum(weights, axis=0, keepdims=True)
            out_t = out_t + tall_times(value_t[:, low:high], halves(weights))
        out_ref[at, :] = (out_t * (1.0 / total)).T
        lse_ref[0, :, at] = top + jnp.log2(total)


def mix_kernel(q_ref, local_ref, mem_ref, g_ref, hi_ref, lo_ref, memout_ref, lqd_ref):
    g = g_ref[0]
    lq = lifted(q_ref[...])
    norm = mem_ref[0, HEAD : HEAD + 1, :]
    denom = jnp.sum(lq * norm, axis=1, keepdims=True) + 1.0
    inverse = 1.0 / denom
    memory_out = mm(halves(lq), halves(mem_ref[0, :HEAD, :]), NN) * inverse
    memout_ref[...] = memory_out
    mixed = g * memory_out + (1.0 - g) * local_ref[...]
    hi_ref[...], lo_ref[...] = halves(mixed.T)
    lqd_ref[...] = lq * (inverse * g)


def add_weight_part(mixed, block, first, start, mine_ref, send_ref):
    part = mm(mixed, block, NN)
    groups = part.shape[1] // (2 * HEAD)
    for k in range(groups):
        even = part[:, 2 * k * HEAD : (2 * k + 1) * HEAD]
        odd = part[:, (2 * k + 1) * HEAD : (2 * k + 2) * HEAD]
        mine_ref[start + k] += jnp.where(first, even, odd)
        send_ref[start + k] += jnp.where(first, odd, even)


def block_kernel(at_ref, *refs, blocks, added, project, weigh):
    refs = list(refs)

    def take(n):
        taken, refs[:] = refs[:n], refs[n:]
        return taken

    acc, block_refs = take(added), take(blocks)
    w_refs = take(blocks if project else 0)
    mixed_refs = take(2 if weigh else 0)
    out_refs, by_core = take(1 if project else 0), take(2 if weigh else 0)

    @pl.when(pl.program_id(0) == 0)
    def _():
        for n, w_ref in enumerate(w_refs):
            refs[2 * n][...], refs[2 * n + 1][...] = halves(w_ref[...])
        for ref in by_core:
            ref[...] = jnp.zeros_like(ref)

    mixed = tuple(ref[...] for ref in mixed_refs)
    total = acc[0][...] if added else None
    start = 0
    for n, block_ref in enumerate(block_refs):
        block = halves(block_ref[...])
        if project:
            product = mm(block, (refs[2 * n][...], refs[2 * n + 1][...]), NT)
            total = product if total is None else total + product
        if weigh:
            add_weight_part(mixed, block, at_ref[blocks] == 0, start, *by_core)
            start += block_ref.shape[1] // (2 * HEAD)
    if project:
        out_refs[0][...] = total


def tail_kernel(
    at_ref, acc_ref, a_ref, b_ref, wa_ref, wb_ref, lqd_ref, memout_ref, local_ref,
    mg_ref, state_ref, *w,
):
    del at_ref

    @pl.when(pl.program_id(0) == 0)
    def _():
        w[0][...], w[1][...] = halves(wa_ref[...])
        w[2][...], w[3][...] = halves(wb_ref[...])
        state_ref[...] = jnp.zeros_like(state_ref)

    mg = acc_ref[...] + mm(halves(a_ref[...]), (w[0][...], w[1][...]), NT)
    mg = mg + mm(halves(b_ref[...]), (w[2][...], w[3][...]), NT)
    mg_ref[...] = mg
    for h in range(state_ref.shape[0]):
        at = slice(h * HEAD, (h + 1) * HEAD)
        here, lqd, memory_out = mg[:, at], lqd_ref[:, at], memout_ref[:, at]
        state_ref[h, :HEAD, :] += mm(halves(lqd.T), halves(here), NN)
        r = jnp.sum(here * memory_out, axis=1, keepdims=True)
        state_ref[h, HEAD : HEAD + 1, :] -= jnp.sum(lqd * r, axis=0, keepdims=True)
        state_ref[h, HEAD + 1 : HEAD + 2, :] += jnp.sum(
            here * (memory_out - local_ref[:, at]), axis=0, keepdims=True
        )


def rows_of(width):
    return pl.BlockSpec((STEP, width), lambda i, at: (i, 0))


def weight_specs(width, blocks):
    return [
        pl.BlockSpec((width, block.shape[1]), lambda i, at, k=k: (0, at[k]))
        for k, block in enumerate(blocks)
    ]


def round_of(acc, blocks, places, out_weight, mixed, core, project=True, weigh=True, micros=0):
    rows = blocks[0].shape[0]
    width = out_weight.shape[0]
    n = len(blocks)
    groups = sum(block.shape[1] for block in blocks) // (2 * HEAD)
    at = jnp.stack([*places, core]).astype(jnp.int32)
    acc = [] if acc is None else [acc]
    by_core = pl.BlockSpec((groups, width, HEAD), lambda i, at: (0, 0, 0))
    by_core_shape = jax.ShapeDtypeStruct((groups, width, HEAD), f32)
    return pl.pallas_call(
        functools.partial(
            block_kernel, blocks=n, added=len(acc), project=project, weigh=weigh
        ),
        grid_spec=pltpu.PrefetchScalarGridSpec(
            num_scalar_prefetch=1,
            grid=(rows // STEP,),
            in_specs=[rows_of(width) for _ in acc]
            + [rows_of(block.shape[1]) for block in blocks]
            + (weight_specs(width, blocks) if project else [])
            + [pl.BlockSpec((width, STEP), lambda i, at: (0, i))] * (2 if weigh else 0),
            out_specs=[rows_of(width)] * project + [by_core] * (2 * weigh),
            scratch_shapes=[
                pltpu.VMEM((width, block.shape[1]), bf16) for block in blocks for _ in range(2)
            ]
            * project,
        ),
        out_shape=[jax.ShapeDtypeStruct((rows, width), f32)] * project
        + [by_core_shape] * (2 * weigh),
        compiler_params=pltpu.CompilerParams(vmem_limit_bytes=VMEM_LIMIT),
        cost_estimate=pl.CostEstimate(
            flops=LIGHT, bytes_accessed=micros * MICROSECOND or LIGHT, transcendentals=0
        ),
        name="round",
    )(at, *acc, *blocks, *([out_weight] * n if project else []), *(mixed if weigh else []))


def tail_of(acc, blocks, places, out_weight, lqd, memory_out, local_out):
    rows, deep = blocks[0].shape
    width = out_weight.shape[0]
    heads = width // HEAD
    whole = pl.BlockSpec((heads, ROWS, HEAD), lambda i, at: (0, 0, 0))
    return pl.pallas_call(
        tail_kernel,
        grid_spec=pltpu.PrefetchScalarGridSpec(
            num_scalar_prefetch=1,
            grid=(rows // STEP,),
            in_specs=[rows_of(width)]
            + [rows_of(deep)] * 2
            + weight_specs(width, blocks)
            + [rows_of(width)] * 3,
            out_specs=[rows_of(width), whole],
            scratch_shapes=[pltpu.VMEM((width, deep), bf16) for _ in range(4)],
        ),
        out_shape=[
            jax.ShapeDtypeStruct((rows, width), f32),
            jax.ShapeDtypeStruct((heads, ROWS, HEAD), f32),
        ],
        compiler_params=pltpu.CompilerParams(vmem_limit_bytes=VMEM_LIMIT),
        cost_estimate=pl.CostEstimate(flops=LIGHT, bytes_accessed=LIGHT, transcendentals=0),
        name="tail",
    )(
        jnp.stack(places).astype(jnp.int32),
        acc, *blocks, out_weight, out_weight, lqd, memory_out, local_out,
    )


def backward_kernel(
    q_ref, k_ref, v_ref, mg_ref, local_ref, memout_ref, lse_ref, mem_ref, g_ref, *refs
):
    dq_ref, dk_ref, dv_ref = refs[-3:]
    g = g_ref[0]
    q = q_ref[...]
    mg = mg_ref[...]
    local_grad = (1.0 - g) * TEMPER * mg
    key = halves(k_ref[...])
    key_t = jnp.concatenate([key[0].T, key[1].T], axis=0)
    key = wide(key)
    value = wide(halves(v_ref[...]))
    query = halves(q * (TEMPER * LOG2E))
    q_twice, q_wide = doubled(query[0]), wide(query)
    grad = halves(local_grad)
    g_twice, g_wide = doubled(grad[0]), wide(grad)
    delta = jnp.sum((local_grad * local_ref[...]).T, axis=0, keepdims=True)
    lq = lifted(q)
    norm = mem_ref[0, HEAD : HEAD + 1, :]
    inverse = 1.0 / (jnp.sum(lq * norm, axis=1, keepdims=True) + 1.0)
    r = jnp.sum(mg * memout_ref[...], axis=1, keepdims=True)
    lift_grad = mm(halves(mg), halves(mem_ref[0, :HEAD, :].T), NN) - r * norm
    dq_ref[...] = lift_grad * (inverse * g) * lifted_slope(q)
    dk_ref[...] = jnp.zeros((SEG, HEAD), f32)
    dv_ref[...] = jnp.zeros((SEG, HEAD), f32)
    seen = causal(BACKWARD_QB)
    for qb in range(SEG // BACKWARD_QB):
        at = slice(qb * BACKWARD_QB, (qb + 1) * BACKWARD_QB)
        dq_t = 0.0
        for low, high, own in parts_of(qb, BACKWARD_QB):
            scores = scores_of(key[low:high], q_twice[at], query[1][at])
            if own:
                scores = jnp.where(seen, scores, -1e30)
            weights = jnp.exp2(scores - lse_ref[0, :, at])
            dp = scores_of(value[low:high], g_twice[at], grad[1][at])
            ds = halves(weights * (dp - delta[:, at]))
            dv_ref[low:high, :] += times_wide(halves(weights), g_wide[at])
            dk_ref[low:high, :] += times_wide(ds, q_wide[at])
            dq_t = dq_t + tall_times(key_t[:, low:high], ds)
        dq_ref[at, :] += dq_t.T
    dk_ref[...] = dk_ref[...] * (1.0 / (TEMPER * LOG2E))
    dv_ref[...] = dv_ref[...] * (1.0 / TEMPER)


def one_head(kernel, head, earlier, ins, kinds, outs, micros, name):
    width = ins[0].shape[1]
    heads = width // HEAD
    column = pl.BlockSpec((SEG, HEAD), lambda i: (0, head))

    def of_head(shape):
        return pl.BlockSpec((1, *shape[1:]), lambda i: (head, 0, 0))

    shapes = {"c": (SEG, width), "l": (heads, 1, SEG)}
    return pl.pallas_call(
        kernel,
        grid=(1,),
        in_specs=[column if k == "c" else of_head(x.shape) for k, x in zip(kinds, ins)]
        + [pl.BlockSpec(memory_space=pl.ANY)] * len(earlier),
        out_specs=[column if k == "c" else of_head(shapes[k]) for k in outs],
        out_shape=[jax.ShapeDtypeStruct(shapes[k], f32) for k in outs],
        input_output_aliases={len(ins) + i: i for i in range(len(earlier))},
        compiler_params=pltpu.CompilerParams(vmem_limit_bytes=VMEM_LIMIT),
        cost_estimate=pl.CostEstimate(
            flops=LIGHT, bytes_accessed=micros * MICROSECOND or LIGHT, transcendentals=0
        ),
        name=name,
    )(*ins, *earlier)


def finish_kernel(k_ref, v_ref, dk_ref, dv_ref, state_ref, kg_ref, vg_ref):
    key = k_ref[...]
    state = state_ref[0, :HEAD, :]
    norm = state_ref[0, HEAD : HEAD + 1, :]
    lift_grad = mm(halves(v_ref[...]), halves(state.T), NN) + norm
    kg_ref[...] = dk_ref[...] + lift_grad * lifted_slope(key)
    vg_ref[...] = dv_ref[...] + mm(halves(lifted(key)), halves(state), NN)


def columns():
    return pl.BlockSpec((SEG, HEAD), lambda h: (0, h))


def state():
    return pl.BlockSpec((1, ROWS, HEAD), lambda h: (h, 0, 0))


def row(width):
    return pl.BlockSpec((1, 1, width), lambda h: (h, 0, 0))


def per_head(kernel, heads, ins, outs, name):
    width = heads * HEAD
    kinds = {
        "c": (columns(), jax.ShapeDtypeStruct((SEG, width), f32)),
        "s": (state(), jax.ShapeDtypeStruct((heads, ROWS, HEAD), f32)),
        "g": (row(HEAD), jax.ShapeDtypeStruct((heads, 1, HEAD), f32)),
        "t": (
            pl.BlockSpec((HEAD, SEG), lambda h: (h, 0)),
            jax.ShapeDtypeStruct((width, SEG), bf16),
        ),
        "l": (row(SEG), jax.ShapeDtypeStruct((heads, 1, SEG), f32)),
    }
    return pl.pallas_call(
        kernel,
        grid=(heads,),
        in_specs=[kinds[i][0] for i in ins],
        out_specs=[kinds[o][0] for o in outs],
        out_shape=[kinds[o][1] for o in outs],
        compiler_params=pltpu.CompilerParams(vmem_limit_bytes=VMEM_LIMIT),
        cost_estimate=pl.CostEstimate(
            flops=LIGHT, bytes_accessed=LIGHT, transcendentals=0
        ),
        name=name,
    )


def ring(n, step):
    return [(i, (i + step) % n) for i in range(n)]


def grid_sizes():
    heads = lax.axis_size("head")
    return heads, lax.axis_size("ctx") // (2 * heads)


def place():
    xs, zs = grid_sizes()
    at = lax.axis_index("ctx")
    return at // (2 * zs), (at // 2) % zs, at % 2


def core_swap(block):
    n = lax.axis_size("ctx")
    return lax.ppermute(block, "ctx", [(i, i ^ 1) for i in range(n)])


def moved(block, axis, to):
    xs, zs = grid_sizes()
    pairs = []
    for x in range(xs):
        for z in range(zs):
            x_to, z_to = (to(x), z) if axis == "x" else (x, to(z))
            if x_to is not None and z_to is not None:
                for c in range(2):
                    pairs.append(((x * zs + z) * 2 + c, (x_to * zs + z_to) * 2 + c))
    return lax.ppermute(block, "ctx", pairs)


def scan_of_four(block, axis, at, later, beside_first, beside_second):
    near = beside_first(moved(block, axis, lambda i: i ^ 1))
    pair = block + near
    other = beside_second(moved(pair, axis, lambda i: 3 - i))
    counts_near = (at % 2 == 0) if later else (at % 2 == 1)
    counts_other = (at < 2) if later else (at >= 2)
    return jnp.where(counts_near, near, 0.0) + jnp.where(counts_other, other, 0.0), pair + other


def scan_over_ctx(packed, later, work=None):
    xs, zs = grid_sizes()
    x, z, core = place()
    half = packed.shape[0] // 2
    first, second = packed[:half], packed[half:]
    is_first = core == 0
    mine = jnp.where(is_first, first, second)
    theirs = core_swap(jnp.where(is_first, second, first))
    chip = mine + theirs

    def beside_step(i):
        def tie(arrived):
            if work is None:
                return arrived
            done = work(i)
            arrived, *done[:] = lax.optimization_barrier((arrived, *done))
            return arrived

        return tie

    before_z, total_z = scan_of_four(chip, "z", z, later, beside_step(0), beside_step(1))
    before_x, total = scan_of_four(
        total_z, "x", x, later, beside_step(2), beside_step(3)
    )
    outside = before_z + before_x
    counts_other = is_first if later else jnp.logical_not(is_first)
    for_me = outside + jnp.where(counts_other, theirs, 0.0)
    for_other = outside + jnp.where(counts_other, 0.0, mine)
    row = lax.broadcasted_iota(jnp.int32, (1, ROWS, 1), 1)
    totals = jnp.where(row == ROWS - 1, total[:, HEAD + 1 : HEAD + 2, :], 0.0)
    for_me, for_other = for_me + totals, for_other + totals
    swapped = core_swap(for_other)
    low = jnp.where(is_first, for_me, swapped)
    high = jnp.where(is_first, swapped, for_me)
    return jnp.concatenate([low, high], axis=0)


def across(i):
    return 3 - i


def beside(i):
    return i ^ 1


def scattered_of_four(piece, axis, at, first=across, second=beside):
    far = first(at)
    sent = moved(jnp.stack([piece(far), piece(second(far))]), axis, first)
    kept, passed = piece(at) + sent[0], piece(second(at)) + sent[1]
    return kept + moved(passed, axis, second)


def at_place(pieces, i):
    return lax.dynamic_index_in_dim(pieces, i, 0, keepdims=False)


def reduced_on_x(block, distance):
    xs, zs = grid_sizes()
    x, z, core = place()
    hs = lax.axis_size("head")
    head = lax.axis_index("head")
    total = jnp.where(x == (head + hs - distance) % hs, block, 0.0)
    for step in range(1, xs):
        pairs = []
        for h in range(hs):
            to = (h - distance) % hs
            source = (to - step) % xs
            for i in range(2 * zs):
                pairs.append(((source * 2 * zs + i) * hs + h, (to * 2 * zs + i) * hs + h))
        total = total + lax.ppermute(block, ("ctx", "head"), pairs)
    return total


def on_device(queries, keys, values, gate_logit, out_weight, out_grad):
    heads = gate_logit.shape[0]
    width = heads * HEAD
    hs = lax.axis_size("head")
    head = lax.axis_index("head")
    xs, zs = grid_sizes()
    x, z, core = place()
    rows, cols = out_grad.shape

    half, quarter = cols // 2, cols // 4

    def up(block):
        return lax.ppermute(block, "head", ring(hs, 1))

    def down(block):
        return lax.ppermute(block, "head", ring(hs, -1))

    left, right = up(out_grad), down(out_grad)
    far_a1, far_b1 = up(left[:, :quarter]), down(right[:, half : half + quarter])
    rest_a, rest_b, far_a1, far_b1 = lax.optimization_barrier(
        (left[:, quarter:half], right[:, half + quarter :], far_a1, far_b1)
    )
    far_a2, far_b2 = up(rest_a), down(rest_b)

    gate = jax.nn.sigmoid(gate_logit)
    g = jnp.broadcast_to(gate[:, None, None], (heads, 1, HEAD))

    (packed,) = per_head(update_kernel, heads, "cc", "s", "update")(keys, values)
    forwards = []

    def forward(head):
        ins = (queries, keys, values)
        forwards[:] = one_head(forward_kernel, head, forwards, ins, "ccc", "cl", 0, "forward")
        return forwards

    before = scan_over_ctx(packed, False, forward)
    local_out, lse = forwards
    *mixed, memory_out, lqd = per_head(mix_kernel, heads, "ccsg", "ttcc", "mix")(
        queries, local_out, before, g
    )

    def block_at(distance):
        return (head + hs - distance) % hs

    own_at, left_at, far_at, right_at = (block_at(d) for d in range(4))
    add = functools.partial(round_of, out_weight=out_weight, mixed=mixed, core=core)

    def summed_on_z(mine, send, *order):
        came = core_swap(send)
        return scattered_of_four(lambda i: at_place(mine, i) + at_place(came, i), "z", z, *order)

    mg, mine_own, send_own = add(None, [out_grad], [own_at])
    sum_own = summed_on_z(mine_own, send_own)
    left, right, sum_own = lax.optimization_barrier((left, right, sum_own))
    mg, mine_left, send_left = add(mg, [left], [left_at])
    right, far_a1, far_b1, mine_left, send_left = lax.optimization_barrier(
        (right, far_a1, far_b1, mine_left, send_left)
    )
    sum_left = summed_on_z(mine_left, send_left, across, beside)
    mg, mine_right, send_right = add(mg, [right], [right_at])
    sum_right = summed_on_z(mine_right, send_right, beside, across)
    mg, mine_1, send_1 = add(mg, [far_a1, far_b1], [4 * far_at, 4 * far_at + 2])
    far_a2, far_b2, sum_own, sum_left, sum_right = lax.optimization_barrier(
        (far_a2, far_b2, sum_own, sum_left, sum_right)
    )
    mg, back = tail_of(
        mg, [far_a2, far_b2], [4 * far_at + 1, 4 * far_at + 3], out_weight,
        lqd, memory_out, local_out,
    )
    far_a2, far_b2, back = lax.optimization_barrier((far_a2, far_b2, back))
    mine_2, send_2 = add(None, [far_a2, far_b2], [far_at, far_at], project=False, micros=4)

    grads = []

    def backward(head):
        ins = (queries, keys, values, mg, local_out, memory_out, lse, before, g)
        grads[:] = one_head(backward_kernel, head, grads, ins, "ccccccl" + "sg", "ccc", 5, "backward")
        return grads

    after = scan_over_ctx(back, True, backward)
    dq, dk, dv = grads

    parts = jnp.stack([sum_own, sum_left, jnp.zeros_like(sum_own), sum_right])

    def piece_x(i):
        return at_place(parts, (head + hs - i) % hs)

    early = scattered_of_four(piece_x, "x", x)

    def far_sum(mine, send, odd):
        chip = mine + core_swap(send)
        pair = z // 2
        kept = at_place(chip, pair) + moved(at_place(chip, 1 - pair), "z", across)
        return kept + moved(kept, "z", lambda i: (i ^ 1) if i % 2 != odd else None)

    far_block = jnp.where(z % 2 == 0, far_sum(mine_1, send_1, 0), far_sum(mine_2, send_2, 1))
    weight_grad = (early + reduced_on_x(far_block, 2)).T
    is_first = core == 0

    key_grad, value_grad = per_head(finish_kernel, heads, "ccccs", "cc", "finish")(
        keys, values, dk, dv, after
    )

    gate_sum = jnp.sum(after[:, ROWS - 1, :], axis=-1)
    gate_grad = gate_sum * gate * (1.0 - gate)
    return dq, key_grad, value_grad, weight_grad, gate_grad


def solution(mesh):
    in_specs = (
        P("ctx", "head"),
        P("ctx", "head"),
        P("ctx", "head"),
        P("head"),
        P("head", None),
        P("ctx", "head"),
    )
    out_specs = (P("ctx", "head"), P("ctx", "head"), P("ctx", "head"), P("ctx", "head"), P("head"))
    return jax.shard_map(
        on_device, mesh=mesh, in_specs=in_specs, out_specs=out_specs, check_vma=False
    )
```

```python
import functools
import math

import jax
import jax.numpy as jnp
from jax import lax
from jax.experimental import pallas as pl
from jax.experimental.pallas import tpu as pltpu
from jax.sharding import PartitionSpec as P

SEG = 1024
HEAD = 128
ROWS = 136
FORWARD_QB = 512
BACKWARD_QB = 256
HALF = SEG // 2
STEP = 256
LIGHT = 2**16
VMEM_LIMIT = 60 * 2**20
MICROSECOND = 3_600_000

f32 = jnp.float32
bf16 = jnp.bfloat16
HIGH = lax.Precision.HIGH


def lifted(x):
    return jnp.where(x > 0, x + 1.0, jnp.exp(jnp.minimum(x, 0.0)))


def lifted_slope(x):
    return jnp.where(x > 0, 1.0, jnp.exp(jnp.minimum(x, 0.0)))


def halves(x):
    hi = x.astype(bf16)
    return hi, (x - hi.astype(f32)).astype(bf16)


def mm(a, b, contract):
    dims = ((contract[:1], contract[1:]), ((), ()))

    def one(x, y):
        return lax.dot_general(x, y, dims, preferred_element_type=f32)

    return one(a[0], b[0]) + (one(a[0], b[1]) + one(a[1], b[0]))


NN = (1, 0)
NT = (1, 1)
TN = (0, 0)


def dot(a, b, contract):
    return lax.dot_general(
        a, b, ((contract[:1], contract[1:]), ((), ())), preferred_element_type=f32
    )


def wide(pair):
    return jnp.concatenate(pair, axis=1)


def doubled(x):
    return jnp.concatenate([x, x], axis=1)


def scores_of(a_wide, b_hi_twice, b_lo):
    return dot(a_wide, b_hi_twice, NT) + dot(a_wide[:, :HEAD], b_lo, NT)


def times_wide(a, b_wide):
    both = dot(a[0], b_wide, NN)
    return both[:, :HEAD] + (both[:, HEAD:] + dot(a[1], b_wide[:, :HEAD], NN))


def tall_times(a_tall, b):
    both = dot(a_tall, b[0], NN)
    return both[:HEAD] + (both[HEAD:] + dot(a_tall[:HEAD], b[1], NN))


def update_kernel(k_ref, v_ref, out_ref):
    lk = lifted(k_ref[...])
    out_ref[0, :HEAD, :] = mm(halves(lk.T), halves(v_ref[...]), NN)
    out_ref[0, HEAD : HEAD + 1, :] = jnp.sum(lk, axis=0, keepdims=True)
    out_ref[0, HEAD + 1 :, :] = jnp.zeros((ROWS - HEAD - 1, HEAD), f32)


LOG2E = math.log2(math.e)
TEMPER = 1.0 / math.sqrt(HEAD)


def parts_of(qb, size):
    return ([(0, qb * size, False)] if qb else []) + [(qb * size, (qb + 1) * size, True)]


def causal(size):
    t = lax.broadcasted_iota(jnp.int32, (size, size), 0)
    return t <= lax.broadcasted_iota(jnp.int32, (size, size), 1)


def forward_kernel(q_ref, k_ref, v_ref, *refs):
    out_ref, lse_ref = refs[-2:]
    key = wide(halves(k_ref[...]))
    value_t = jnp.concatenate(halves(v_ref[...].T), axis=0)
    q_hi, q_lo = halves(q_ref[...] * (TEMPER * LOG2E))
    q_twice = doubled(q_hi)
    seen = causal(FORWARD_QB)
    for qb in range(SEG // FORWARD_QB):
        at = slice(qb * FORWARD_QB, (qb + 1) * FORWARD_QB)
        scores = []
        for low, high, own in parts_of(qb, FORWARD_QB):
            part = scores_of(key[low:high], q_twice[at], q_lo[at])
            scores.append(jnp.where(seen, part, -1e30) if own else part)
        top = functools.reduce(
            jnp.maximum, [jnp.max(part, axis=0, keepdims=True) for part in scores]
        )
        total, out_t = 0.0, 0.0
        for (low, high, _), part in zip(parts_of(qb, FORWARD_QB), scores):
            weights = jnp.exp2(part - top)
            total = total + jnp.sum(weights, axis=0, keepdims=True)
            out_t = out_t + tall_times(value_t[:, low:high], halves(weights))
        out_ref[at, :] = (out_t * (1.0 / total)).T
        lse_ref[0, :, at] = top + jnp.log2(total)


def mix_kernel(q_ref, local_ref, mem_ref, g_ref, hi_ref, lo_ref, memout_ref, lqd_ref):
    g = g_ref[0]
    lq = lifted(q_ref[...])
    norm = mem_ref[0, HEAD : HEAD + 1, :]
    denom = jnp.sum(lq * norm, axis=1, keepdims=True) + 1.0
    inverse = 1.0 / denom
    memory_out = mm(halves(lq), halves(mem_ref[0, :HEAD, :]), NN) * inverse
    memout_ref[...] = memory_out
    mixed = g * memory_out + (1.0 - g) * local_ref[...]
    hi_ref[...], lo_ref[...] = halves(mixed.T)
    lqd_ref[...] = lq * (inverse * g)


def add_weight_part(mixed, block, first, start, mine_ref, send_ref):
    part = mm(mixed, block, NN)
    groups = part.shape[1] // (2 * HEAD)
    for k in range(groups):
        even = part[:, 2 * k * HEAD : (2 * k + 1) * HEAD]
        odd = part[:, (2 * k + 1) * HEAD : (2 * k + 2) * HEAD]
        mine_ref[start + k] += jnp.where(first, even, odd)
        send_ref[start + k] += jnp.where(first, odd, even)


def block_kernel(at_ref, *refs, blocks, added, project, weigh, summed):
    refs = list(refs)

    def take(n):
        taken, refs[:] = refs[:n], refs[n:]
        return taken

    acc, block_refs = take(added), take(blocks)
    w_refs = take(blocks if project else 0)
    mixed_refs = take(2 if weigh else 0)
    before = take(2 if summed else 0)
    out_refs, by_core = take(1 if project else 0), take(2 if weigh else 0)

    @pl.when(pl.program_id(0) == 0)
    def _():
        for n, w_ref in enumerate(w_refs):
            refs[2 * n][...], refs[2 * n + 1][...] = halves(w_ref[...])
        for n, ref in enumerate(by_core):
            ref[...] = before[n][...] if summed else jnp.zeros_like(ref)

    mixed = tuple(ref[...] for ref in mixed_refs)
    total = acc[0][...] if added else None
    start = 0
    for n, block_ref in enumerate(block_refs):
        block = halves(block_ref[...])
        if project:
            product = mm(block, (refs[2 * n][...], refs[2 * n + 1][...]), NT)
            total = product if total is None else total + product
        if weigh:
            add_weight_part(mixed, block, at_ref[blocks] == 0, start, *by_core)
            start += block_ref.shape[1] // (2 * HEAD)
    if project:
        out_refs[0][...] = total


def tail_kernel(at_ref, *refs):
    del at_ref
    acc_ref, a_ref, b_ref, wa_ref, wb_ref, lqd_ref, memout_ref, local_ref, *before = refs[:-6]
    mg_ref, state_ref, *w = refs[-6:]

    @pl.when(pl.program_id(0) == 0)
    def _():
        w[0][...], w[1][...] = halves(wa_ref[...])
        w[2][...], w[3][...] = halves(wb_ref[...])
        state_ref[...] = before[0][...] if before else jnp.zeros_like(state_ref)

    mg = acc_ref[...] + mm(halves(a_ref[...]), (w[0][...], w[1][...]), NT)
    mg = mg + mm(halves(b_ref[...]), (w[2][...], w[3][...]), NT)
    mg_ref[...] = mg
    for h in range(state_ref.shape[0]):
        at = slice(h * HEAD, (h + 1) * HEAD)
        here, lqd, memory_out = mg[:, at], lqd_ref[:, at], memout_ref[:, at]
        state_ref[h, :HEAD, :] += mm(halves(lqd.T), halves(here), NN)
        r = jnp.sum(here * memory_out, axis=1, keepdims=True)
        state_ref[h, HEAD : HEAD + 1, :] -= jnp.sum(lqd * r, axis=0, keepdims=True)
        state_ref[h, HEAD + 1 : HEAD + 2, :] += jnp.sum(
            here * (memory_out - local_ref[:, at]), axis=0, keepdims=True
        )


def rows_of(width, first=0):
    return pl.BlockSpec((STEP, width), lambda i, at: (i + first // STEP, 0))


def weight_specs(width, blocks):
    return [
        pl.BlockSpec((width, block.shape[1]), lambda i, at, k=k: (0, at[k]))
        for k, block in enumerate(blocks)
    ]


def round_of(
    acc, blocks, places, out_weight, mixed, core, project=True, weigh=True, micros=0, first=0, before=()
):
    rows = blocks[0].shape[0]
    width = out_weight.shape[0]
    n = len(blocks)
    groups = sum(block.shape[1] for block in blocks) // (2 * HEAD)
    at = jnp.stack([*places, core]).astype(jnp.int32)
    acc = [] if acc is None else [acc]
    by_core = pl.BlockSpec((groups, width, HEAD), lambda i, at: (0, 0, 0))
    by_core_shape = jax.ShapeDtypeStruct((groups, width, HEAD), f32)
    return pl.pallas_call(
        functools.partial(
            block_kernel,
            blocks=n,
            added=len(acc),
            project=project,
            weigh=weigh,
            summed=len(before) > 0,
        ),
        grid_spec=pltpu.PrefetchScalarGridSpec(
            num_scalar_prefetch=1,
            grid=(rows // STEP,),
            in_specs=[rows_of(width) for _ in acc]
            + [rows_of(block.shape[1]) for block in blocks]
            + (weight_specs(width, blocks) if project else [])
            + [pl.BlockSpec((width, STEP), lambda i, at: (0, i + first // STEP))] * (2 * weigh)
            + [by_core] * len(before),
            out_specs=[rows_of(width)] * project + [by_core] * (2 * weigh),
            scratch_shapes=[
                pltpu.VMEM((width, block.shape[1]), bf16) for block in blocks for _ in range(2)
            ]
            * project,
        ),
        out_shape=[jax.ShapeDtypeStruct((rows, width), f32)] * project
        + [by_core_shape] * (2 * weigh),
        compiler_params=pltpu.CompilerParams(vmem_limit_bytes=VMEM_LIMIT),
        cost_estimate=pl.CostEstimate(
            flops=LIGHT, bytes_accessed=micros * MICROSECOND or LIGHT, transcendentals=0
        ),
        name="round",
    )(at, *acc, *blocks, *([out_weight] * n if project else []), *(mixed if weigh else []), *before)


def tail_of(second, acc, blocks, places, out_weight, whole, before):
    rows, deep = blocks[0].shape
    width = out_weight.shape[0]
    first = second * HALF
    state_shape = (width // HEAD, ROWS, HEAD)
    states = pl.BlockSpec(state_shape, lambda i, at: (0, 0, 0))
    return pl.pallas_call(
        tail_kernel,
        grid_spec=pltpu.PrefetchScalarGridSpec(
            num_scalar_prefetch=1,
            grid=(rows // STEP,),
            in_specs=[rows_of(width, first)]
            + [rows_of(deep)] * 2
            + weight_specs(width, blocks)
            + [rows_of(width, first)] * 3
            + [states] * len(before),
            out_specs=[rows_of(width), states],
            scratch_shapes=[pltpu.VMEM((width, deep), bf16) for _ in range(4)],
        ),
        out_shape=[
            jax.ShapeDtypeStruct((rows, width), f32),
            jax.ShapeDtypeStruct(state_shape, f32),
        ],
        compiler_params=pltpu.CompilerParams(vmem_limit_bytes=VMEM_LIMIT),
        cost_estimate=pl.CostEstimate(flops=LIGHT, bytes_accessed=LIGHT, transcendentals=0),
        name="tail",
    )(
        jnp.stack(places).astype(jnp.int32),
        acc, *blocks, out_weight, out_weight, *whole, *before,
    )


def backward_kernel(*refs, first):
    q_ref, k_ref, v_ref, mg_ref, local_ref, memout_ref, lse_ref, mem_ref, g_ref = refs[:9]
    dq_ref, dk_ref, dv_ref = refs[-3:]
    g = g_ref[0]
    q = q_ref[...]
    mg = mg_ref[...]
    local_grad = (1.0 - g) * TEMPER * mg
    key = halves(k_ref[...])
    key_t = jnp.concatenate([key[0].T, key[1].T], axis=0)
    key = wide(key)
    value = wide(halves(v_ref[...]))
    query = halves(q * (TEMPER * LOG2E))
    q_twice, q_wide = doubled(query[0]), wide(query)
    grad = halves(local_grad)
    g_twice, g_wide = doubled(grad[0]), wide(grad)
    delta = jnp.sum((local_grad * local_ref[...]).T, axis=0, keepdims=True)
    lq = lifted(q)
    norm = mem_ref[0, HEAD : HEAD + 1, :]
    inverse = 1.0 / (jnp.sum(lq * norm, axis=1, keepdims=True) + 1.0)
    r = jnp.sum(mg * memout_ref[...], axis=1, keepdims=True)
    lift_grad = mm(halves(mg), halves(mem_ref[0, :HEAD, :].T), NN) - r * norm
    dq_ref[...] = lift_grad * (inverse * g) * lifted_slope(q)
    for ref, before in zip((dk_ref, dv_ref), refs[9:11] if first else (None, None)):
        ref[first:, :] = jnp.zeros((HALF, HEAD), f32)
        if first:
            ref[:first, :] = before[...]
    seen = causal(BACKWARD_QB)
    for qb in range(HALF // BACKWARD_QB):
        at = slice(qb * BACKWARD_QB, (qb + 1) * BACKWARD_QB)
        dq_t = 0.0
        for low, high, own in parts_of(qb + first // BACKWARD_QB, BACKWARD_QB):
            scores = scores_of(key[low:high], q_twice[at], query[1][at])
            if own:
                scores = jnp.where(seen, scores, -1e30)
            weights = jnp.exp2(scores - lse_ref[0, :, at])
            dp = scores_of(value[low:high], g_twice[at], grad[1][at])
            ds = halves(weights * (dp - delta[:, at]))
            dv_ref[low:high, :] += times_wide(halves(weights), g_wide[at])
            dk_ref[low:high, :] += times_wide(ds, q_wide[at])
            dq_t = dq_t + tall_times(key_t[:, low:high], ds)
        dq_ref[at, :] += dq_t.T
    if first:
        dk_ref[...] = dk_ref[...] * (1.0 / (TEMPER * LOG2E))
        dv_ref[...] = dv_ref[...] * (1.0 / TEMPER)


def backward_of(second, heads, ins, before, earlier, micros):
    width = ins[0].shape[1]
    low, count = heads

    def rows(n, at=0):
        return pl.BlockSpec((n, HEAD), lambda h: (at, h + low))

    def of_head(x, n=None, at=0):
        return pl.BlockSpec((1, x.shape[1], n or x.shape[2]), lambda h: (h + low, 0, at))

    here = rows(HALF, second)
    seen = rows(SEG if second else HALF)
    shapes = [(SEG, width)] + [(SEG if second else HALF, width)] * 2
    return pl.pallas_call(
        functools.partial(backward_kernel, first=second * HALF),
        grid=(count,),
        in_specs=[here, seen, seen, rows(HALF), here, here]
        + [of_head(ins[6], HALF, second), of_head(ins[7]), of_head(ins[8])]
        + [rows(HALF)] * len(before)
        + [pl.BlockSpec(memory_space=pl.ANY)] * len(earlier),
        out_specs=[here, seen, seen],
        out_shape=[jax.ShapeDtypeStruct(shape, f32) for shape in shapes],
        input_output_aliases={len(ins) + len(before) + i: i for i in range(len(earlier))},
        compiler_params=pltpu.CompilerParams(vmem_limit_bytes=VMEM_LIMIT),
        cost_estimate=pl.CostEstimate(
            flops=LIGHT, bytes_accessed=micros * MICROSECOND or LIGHT, transcendentals=0
        ),
        name="backward",
    )(*ins, *before, *earlier)


def forward_of(heads, ins, earlier):
    width = ins[0].shape[1]
    low, count = heads
    column = pl.BlockSpec((SEG, HEAD), lambda h: (0, h + low))
    line = pl.BlockSpec((1, 1, SEG), lambda h: (h + low, 0, 0))
    return pl.pallas_call(
        forward_kernel,
        grid=(count,),
        in_specs=[column] * 3 + [pl.BlockSpec(memory_space=pl.ANY)] * len(earlier),
        out_specs=[column, line],
        out_shape=[
            jax.ShapeDtypeStruct((SEG, width), f32),
            jax.ShapeDtypeStruct((width // HEAD, 1, SEG), f32),
        ],
        input_output_aliases={len(ins) + i: i for i in range(len(earlier))},
        compiler_params=pltpu.CompilerParams(vmem_limit_bytes=VMEM_LIMIT),
        cost_estimate=pl.CostEstimate(flops=LIGHT, bytes_accessed=LIGHT, transcendentals=0),
        name="forward",
    )(*ins, *earlier)


def finish_kernel(k_ref, v_ref, dk_ref, dv_ref, state_ref, kg_ref, vg_ref):
    key = k_ref[...]
    state = state_ref[0, :HEAD, :]
    norm = state_ref[0, HEAD : HEAD + 1, :]
    lift_grad = mm(halves(v_ref[...]), halves(state.T), NN) + norm
    kg_ref[...] = dk_ref[...] + lift_grad * lifted_slope(key)
    vg_ref[...] = dv_ref[...] + mm(halves(lifted(key)), halves(state), NN)


def columns():
    return pl.BlockSpec((SEG, HEAD), lambda h: (0, h))


def state():
    return pl.BlockSpec((1, ROWS, HEAD), lambda h: (h, 0, 0))


def row(width):
    return pl.BlockSpec((1, 1, width), lambda h: (h, 0, 0))


def per_head(kernel, heads, ins, outs, name):
    width = heads * HEAD
    kinds = {
        "c": (columns(), jax.ShapeDtypeStruct((SEG, width), f32)),
        "s": (state(), jax.ShapeDtypeStruct((heads, ROWS, HEAD), f32)),
        "g": (row(HEAD), jax.ShapeDtypeStruct((heads, 1, HEAD), f32)),
        "t": (
            pl.BlockSpec((HEAD, SEG), lambda h: (h, 0)),
            jax.ShapeDtypeStruct((width, SEG), bf16),
        ),
        "l": (row(SEG), jax.ShapeDtypeStruct((heads, 1, SEG), f32)),
    }
    return pl.pallas_call(
        kernel,
        grid=(heads,),
        in_specs=[kinds[i][0] for i in ins],
        out_specs=[kinds[o][0] for o in outs],
        out_shape=[kinds[o][1] for o in outs],
        compiler_params=pltpu.CompilerParams(vmem_limit_bytes=VMEM_LIMIT),
        cost_estimate=pl.CostEstimate(
            flops=LIGHT, bytes_accessed=LIGHT, transcendentals=0
        ),
        name=name,
    )


def ring(n, step):
    return [(i, (i + step) % n) for i in range(n)]


def grid_sizes():
    heads = lax.axis_size("head")
    return heads, lax.axis_size("ctx") // (2 * heads)


def place():
    xs, zs = grid_sizes()
    at = lax.axis_index("ctx")
    return at // (2 * zs), (at // 2) % zs, at % 2


def core_swap(block):
    n = lax.axis_size("ctx")
    return lax.ppermute(block, "ctx", [(i, i ^ 1) for i in range(n)])


def moved(block, axis, to):
    xs, zs = grid_sizes()
    pairs = []
    for x in range(xs):
        for z in range(zs):
            x_to, z_to = (to(x), z) if axis == "x" else (x, to(z))
            if x_to is not None and z_to is not None:
                for c in range(2):
                    pairs.append(((x * zs + z) * 2 + c, (x_to * zs + z_to) * 2 + c))
    return lax.ppermute(block, "ctx", pairs)


def scan_of_four(block, axis, at, later, beside_first, beside_second):
    near = beside_first(moved(block, axis, lambda i: i ^ 1))
    pair = block + near
    other = beside_second(moved(pair, axis, lambda i: 3 - i))
    counts_near = (at % 2 == 0) if later else (at % 2 == 1)
    counts_other = (at < 2) if later else (at >= 2)
    return jnp.where(counts_near, near, 0.0) + jnp.where(counts_other, other, 0.0), pair + other


def scan_over_ctx(packed, later, work=None):
    xs, zs = grid_sizes()
    x, z, core = place()
    half = packed.shape[0] // 2
    first, second = packed[:half], packed[half:]
    is_first = core == 0
    mine = jnp.where(is_first, first, second)
    theirs = core_swap(jnp.where(is_first, second, first))
    chip = mine + theirs

    def beside_step(i):
        def tie(arrived):
            if work is None:
                return arrived
            done = work(i)
            arrived, *done[:] = lax.optimization_barrier((arrived, *done))
            return arrived

        return tie

    before_z, total_z = scan_of_four(chip, "z", z, later, beside_step(0), beside_step(1))
    before_x, total = scan_of_four(
        total_z, "x", x, later, beside_step(2), beside_step(3)
    )
    outside = before_z + before_x
    counts_other = is_first if later else jnp.logical_not(is_first)
    for_me = outside + jnp.where(counts_other, theirs, 0.0)
    for_other = outside + jnp.where(counts_other, 0.0, mine)
    row = lax.broadcasted_iota(jnp.int32, (1, ROWS, 1), 1)
    totals = jnp.where(row == ROWS - 1, total[:, HEAD + 1 : HEAD + 2, :], 0.0)
    for_me, for_other = for_me + totals, for_other + totals
    swapped = core_swap(for_other)
    low = jnp.where(is_first, for_me, swapped)
    high = jnp.where(is_first, swapped, for_me)
    return jnp.concatenate([low, high], axis=0)


def across(i):
    return 3 - i


def beside(i):
    return i ^ 1


def scattered_of_four(piece, axis, at, first=across, second=beside):
    far = first(at)
    sent = moved(jnp.stack([piece(far), piece(second(far))]), axis, first)
    kept, passed = piece(at) + sent[0], piece(second(at)) + sent[1]
    return kept + moved(passed, axis, second)


def at_place(pieces, i):
    return lax.dynamic_index_in_dim(pieces, i, 0, keepdims=False)


def on_device(queries, keys, values, gate_logit, out_weight, out_grad):
    heads = gate_logit.shape[0]
    width = heads * HEAD
    hs = lax.axis_size("head")
    head = lax.axis_index("head")
    xs, zs = grid_sizes()
    x, z, core = place()
    rows, cols = out_grad.shape

    half = cols // 2

    def up(block):
        return lax.ppermute(block, "head", ring(hs, 1))

    def down(block):
        return lax.ppermute(block, "head", ring(hs, -1))

    left, right = up(out_grad), down(out_grad)
    far_1 = up(left[:HALF, :half]), down(right[:HALF, half:])
    far_2 = up(left[HALF:, :half]), down(right[HALF:, half:])

    gate = jax.nn.sigmoid(gate_logit)
    g = jnp.broadcast_to(gate[:, None, None], (heads, 1, HEAD))

    (packed,) = per_head(update_kernel, heads, "cc", "s", "update")(keys, values)
    forwards = []

    def forward(step):
        if step % 2 == 0:
            forwards[:] = forward_of((step, heads // 2), (queries, keys, values), forwards)
        return forwards

    before = scan_over_ctx(packed, False, forward)
    local_out, lse = forwards
    *mixed, memory_out, lqd = per_head(mix_kernel, heads, "ccsg", "ttcc", "mix")(
        queries, local_out, before, g
    )

    def block_at(distance):
        return (head + hs - distance) % hs

    own_at, left_at, far_at, right_at = (block_at(d) for d in range(4))
    add = functools.partial(round_of, out_weight=out_weight, mixed=mixed, core=core)

    def summed_on_z(mine, send, *order):
        came = core_swap(send)
        return scattered_of_four(lambda i: at_place(mine, i) + at_place(came, i), "z", z, *order)

    mg, mine_own, send_own = add(None, [out_grad], [own_at])
    sum_own = summed_on_z(mine_own, send_own)
    left, right, sum_own = lax.optimization_barrier((left, right, sum_own))
    mg, mine_sides, send_sides = add(mg, [left, right], [left_at, right_at])
    *far_1, mine_sides, send_sides = lax.optimization_barrier((*far_1, mine_sides, send_sides))
    came_sides = core_swap(send_sides)
    far_places = [2 * far_at, 2 * far_at + 1]
    whole = (lqd, memory_out, local_out)
    mg_1, back = tail_of(0, mg, far_1, far_places, out_weight, whole, ())
    far_sums = add(None, far_1, far_places, project=False)
    attended = queries, keys, values

    def backward_ins(part):
        return (*attended, part, local_out, memory_out, lse, before, g)

    dq, dk, dv = backward_of(0, (0, heads), backward_ins(mg_1), (), (), 0)

    came_sides, far_2, dq, far_sums = lax.optimization_barrier((came_sides, far_2, dq, far_sums))
    sum_left = scattered_of_four(
        lambda i: at_place(mine_sides, i) + at_place(came_sides, i), "z", z
    )
    sum_right = scattered_of_four(
        lambda i: at_place(mine_sides, zs + i) + at_place(came_sides, zs + i),
        "z", z, beside, across,
    )
    mg_2, back = tail_of(1, mg, far_2, far_places, out_weight, whole, (back,))
    far_2, back = lax.optimization_barrier((far_2, back))
    mine_far, send_far = add(
        None, far_2, far_places, project=False, micros=5, first=HALF, before=far_sums
    )
    sum_far = summed_on_z(mine_far, send_far)

    early_sums = dk, dv
    grads = [dq]

    def backward(step):
        if step % 2 == 0:
            pair = (step, heads // 2)
            grads[:] = backward_of(1, pair, backward_ins(mg_2), early_sums, grads, 7)
        return grads

    after = scan_over_ctx(back, True, backward)
    dq, dk, dv = grads

    parts = jnp.stack([sum_own, sum_left, sum_far, sum_right])

    def piece_x(i):
        return at_place(parts, (head + hs - i) % hs)

    weight_grad = scattered_of_four(piece_x, "x", x).T

    key_grad, value_grad = per_head(finish_kernel, heads, "ccccs", "cc", "finish")(
        keys, values, dk, dv, after
    )

    gate_sum = jnp.sum(after[:, ROWS - 1, :], axis=-1)
    gate_grad = gate_sum * gate * (1.0 - gate)
    return dq, key_grad, value_grad, weight_grad, gate_grad


def solution(mesh):
    in_specs = (
        P("ctx", "head"),
        P("ctx", "head"),
        P("ctx", "head"),
        P("head"),
        P("head", None),
        P("ctx", "head"),
    )
    out_specs = (P("ctx", "head"), P("ctx", "head"), P("ctx", "head"), P("ctx", "head"), P("head"))
    return jax.shard_map(
        on_device, mesh=mesh, in_specs=in_specs, out_specs=out_specs, check_vma=False
    )
```

```python
import functools
import math

import jax
import jax.numpy as jnp
from jax import lax
from jax.experimental import pallas as pl
from jax.experimental.pallas import tpu as pltpu
from jax.sharding import PartitionSpec as P

SEG = 1024
HEAD = 128
ROWS = 136
FORWARD_QB = 512
BACKWARD_QB = 256
MOST = 3 * SEG // 4
REST = SEG - MOST
STEP = 256
LIGHT = 2**16
VMEM_LIMIT = 60 * 2**20
MICROSECOND = 3_600_000

f32 = jnp.float32
bf16 = jnp.bfloat16
HIGH = lax.Precision.HIGH


def lifted(x):
    return jnp.where(x > 0, x + 1.0, jnp.exp(jnp.minimum(x, 0.0)))


def lifted_slope(x):
    return jnp.where(x > 0, 1.0, jnp.exp(jnp.minimum(x, 0.0)))


def halves(x):
    hi = x.astype(bf16)
    return hi, (x - hi.astype(f32)).astype(bf16)


def mm(a, b, contract):
    dims = ((contract[:1], contract[1:]), ((), ()))

    def one(x, y):
        return lax.dot_general(x, y, dims, preferred_element_type=f32)

    return one(a[0], b[0]) + (one(a[0], b[1]) + one(a[1], b[0]))


NN = (1, 0)
NT = (1, 1)
TN = (0, 0)


def dot(a, b, contract):
    return lax.dot_general(
        a, b, ((contract[:1], contract[1:]), ((), ())), preferred_element_type=f32
    )


def wide(pair):
    return jnp.concatenate(pair, axis=1)


def doubled(x):
    return jnp.concatenate([x, x], axis=1)


def scores_of(a_wide, b_hi_twice, b_lo):
    return dot(a_wide, b_hi_twice, NT) + dot(a_wide[:, :HEAD], b_lo, NT)


def times_wide(a, b_wide):
    both = dot(a[0], b_wide, NN)
    return both[:, :HEAD] + (both[:, HEAD:] + dot(a[1], b_wide[:, :HEAD], NN))


def tall_times(a_tall, b):
    both = dot(a_tall, b[0], NN)
    return both[:HEAD] + (both[HEAD:] + dot(a_tall[:HEAD], b[1], NN))


def update_kernel(k_ref, v_ref, out_ref):
    lk = lifted(k_ref[...])
    out_ref[0, :HEAD, :] = mm(halves(lk.T), halves(v_ref[...]), NN)
    out_ref[0, HEAD : HEAD + 1, :] = jnp.sum(lk, axis=0, keepdims=True)
    out_ref[0, HEAD + 1 :, :] = jnp.zeros((ROWS - HEAD - 1, HEAD), f32)


LOG2E = math.log2(math.e)
TEMPER = 1.0 / math.sqrt(HEAD)


def parts_of(qb, size):
    return ([(0, qb * size, False)] if qb else []) + [(qb * size, (qb + 1) * size, True)]


def causal(size):
    t = lax.broadcasted_iota(jnp.int32, (size, size), 0)
    return t <= lax.broadcasted_iota(jnp.int32, (size, size), 1)


def forward_kernel(q_ref, k_ref, v_ref, *refs):
    out_ref, lse_ref = refs[-2:]
    key = wide(halves(k_ref[...]))
    value_t = jnp.concatenate(halves(v_ref[...].T), axis=0)
    q_hi, q_lo = halves(q_ref[...] * (TEMPER * LOG2E))
    q_twice = doubled(q_hi)
    seen = causal(FORWARD_QB)
    for qb in range(SEG // FORWARD_QB):
        at = slice(qb * FORWARD_QB, (qb + 1) * FORWARD_QB)
        scores = []
        for low, high, own in parts_of(qb, FORWARD_QB):
            part = scores_of(key[low:high], q_twice[at], q_lo[at])
            scores.append(jnp.where(seen, part, -1e30) if own else part)
        top = functools.reduce(
            jnp.maximum, [jnp.max(part, axis=0, keepdims=True) for part in scores]
        )
        total, out_t = 0.0, 0.0
        for (low, high, _), part in zip(parts_of(qb, FORWARD_QB), scores):
            weights = jnp.exp2(part - top)
            total = total + jnp.sum(weights, axis=0, keepdims=True)
            out_t = out_t + tall_times(value_t[:, low:high], halves(weights))
        out_ref[at, :] = (out_t * (1.0 / total)).T
        lse_ref[0, :, at] = top + jnp.log2(total)


def mix_kernel(q_ref, local_ref, mem_ref, g_ref, hi_ref, lo_ref, memout_ref, lqd_ref):
    g = g_ref[0]
    lq = lifted(q_ref[...])
    norm = mem_ref[0, HEAD : HEAD + 1, :]
    denom = jnp.sum(lq * norm, axis=1, keepdims=True) + 1.0
    inverse = 1.0 / denom
    memory_out = mm(halves(lq), halves(mem_ref[0, :HEAD, :]), NN) * inverse
    memout_ref[...] = memory_out
    mixed = g * memory_out + (1.0 - g) * local_ref[...]
    hi_ref[...], lo_ref[...] = halves(mixed.T)
    lqd_ref[...] = lq * (inverse * g)


def add_weight_part(mixed, block, first, start, mine_ref, send_ref):
    part = mm(mixed, block, NN)
    groups = part.shape[1] // (2 * HEAD)
    for k in range(groups):
        even = part[:, 2 * k * HEAD : (2 * k + 1) * HEAD]
        odd = part[:, (2 * k + 1) * HEAD : (2 * k + 2) * HEAD]
        mine_ref[start + k] += jnp.where(first, even, odd)
        send_ref[start + k] += jnp.where(first, odd, even)


def block_kernel(at_ref, *refs, blocks, added, summed):
    refs = list(refs)

    def take(n):
        taken, refs[:] = refs[:n], refs[n:]
        return taken

    acc, block_refs, w_refs, mixed_refs = take(added), take(blocks), take(blocks), take(2)
    before, (out_ref,), by_core = take(summed), take(1), take(2)

    @pl.when(pl.program_id(0) == 0)
    def _():
        for n, w_ref in enumerate(w_refs):
            refs[2 * n][...], refs[2 * n + 1][...] = halves(w_ref[...])
        for n, ref in enumerate(by_core):
            ref[...] = before[n][...] if summed else jnp.zeros_like(ref)

    mixed = tuple(ref[...] for ref in mixed_refs)
    total = acc[0][...] if added else None
    start = 0
    for n, block_ref in enumerate(block_refs):
        block = halves(block_ref[...])
        product = mm(block, (refs[2 * n][...], refs[2 * n + 1][...]), NT)
        total = product if total is None else total + product
        add_weight_part(mixed, block, at_ref[blocks] == 0, start, *by_core)
        start += block_ref.shape[1] // (2 * HEAD)
    out_ref[...] = total


def tail_kernel(at_ref, *refs):
    acc_ref, a_ref, b_ref, wa_ref, wb_ref, lqd_ref, memout_ref, local_ref = refs[:8]
    mhi_ref, mlo_ref, *before = refs[8:-8]
    mg_ref, state_ref, mine_ref, send_ref, *w = refs[-8:]

    @pl.when(pl.program_id(0) == 0)
    def _():
        w[0][...], w[1][...] = halves(wa_ref[...])
        w[2][...], w[3][...] = halves(wb_ref[...])
        for n, ref in enumerate((state_ref, mine_ref, send_ref)):
            ref[...] = before[n][...] if before else jnp.zeros_like(ref)

    a, b = halves(a_ref[...]), halves(b_ref[...])
    mg = acc_ref[...] + mm(a, (w[0][...], w[1][...]), NT)
    mg = mg + mm(b, (w[2][...], w[3][...]), NT)
    mg_ref[...] = mg
    for h in range(state_ref.shape[0]):
        at = slice(h * HEAD, (h + 1) * HEAD)
        here, lqd, memory_out = mg[:, at], lqd_ref[:, at], memout_ref[:, at]
        state_ref[h, :HEAD, :] += mm(halves(lqd.T), halves(here), NN)
        r = jnp.sum(here * memory_out, axis=1, keepdims=True)
        state_ref[h, HEAD : HEAD + 1, :] -= jnp.sum(lqd * r, axis=0, keepdims=True)
        state_ref[h, HEAD + 1 : HEAD + 2, :] += jnp.sum(
            here * (memory_out - local_ref[:, at]), axis=0, keepdims=True
        )
    mixed, first = (mhi_ref[...], mlo_ref[...]), at_ref[2] == 0
    groups = a_ref.shape[1] // (2 * HEAD)
    add_weight_part(mixed, a, first, 0, mine_ref, send_ref)
    add_weight_part(mixed, b, first, groups, mine_ref, send_ref)


def rows_of(width, first=0):
    return pl.BlockSpec((STEP, width), lambda i, at: (i + first // STEP, 0))


def weight_specs(width, blocks):
    return [
        pl.BlockSpec((width, block.shape[1]), lambda i, at, k=k: (0, at[k]))
        for k, block in enumerate(blocks)
    ]


def tail_kernel(at_ref, *refs):
    acc_ref, a_ref, b_ref, wa_ref, wb_ref, lqd_ref, memout_ref, local_ref = refs[:8]
    mhi_ref, mlo_ref, *before = refs[8:-8]
    mg_ref, state_ref, mine_ref, send_ref, *w = refs[-8:]

    @pl.when(pl.program_id(0) == 0)
    def _():
        w[0][...], w[1][...] = halves(wa_ref[...])
        w[2][...], w[3][...] = halves(wb_ref[...])
        for n, ref in enumerate((state_ref, mine_ref, send_ref)):
            ref[...] = before[n][...] if before else jnp.zeros_like(ref)

    a, b = halves(a_ref[...]), halves(b_ref[...])
    mg = acc_ref[...] + mm(a, (w[0][...], w[1][...]), NT)
    mg = mg + mm(b, (w[2][...], w[3][...]), NT)
    mg_ref[...] = mg
    for h in range(state_ref.shape[0]):
        at = slice(h * HEAD, (h + 1) * HEAD)
        here, lqd, memory_out = mg[:, at], lqd_ref[:, at], memout_ref[:, at]
        state_ref[h, :HEAD, :] += mm(halves(lqd.T), halves(here), NN)
        r = jnp.sum(here * memory_out, axis=1, keepdims=True)
        state_ref[h, HEAD : HEAD + 1, :] -= jnp.sum(lqd * r, axis=0, keepdims=True)
        state_ref[h, HEAD + 1 : HEAD + 2, :] += jnp.sum(
            here * (memory_out - local_ref[:, at]), axis=0, keepdims=True
        )
    mixed, first = (mhi_ref[...], mlo_ref[...]), at_ref[2] == 0
    groups = a_ref.shape[1] // (2 * HEAD)
    add_weight_part(mixed, a, first, 0, mine_ref, send_ref)
    add_weight_part(mixed, b, first, groups, mine_ref, send_ref)


def rows_of(width, first=0):
    return pl.BlockSpec((STEP, width), lambda i, at: (i + first // STEP, 0))


def weight_specs(width, blocks):
    return [
        pl.BlockSpec((width, block.shape[1]), lambda i, at, k=k: (0, at[k]))
        for k, block in enumerate(blocks)
    ]


def round_of(acc, blocks, places, out_weight, mixed, core, first=0, before=(), micros=0):
    rows = blocks[0].shape[0]
    width = out_weight.shape[0]
    n = len(blocks)
    groups = sum(block.shape[1] for block in blocks) // (2 * HEAD)
    at = jnp.stack([*places, core]).astype(jnp.int32)
    acc = [] if acc is None else [acc]
    by_core = pl.BlockSpec((groups, width, HEAD), lambda i, at: (0, 0, 0))
    by_core_shape = jax.ShapeDtypeStruct((groups, width, HEAD), f32)
    return pl.pallas_call(
        functools.partial(block_kernel, blocks=n, added=len(acc), summed=len(before)),
        grid_spec=pltpu.PrefetchScalarGridSpec(
            num_scalar_prefetch=1,
            grid=(rows // STEP,),
            in_specs=[rows_of(width, first) for _ in acc]
            + [rows_of(block.shape[1]) for block in blocks]
            + weight_specs(width, blocks)
            + [pl.BlockSpec((width, STEP), lambda i, at: (0, i + first // STEP))] * 2
            + [by_core] * len(before),
            out_specs=[rows_of(width, first)] + [by_core] * 2,
            scratch_shapes=[
                pltpu.VMEM((width, block.shape[1]), bf16) for block in blocks for _ in range(2)
            ],
        ),
        out_shape=[jax.ShapeDtypeStruct((SEG, width), f32)] + [by_core_shape] * 2,
        input_output_aliases={1: 0} if acc else {},
        compiler_params=pltpu.CompilerParams(vmem_limit_bytes=VMEM_LIMIT),
        cost_estimate=pl.CostEstimate(flops=LIGHT, bytes_accessed=LIGHT, transcendentals=0),
        name="round",
    )(at, *acc, *blocks, *([out_weight] * n), *mixed, *before)


def tail_of(second, acc, blocks, places, out_weight, mixed, core, whole, before):
    rows, deep = blocks[0].shape
    width = out_weight.shape[0]
    first = second * MOST
    by_core = deep // HEAD, width, HEAD
    sums = [(width // HEAD, ROWS, HEAD), by_core, by_core]
    sum_specs = [pl.BlockSpec(shape, lambda i, at: (0, 0, 0)) for shape in sums]
    return pl.pallas_call(
        tail_kernel,
        grid_spec=pltpu.PrefetchScalarGridSpec(
            num_scalar_prefetch=1,
            grid=(rows // STEP,),
            in_specs=[rows_of(width, first)]
            + [rows_of(deep)] * 2
            + weight_specs(width, blocks)
            + [rows_of(width, first)] * 3
            + [pl.BlockSpec((width, STEP), lambda i, at: (0, i + first // STEP))] * 2
            + sum_specs[: len(before)],
            out_specs=[rows_of(width), *sum_specs],
            scratch_shapes=[pltpu.VMEM((width, deep), bf16) for _ in range(4)],
        ),
        out_shape=[jax.ShapeDtypeStruct(shape, f32) for shape in [(rows, width), *sums]],
        compiler_params=pltpu.CompilerParams(vmem_limit_bytes=VMEM_LIMIT),
        cost_estimate=pl.CostEstimate(flops=LIGHT, bytes_accessed=LIGHT, transcendentals=0),
        name="tail",
    )(
        jnp.stack([*places, core]).astype(jnp.int32),
        acc, *blocks, out_weight, out_weight, *whole, *mixed, *before,
    )


def backward_kernel(*refs, first):
    q_ref, k_ref, v_ref, mg_ref, local_ref, memout_ref, lse_ref, mem_ref, g_ref = refs[:9]
    dq_ref, dk_ref, dv_ref = refs[-3:]
    g = g_ref[0]
    q = q_ref[...]
    mg = mg_ref[...]
    local_grad = (1.0 - g) * TEMPER * mg
    key = halves(k_ref[...])
    key_t = jnp.concatenate([key[0].T, key[1].T], axis=0)
    key = wide(key)
    value = wide(halves(v_ref[...]))
    query = halves(q * (TEMPER * LOG2E))
    q_twice, q_wide = doubled(query[0]), wide(query)
    grad = halves(local_grad)
    g_twice, g_wide = doubled(grad[0]), wide(grad)
    delta = jnp.sum((local_grad * local_ref[...]).T, axis=0, keepdims=True)
    lq = lifted(q)
    norm = mem_ref[0, HEAD : HEAD + 1, :]
    inverse = 1.0 / (jnp.sum(lq * norm, axis=1, keepdims=True) + 1.0)
    r = jnp.sum(mg * memout_ref[...], axis=1, keepdims=True)
    lift_grad = mm(halves(mg), halves(mem_ref[0, :HEAD, :].T), NN) - r * norm
    dq_ref[...] = lift_grad * (inverse * g) * lifted_slope(q)
    for ref, before in zip((dk_ref, dv_ref), refs[9:11] if first else (None, None)):
        ref[first:, :] = jnp.zeros(q.shape, f32)
        if first:
            ref[:first, :] = before[...]
    seen = causal(BACKWARD_QB)
    for qb in range(q.shape[0] // BACKWARD_QB):
        at = slice(qb * BACKWARD_QB, (qb + 1) * BACKWARD_QB)
        dq_t = 0.0
        for low, high, own in parts_of(qb + first // BACKWARD_QB, BACKWARD_QB):
            scores = scores_of(key[low:high], q_twice[at], query[1][at])
            if own:
                scores = jnp.where(seen, scores, -1e30)
            weights = jnp.exp2(scores - lse_ref[0, :, at])
            dp = scores_of(value[low:high], g_twice[at], grad[1][at])
            ds = halves(weights * (dp - delta[:, at]))
            dv_ref[low:high, :] += times_wide(halves(weights), g_wide[at])
            dk_ref[low:high, :] += times_wide(ds, q_wide[at])
            dq_t = dq_t + tall_times(key_t[:, low:high], ds)
        dq_ref[at, :] += dq_t.T
    if first:
        dk_ref[...] = dk_ref[...] * (1.0 / (TEMPER * LOG2E))
        dv_ref[...] = dv_ref[...] * (1.0 / TEMPER)


def backward_of(second, heads, ins, before, earlier, micros):
    width = ins[0].shape[1]
    low, count = heads

    def rows(n, at=0):
        return pl.BlockSpec((n, HEAD), lambda h: (at, h + low))

    def of_head(x, n=None, at=0):
        return pl.BlockSpec((1, x.shape[1], n or x.shape[2]), lambda h: (h + low, 0, at))

    size, at_part = (REST, MOST // REST) if second else (MOST, 0)
    here = rows(size, at_part)
    seen = rows(SEG if second else MOST)
    shapes = [(SEG, width)] + [(SEG if second else MOST, width)] * 2
    return pl.pallas_call(
        functools.partial(backward_kernel, first=second * MOST),
        grid=(count,),
        in_specs=[here, seen, seen, rows(size), here, here]
        + [of_head(ins[6], size, at_part), of_head(ins[7]), of_head(ins[8])]
        + [rows(MOST)] * len(before)
        + [pl.BlockSpec(memory_space=pl.ANY)] * len(earlier),
        out_specs=[here, seen, seen],
        out_shape=[jax.ShapeDtypeStruct(shape, f32) for shape in shapes],
        input_output_aliases={len(ins) + len(before) + i: i for i in range(len(earlier))},
        compiler_params=pltpu.CompilerParams(vmem_limit_bytes=VMEM_LIMIT),
        cost_estimate=pl.CostEstimate(
            flops=LIGHT, bytes_accessed=micros * MICROSECOND or LIGHT, transcendentals=0
        ),
        name="backward",
    )(*ins, *before, *earlier)


def forward_of(heads, ins, earlier):
    width = ins[0].shape[1]
    low, count = heads
    column = pl.BlockSpec((SEG, HEAD), lambda h: (0, h + low))
    line = pl.BlockSpec((1, 1, SEG), lambda h: (h + low, 0, 0))
    return pl.pallas_call(
        forward_kernel,
        grid=(count,),
        in_specs=[column] * 3 + [pl.BlockSpec(memory_space=pl.ANY)] * len(earlier),
        out_specs=[column, line],
        out_shape=[
            jax.ShapeDtypeStruct((SEG, width), f32),
            jax.ShapeDtypeStruct((width // HEAD, 1, SEG), f32),
        ],
        input_output_aliases={len(ins) + i: i for i in range(len(earlier))},
        compiler_params=pltpu.CompilerParams(vmem_limit_bytes=VMEM_LIMIT),
        cost_estimate=pl.CostEstimate(flops=LIGHT, bytes_accessed=LIGHT, transcendentals=0),
        name="forward",
    )(*ins, *earlier)


def finish_kernel(k_ref, v_ref, dk_ref, dv_ref, state_ref, kg_ref, vg_ref):
    key = k_ref[...]
    state = state_ref[0, :HEAD, :]
    norm = state_ref[0, HEAD : HEAD + 1, :]
    lift_grad = mm(halves(v_ref[...]), halves(state.T), NN) + norm
    kg_ref[...] = dk_ref[...] + lift_grad * lifted_slope(key)
    vg_ref[...] = dv_ref[...] + mm(halves(lifted(key)), halves(state), NN)


def columns():
    return pl.BlockSpec((SEG, HEAD), lambda h: (0, h))


def state():
    return pl.BlockSpec((1, ROWS, HEAD), lambda h: (h, 0, 0))


def row(width):
    return pl.BlockSpec((1, 1, width), lambda h: (h, 0, 0))


def per_head(kernel, heads, ins, outs, name):
    width = heads * HEAD
    kinds = {
        "c": (columns(), jax.ShapeDtypeStruct((SEG, width), f32)),
        "s": (state(), jax.ShapeDtypeStruct((heads, ROWS, HEAD), f32)),
        "g": (row(HEAD), jax.ShapeDtypeStruct((heads, 1, HEAD), f32)),
        "t": (
            pl.BlockSpec((HEAD, SEG), lambda h: (h, 0)),
            jax.ShapeDtypeStruct((width, SEG), bf16),
        ),
        "l": (row(SEG), jax.ShapeDtypeStruct((heads, 1, SEG), f32)),
    }
    return pl.pallas_call(
        kernel,
        grid=(heads,),
        in_specs=[kinds[i][0] for i in ins],
        out_specs=[kinds[o][0] for o in outs],
        out_shape=[kinds[o][1] for o in outs],
        compiler_params=pltpu.CompilerParams(vmem_limit_bytes=VMEM_LIMIT),
        cost_estimate=pl.CostEstimate(
            flops=LIGHT, bytes_accessed=LIGHT, transcendentals=0
        ),
        name=name,
    )


def ring(n, step):
    return [(i, (i + step) % n) for i in range(n)]


def grid_sizes():
    heads = lax.axis_size("head")
    return heads, lax.axis_size("ctx") // (2 * heads)


def place():
    xs, zs = grid_sizes()
    at = lax.axis_index("ctx")
    return at // (2 * zs), (at // 2) % zs, at % 2


def core_swap(block):
    n = lax.axis_size("ctx")
    return lax.ppermute(block, "ctx", [(i, i ^ 1) for i in range(n)])


def moved(block, axis, to):
    xs, zs = grid_sizes()
    pairs = []
    for x in range(xs):
        for z in range(zs):
            x_to, z_to = (to(x), z) if axis == "x" else (x, to(z))
            if x_to is not None and z_to is not None:
                for c in range(2):
                    pairs.append(((x * zs + z) * 2 + c, (x_to * zs + z_to) * 2 + c))
    return lax.ppermute(block, "ctx", pairs)


def scan_of_four(block, axis, at, later, beside_first, beside_second):
    near = beside_first(moved(block, axis, lambda i: i ^ 1))
    pair = block + near
    other = beside_second(moved(pair, axis, lambda i: 3 - i))
    counts_near = (at % 2 == 0) if later else (at % 2 == 1)
    counts_other = (at < 2) if later else (at >= 2)
    return jnp.where(counts_near, near, 0.0) + jnp.where(counts_other, other, 0.0), pair + other


def scan_over_ctx(packed, later, work=None):
    xs, zs = grid_sizes()
    x, z, core = place()
    half = packed.shape[0] // 2
    first, second = packed[:half], packed[half:]
    is_first = core == 0
    mine = jnp.where(is_first, first, second)
    theirs = core_swap(jnp.where(is_first, second, first))
    chip = mine + theirs

    def beside_step(i):
        def tie(arrived):
            if work is None:
                return arrived
            done = work(i)
            arrived, *done[:] = lax.optimization_barrier((arrived, *done))
            return arrived

        return tie

    before_z, total_z = scan_of_four(chip, "z", z, later, beside_step(0), beside_step(1))
    before_x, total = scan_of_four(
        total_z, "x", x, later, beside_step(2), beside_step(3)
    )
    outside = before_z + before_x
    counts_other = is_first if later else jnp.logical_not(is_first)
    for_me = outside + jnp.where(counts_other, theirs, 0.0)
    for_other = outside + jnp.where(counts_other, 0.0, mine)
    row = lax.broadcasted_iota(jnp.int32, (1, ROWS, 1), 1)
    totals = jnp.where(row == ROWS - 1, total[:, HEAD + 1 : HEAD + 2, :], 0.0)
    for_me, for_other = for_me + totals, for_other + totals
    swapped = core_swap(for_other)
    low = jnp.where(is_first, for_me, swapped)
    high = jnp.where(is_first, swapped, for_me)
    return jnp.concatenate([low, high], axis=0)


def across(i):
    return 3 - i


def beside(i):
    return i ^ 1


def scattered_of_four(piece, axis, at, first=across, second=beside):
    far = first(at)
    sent = moved(jnp.stack([piece(far), piece(second(far))]), axis, first)
    kept, passed = piece(at) + sent[0], piece(second(at)) + sent[1]
    return kept + moved(passed, axis, second)


def at_place(pieces, i):
    return lax.dynamic_index_in_dim(pieces, i, 0, keepdims=False)


def on_device(queries, keys, values, gate_logit, out_weight, out_grad):
    heads = gate_logit.shape[0]
    width = heads * HEAD
    hs = lax.axis_size("head")
    head = lax.axis_index("head")
    xs, zs = grid_sizes()
    x, z, core = place()
    rows, cols = out_grad.shape

    half = cols // 2
    head_rows, rest_rows = out_grad[:MOST], out_grad[MOST:]

    def up(block):
        return lax.ppermute(block, "head", ring(hs, 1))

    def down(block):
        return lax.ppermute(block, "head", ring(hs, -1))

    left, right = up(head_rows), down(head_rows)
    far_1 = up(left[:, :half]), down(right[:, half:])

    gate = jax.nn.sigmoid(gate_logit)
    g = jnp.broadcast_to(gate[:, None, None], (heads, 1, HEAD))

    (packed,) = per_head(update_kernel, heads, "cc", "s", "update")(keys, values)
    forwards = []

    def forward(step):
        if step % 2 == 0:
            forwards[:] = forward_of((step, heads // 2), (queries, keys, values), forwards)
        return forwards

    before = scan_over_ctx(packed, False, forward)
    local_out, lse = forwards
    *mixed, memory_out, lqd = per_head(mix_kernel, heads, "ccsg", "ttcc", "mix")(
        queries, local_out, before, g
    )

    def block_at(distance):
        return (head + hs - distance) % hs

    own_at, left_at, far_at, right_at = (block_at(d) for d in range(4))
    add = functools.partial(round_of, out_weight=out_weight, mixed=mixed, core=core)

    def summed_on_z(mine, send, *order):
        came = core_swap(send)
        return scattered_of_four(lambda i: at_place(mine, i) + at_place(came, i), "z", z, *order)

    mg, mine_own, send_own = add(None, [out_grad], [own_at])
    sides = [left_at, right_at]
    early_left, early_right, rest_rows, mine_own, send_own = lax.optimization_barrier(
        (left, right, rest_rows, mine_own, send_own)
    )
    left_rest, right_rest = up(rest_rows), down(rest_rows)
    sum_own = summed_on_z(mine_own, send_own)
    mg, *side_sums = add(mg, [early_left, early_right], sides)

    far_places = [2 * far_at, 2 * far_at + 1]
    tail = functools.partial(
        tail_of, places=far_places, out_weight=out_weight, mixed=mixed, core=core,
        whole=(lqd, memory_out, local_out),
    )
    mg_1, *far_sums = tail(0, mg, far_1, before=())
    attended = queries, keys, values

    def backward_ins(part):
        return (*attended, part, local_out, memory_out, lse, before, g)

    pairs = [(0, heads // 2), (heads // 2, heads // 2)]
    early = backward_of(0, pairs[0], backward_ins(mg_1), (), (), 0)

    left_rest, right_rest, *early = lax.optimization_barrier((left_rest, right_rest, *early))
    far_a, far_b = left_rest[:, :half], right_rest[:, half:]
    left_rest, right_rest, far_a, far_b, sum_own, mg, *early = lax.optimization_barrier(
        (left_rest, right_rest, far_a, far_b, sum_own, mg, *early)
    )
    far_2 = up(far_a), down(far_b)
    early = backward_of(0, pairs[1], backward_ins(mg_1), (), early, 0)
    mg, mine_sides, send_sides = add(
        mg, [left_rest, right_rest], sides, first=MOST, before=side_sums, micros=7
    )
    came_sides = core_swap(send_sides)

    def piece_sides(i):
        both = [at_place(mine_sides, n + i) + at_place(came_sides, n + i) for n in (0, zs)]
        return jnp.stack(both)

    *far_2, came_sides, dq, dk, dv = lax.optimization_barrier((*far_2, came_sides, *early))
    mg_2, back, mine_far, send_far = tail(1, mg, far_2, before=far_sums)
    sum_left, sum_right = scattered_of_four(piece_sides, "z", z)
    sum_far = summed_on_z(mine_far, send_far)

    early_sums = dk, dv
    grads = [dq]

    def backward(step):
        if step % 2 == 0:
            grads[:] = backward_of(1, pairs[step // 2], backward_ins(mg_2), early_sums, grads, 6)
        return grads

    after = scan_over_ctx(back, True, backward)
    dq, dk, dv = grads

    parts = jnp.stack([sum_own, sum_left, sum_far, sum_right])

    def piece_x(i):
        return at_place(parts, (head + hs - i) % hs)

    weight_grad = scattered_of_four(piece_x, "x", x).T

    key_grad, value_grad = per_head(finish_kernel, heads, "ccccs", "cc", "finish")(
        keys, values, dk, dv, after
    )

    gate_sum = jnp.sum(after[:, ROWS - 1, :], axis=-1)
    gate_grad = gate_sum * gate * (1.0 - gate)
    return dq, key_grad, value_grad, weight_grad, gate_grad


def solution(mesh):
    in_specs = (
        P("ctx", "head"),
        P("ctx", "head"),
        P("ctx", "head"),
        P("head"),
        P("head", None),
        P("ctx", "head"),
    )
    out_specs = (P("ctx", "head"), P("ctx", "head"), P("ctx", "head"), P("ctx", "head"), P("head"))
    return jax.shard_map(
        on_device, mesh=mesh, in_specs=in_specs, out_specs=out_specs, check_vma=False
    )
```

```python
import functools
import math

import jax
import jax.numpy as jnp
from jax import lax
from jax.experimental import pallas as pl
from jax.experimental.pallas import tpu as pltpu
from jax.sharding import PartitionSpec as P

SEG = 1024
HEAD = 128
ROWS = 136
FORWARD_QB = 512
BACKWARD_QB = 256
MOST = SEG // 2
REST = SEG - MOST
STEP = 256
LIGHT = 2**16
VMEM_LIMIT = 60 * 2**20
MICROSECOND = 3_600_000

f32 = jnp.float32
bf16 = jnp.bfloat16
HIGH = lax.Precision.HIGH


def lifted(x):
    return jnp.where(x > 0, x + 1.0, jnp.exp(jnp.minimum(x, 0.0)))


def lifted_slope(x):
    return jnp.where(x > 0, 1.0, jnp.exp(jnp.minimum(x, 0.0)))


def halves(x):
    hi = x.astype(bf16)
    return hi, (x - hi.astype(f32)).astype(bf16)


def mm(a, b, contract):
    dims = ((contract[:1], contract[1:]), ((), ()))

    def one(x, y):
        return lax.dot_general(x, y, dims, preferred_element_type=f32)

    return one(a[0], b[0]) + (one(a[0], b[1]) + one(a[1], b[0]))


NN = (1, 0)
NT = (1, 1)
TN = (0, 0)


def dot(a, b, contract):
    return lax.dot_general(
        a, b, ((contract[:1], contract[1:]), ((), ())), preferred_element_type=f32
    )


def wide(pair):
    return jnp.concatenate(pair, axis=1)


def doubled(x):
    return jnp.concatenate([x, x], axis=1)


def scores_of(a_wide, b_hi_twice, b_lo):
    return dot(a_wide, b_hi_twice, NT) + dot(a_wide[:, :HEAD], b_lo, NT)


def times_wide(a, b_wide):
    both = dot(a[0], b_wide, NN)
    return both[:, :HEAD] + (both[:, HEAD:] + dot(a[1], b_wide[:, :HEAD], NN))


def tall_times(a_tall, b):
    both = dot(a_tall, b[0], NN)
    return both[:HEAD] + (both[HEAD:] + dot(a_tall[:HEAD], b[1], NN))


def update_kernel(k_ref, v_ref, out_ref):
    lk = lifted(k_ref[...])
    out_ref[0, :HEAD, :] = mm(halves(lk.T), halves(v_ref[...]), NN)
    out_ref[0, HEAD : HEAD + 1, :] = jnp.sum(lk, axis=0, keepdims=True)
    out_ref[0, HEAD + 1 :, :] = jnp.zeros((ROWS - HEAD - 1, HEAD), f32)


LOG2E = math.log2(math.e)
TEMPER = 1.0 / math.sqrt(HEAD)


def parts_of(qb, size):
    return ([(0, qb * size, False)] if qb else []) + [(qb * size, (qb + 1) * size, True)]


def causal(size):
    t = lax.broadcasted_iota(jnp.int32, (size, size), 0)
    return t <= lax.broadcasted_iota(jnp.int32, (size, size), 1)


def forward_kernel(q_ref, k_ref, v_ref, *refs):
    out_ref, lse_ref = refs[-2:]
    key = wide(halves(k_ref[...]))
    value_t = jnp.concatenate(halves(v_ref[...].T), axis=0)
    q_hi, q_lo = halves(q_ref[...] * (TEMPER * LOG2E))
    q_twice = doubled(q_hi)
    seen = causal(FORWARD_QB)
    for qb in range(SEG // FORWARD_QB):
        at = slice(qb * FORWARD_QB, (qb + 1) * FORWARD_QB)
        scores = []
        for low, high, own in parts_of(qb, FORWARD_QB):
            part = scores_of(key[low:high], q_twice[at], q_lo[at])
            scores.append(jnp.where(seen, part, -1e30) if own else part)
        top = functools.reduce(
            jnp.maximum, [jnp.max(part, axis=0, keepdims=True) for part in scores]
        )
        total, out_t = 0.0, 0.0
        for (low, high, _), part in zip(parts_of(qb, FORWARD_QB), scores):
            weights = jnp.exp2(part - top)
            total = total + jnp.sum(weights, axis=0, keepdims=True)
            out_t = out_t + tall_times(value_t[:, low:high], halves(weights))
        out_ref[at, :] = (out_t * (1.0 / total)).T
        lse_ref[0, :, at] = top + jnp.log2(total)


def mix_kernel(q_ref, local_ref, mem_ref, g_ref, hi_ref, lo_ref, memout_ref, lqd_ref):
    g = g_ref[0]
    lq = lifted(q_ref[...])
    norm = mem_ref[0, HEAD : HEAD + 1, :]
    denom = jnp.sum(lq * norm, axis=1, keepdims=True) + 1.0
    inverse = 1.0 / denom
    memory_out = mm(halves(lq), halves(mem_ref[0, :HEAD, :]), NN) * inverse
    memout_ref[...] = memory_out
    mixed = g * memory_out + (1.0 - g) * local_ref[...]
    hi_ref[...], lo_ref[...] = halves(mixed.T)
    lqd_ref[...] = lq * (inverse * g)


def add_weight_part(mixed, block, first, start, mine_ref, send_ref):
    part = mm(mixed, block, NN)
    groups = part.shape[1] // (2 * HEAD)
    for k in range(groups):
        even = part[:, 2 * k * HEAD : (2 * k + 1) * HEAD]
        odd = part[:, (2 * k + 1) * HEAD : (2 * k + 2) * HEAD]
        mine_ref[start + k] += jnp.where(first, even, odd)
        send_ref[start + k] += jnp.where(first, odd, even)


def block_kernel(at_ref, *refs, blocks, added, summed):
    refs = list(refs)

    def take(n):
        taken, refs[:] = refs[:n], refs[n:]
        return taken

    acc, block_refs, w_refs, mixed_refs = take(added), take(blocks), take(blocks), take(2)
    before, (out_ref,), by_core = take(summed), take(1), take(2)

    @pl.when(pl.program_id(0) == 0)
    def _():
        for n, w_ref in enumerate(w_refs):
            refs[2 * n][...], refs[2 * n + 1][...] = halves(w_ref[...])
        for n, ref in enumerate(by_core):
            ref[...] = before[n][...] if summed else jnp.zeros_like(ref)

    mixed = tuple(ref[...] for ref in mixed_refs)
    total = acc[0][...] if added else None
    start = 0
    for n, block_ref in enumerate(block_refs):
        block = halves(block_ref[...])
        product = mm(block, (refs[2 * n][...], refs[2 * n + 1][...]), NT)
        total = product if total is None else total + product
        add_weight_part(mixed, block, at_ref[blocks] == 0, start, *by_core)
        start += block_ref.shape[1] // (2 * HEAD)
    out_ref[...] = total


def tail_kernel(at_ref, *refs):
    acc_ref, a_ref, b_ref, wa_ref, wb_ref, lqd_ref, memout_ref, local_ref = refs[:8]
    mhi_ref, mlo_ref, *before = refs[8:-8]
    mg_ref, state_ref, mine_ref, send_ref, *w = refs[-8:]

    @pl.when(pl.program_id(0) == 0)
    def _():
        w[0][...], w[1][...] = halves(wa_ref[...])
        w[2][...], w[3][...] = halves(wb_ref[...])
        for n, ref in enumerate((state_ref, mine_ref, send_ref)):
            ref[...] = before[n][...] if before else jnp.zeros_like(ref)

    a, b = halves(a_ref[...]), halves(b_ref[...])
    mg = acc_ref[...] + mm(a, (w[0][...], w[1][...]), NT)
    mg = mg + mm(b, (w[2][...], w[3][...]), NT)
    mg_ref[...] = mg
    for h in range(state_ref.shape[0]):
        at = slice(h * HEAD, (h + 1) * HEAD)
        here, lqd, memory_out = mg[:, at], lqd_ref[:, at], memout_ref[:, at]
        state_ref[h, :HEAD, :] += mm(halves(lqd.T), halves(here), NN)
        r = jnp.sum(here * memory_out, axis=1, keepdims=True)
        state_ref[h, HEAD : HEAD + 1, :] -= jnp.sum(lqd * r, axis=0, keepdims=True)
        state_ref[h, HEAD + 1 : HEAD + 2, :] += jnp.sum(
            here * (memory_out - local_ref[:, at]), axis=0, keepdims=True
        )
    mixed, first = (mhi_ref[...], mlo_ref[...]), at_ref[2] == 0
    groups = a_ref.shape[1] // (2 * HEAD)
    add_weight_part(mixed, a, first, 0, mine_ref, send_ref)
    add_weight_part(mixed, b, first, groups, mine_ref, send_ref)


def rows_of(width, first=0):
    return pl.BlockSpec((STEP, width), lambda i, at: (i + first // STEP, 0))


def weight_specs(width, blocks):
    return [
        pl.BlockSpec(
            (width, block.shape[1]), lambda i, at, k=k: (0, at[k]), pipeline_mode=pl.Buffered(1)
        )
        for k, block in enumerate(blocks)
    ]


def tail_kernel(at_ref, *refs):
    acc_ref, a_ref, b_ref, wa_ref, wb_ref, lqd_ref, memout_ref, local_ref = refs[:8]
    mhi_ref, mlo_ref, *before = refs[8:-8]
    mg_ref, state_ref, mine_ref, send_ref, *w = refs[-8:]

    @pl.when(pl.program_id(0) == 0)
    def _():
        w[0][...], w[1][...] = halves(wa_ref[...])
        w[2][...], w[3][...] = halves(wb_ref[...])
        for n, ref in enumerate((state_ref, mine_ref, send_ref)):
            ref[...] = before[n][...] if before else jnp.zeros_like(ref)

    a, b = halves(a_ref[...]), halves(b_ref[...])
    mg = acc_ref[...] + mm(a, (w[0][...], w[1][...]), NT)
    mg = mg + mm(b, (w[2][...], w[3][...]), NT)
    mg_ref[...] = mg
    for h in range(state_ref.shape[0]):
        at = slice(h * HEAD, (h + 1) * HEAD)
        here, lqd, memory_out = mg[:, at], lqd_ref[:, at], memout_ref[:, at]
        state_ref[h, :HEAD, :] += mm(halves(lqd.T), halves(here), NN)
        r = jnp.sum(here * memory_out, axis=1, keepdims=True)
        state_ref[h, HEAD : HEAD + 1, :] -= jnp.sum(lqd * r, axis=0, keepdims=True)
        state_ref[h, HEAD + 1 : HEAD + 2, :] += jnp.sum(
            here * (memory_out - local_ref[:, at]), axis=0, keepdims=True
        )
    mixed, first = (mhi_ref[...], mlo_ref[...]), at_ref[2] == 0
    groups = a_ref.shape[1] // (2 * HEAD)
    add_weight_part(mixed, a, first, 0, mine_ref, send_ref)
    add_weight_part(mixed, b, first, groups, mine_ref, send_ref)


def rows_of(width, first=0):
    return pl.BlockSpec((STEP, width), lambda i, at: (i + first // STEP, 0))


def weight_specs(width, blocks):
    return [
        pl.BlockSpec(
            (width, block.shape[1]), lambda i, at, k=k: (0, at[k]), pipeline_mode=pl.Buffered(1)
        )
        for k, block in enumerate(blocks)
    ]


def tail_kernel(at_ref, *refs):
    acc_ref, a_ref, b_ref, wa_ref, wb_ref, lqd_ref, memout_ref, local_ref = refs[:8]
    mhi_ref, mlo_ref, *before = refs[8:-8]
    mg_ref, state_ref, mine_ref, send_ref, *w = refs[-8:]

    @pl.when(pl.program_id(0) == 0)
    def _():
        w[0][...], w[1][...] = halves(wa_ref[...])
        w[2][...], w[3][...] = halves(wb_ref[...])
        for n, ref in enumerate((state_ref, mine_ref, send_ref)):
            ref[...] = before[n][...] if before else jnp.zeros_like(ref)

    a, b = halves(a_ref[...]), halves(b_ref[...])
    mg = acc_ref[...] + mm(a, (w[0][...], w[1][...]), NT)
    mg = mg + mm(b, (w[2][...], w[3][...]), NT)
    mg_ref[...] = mg
    for h in range(state_ref.shape[0]):
        at = slice(h * HEAD, (h + 1) * HEAD)
        here, lqd, memory_out = mg[:, at], lqd_ref[:, at], memout_ref[:, at]
        state_ref[h, :HEAD, :] += mm(halves(lqd.T), halves(here), NN)
        r = jnp.sum(here * memory_out, axis=1, keepdims=True)
        state_ref[h, HEAD : HEAD + 1, :] -= jnp.sum(lqd * r, axis=0, keepdims=True)
        state_ref[h, HEAD + 1 : HEAD + 2, :] += jnp.sum(
            here * (memory_out - local_ref[:, at]), axis=0, keepdims=True
        )
    mixed, first = (mhi_ref[...], mlo_ref[...]), at_ref[2] == 0
    groups = a_ref.shape[1] // (2 * HEAD)
    add_weight_part(mixed, a, first, 0, mine_ref, send_ref)
    add_weight_part(mixed, b, first, groups, mine_ref, send_ref)


def rows_of(width, first=0):
    return pl.BlockSpec((STEP, width), lambda i, at: (i + first // STEP, 0))


def weight_specs(width, blocks):
    return [
        pl.BlockSpec(
            (width, block.shape[1]), lambda i, at, k=k: (0, at[k]), pipeline_mode=pl.Buffered(1)
        )
        for k, block in enumerate(blocks)
    ]


def tail_kernel(at_ref, *refs):
    acc_ref, a_ref, b_ref, wa_ref, wb_ref, lqd_ref, memout_ref, local_ref = refs[:8]
    mhi_ref, mlo_ref, *before = refs[8:-8]
    mg_ref, state_ref, mine_ref, send_ref, *w = refs[-8:]

    @pl.when(pl.program_id(0) == 0)
    def _():
        w[0][...], w[1][...] = halves(wa_ref[...])
        w[2][...], w[3][...] = halves(wb_ref[...])
        for n, ref in enumerate((state_ref, mine_ref, send_ref)):
            ref[...] = before[n][...] if before else jnp.zeros_like(ref)

    a, b = halves(a_ref[...]), halves(b_ref[...])
    mg = acc_ref[...] + mm(a, (w[0][...], w[1][...]), NT)
    mg = mg + mm(b, (w[2][...], w[3][...]), NT)
    mg_ref[...] = mg
    for h in range(state_ref.shape[0]):
        at = slice(h * HEAD, (h + 1) * HEAD)
        here, lqd, memory_out = mg[:, at], lqd_ref[:, at], memout_ref[:, at]
        state_ref[h, :HEAD, :] += mm(halves(lqd.T), halves(here), NN)
        r = jnp.sum(here * memory_out, axis=1, keepdims=True)
        state_ref[h, HEAD : HEAD + 1, :] -= jnp.sum(lqd * r, axis=0, keepdims=True)
        state_ref[h, HEAD + 1 : HEAD + 2, :] += jnp.sum(
            here * (memory_out - local_ref[:, at]), axis=0, keepdims=True
        )
    mixed, first = (mhi_ref[...], mlo_ref[...]), at_ref[2] == 0
    groups = a_ref.shape[1] // (2 * HEAD)
    add_weight_part(mixed, a, first, 0, mine_ref, send_ref)
    add_weight_part(mixed, b, first, groups, mine_ref, send_ref)


def rows_of(width, first=0):
    return pl.BlockSpec((STEP, width), lambda i, at: (i + first // STEP, 0))


def weight_specs(width, blocks):
    return [
        pl.BlockSpec(
            (width, block.shape[1]), lambda i, at, k=k: (0, at[k]), pipeline_mode=pl.Buffered(1)
        )
        for k, block in enumerate(blocks)
    ]


def round_of(acc, blocks, places, out_weight, mixed, core, first=0, before=(), micros=0):
    rows = blocks[0].shape[0]
    width = out_weight.shape[0]
    n = len(blocks)
    groups = sum(block.shape[1] for block in blocks) // (2 * HEAD)
    at = jnp.stack([*places, core]).astype(jnp.int32)
    acc = [] if acc is None else [acc]
    by_core = pl.BlockSpec((groups, width, HEAD), lambda i, at: (0, 0, 0))
    by_core_shape = jax.ShapeDtypeStruct((groups, width, HEAD), f32)
    return pl.pallas_call(
        functools.partial(block_kernel, blocks=n, added=len(acc), summed=len(before)),
        grid_spec=pltpu.PrefetchScalarGridSpec(
            num_scalar_prefetch=1,
            grid=(rows // STEP,),
            in_specs=[rows_of(width, first) for _ in acc]
            + [rows_of(block.shape[1]) for block in blocks]
            + weight_specs(width, blocks)
            + [pl.BlockSpec((width, STEP), lambda i, at: (0, i + first // STEP))] * 2
            + [by_core] * len(before),
            out_specs=[rows_of(width, first)] + [by_core] * 2,
            scratch_shapes=[
                pltpu.VMEM((width, block.shape[1]), bf16) for block in blocks for _ in range(2)
            ],
        ),
        out_shape=[jax.ShapeDtypeStruct((SEG, width), f32)] + [by_core_shape] * 2,
        input_output_aliases={1: 0} if acc else {},
        compiler_params=pltpu.CompilerParams(vmem_limit_bytes=VMEM_LIMIT),
        cost_estimate=pl.CostEstimate(flops=LIGHT, bytes_accessed=LIGHT, transcendentals=0),
        name="round",
    )(at, *acc, *blocks, *([out_weight] * n), *mixed, *before)


def tail_of(second, acc, blocks, places, out_weight, mixed, core, whole, before):
    rows, deep = blocks[0].shape
    width = out_weight.shape[0]
    first = second * MOST
    by_core = deep // HEAD, width, HEAD
    sums = [(width // HEAD, ROWS, HEAD), by_core, by_core]
    sum_specs = [pl.BlockSpec(shape, lambda i, at: (0, 0, 0)) for shape in sums]
    return pl.pallas_call(
        tail_kernel,
        grid_spec=pltpu.PrefetchScalarGridSpec(
            num_scalar_prefetch=1,
            grid=(rows // STEP,),
            in_specs=[rows_of(width, first)]
            + [rows_of(deep)] * 2
            + weight_specs(width, blocks)
            + [rows_of(width, first)] * 3
            + [pl.BlockSpec((width, STEP), lambda i, at: (0, i + first // STEP))] * 2
            + sum_specs[: len(before)],
            out_specs=[rows_of(width), *sum_specs],
            scratch_shapes=[pltpu.VMEM((width, deep), bf16) for _ in range(4)],
        ),
        out_shape=[jax.ShapeDtypeStruct(shape, f32) for shape in [(rows, width), *sums]],
        compiler_params=pltpu.CompilerParams(vmem_limit_bytes=VMEM_LIMIT),
        cost_estimate=pl.CostEstimate(flops=LIGHT, bytes_accessed=LIGHT, transcendentals=0),
        name="tail",
    )(
        jnp.stack([*places, core]).astype(jnp.int32),
        acc, *blocks, out_weight, out_weight, *whole, *mixed, *before,
    )


def backward_kernel(*refs, first):
    q_ref, k_ref, v_ref, mg_ref, local_ref, memout_ref, lse_ref, mem_ref, g_ref = refs[:9]
    dq_ref, dk_ref, dv_ref = refs[-3:]
    g = g_ref[0]
    q = q_ref[...]
    mg = mg_ref[...]
    local_grad = (1.0 - g) * TEMPER * mg
    key = halves(k_ref[...])
    key_t = jnp.concatenate([key[0].T, key[1].T], axis=0)
    key = wide(key)
    value = wide(halves(v_ref[...]))
    query = halves(q * (TEMPER * LOG2E))
    q_twice, q_wide = doubled(query[0]), wide(query)
    grad = halves(local_grad)
    g_twice, g_wide = doubled(grad[0]), wide(grad)
    delta = jnp.sum((local_grad * local_ref[...]).T, axis=0, keepdims=True)
    lq = lifted(q)
    norm = mem_ref[0, HEAD : HEAD + 1, :]
    inverse = 1.0 / (jnp.sum(lq * norm, axis=1, keepdims=True) + 1.0)
    r = jnp.sum(mg * memout_ref[...], axis=1, keepdims=True)
    lift_grad = mm(halves(mg), halves(mem_ref[0, :HEAD, :].T), NN) - r * norm
    dq_ref[...] = lift_grad * (inverse * g) * lifted_slope(q)
    for ref, before in zip((dk_ref, dv_ref), refs[9:11] if first else (None, None)):
        ref[first:, :] = jnp.zeros(q.shape, f32)
        if first:
            ref[:first, :] = before[...]
    seen = causal(BACKWARD_QB)
    for qb in range(q.shape[0] // BACKWARD_QB):
        at = slice(qb * BACKWARD_QB, (qb + 1) * BACKWARD_QB)
        dq_t = 0.0
        for low, high, own in parts_of(qb + first // BACKWARD_QB, BACKWARD_QB):
            scores = scores_of(key[low:high], q_twice[at], query[1][at])
            if own:
                scores = jnp.where(seen, scores, -1e30)
            weights = jnp.exp2(scores - lse_ref[0, :, at])
            dp = scores_of(value[low:high], g_twice[at], grad[1][at])
            ds = halves(weights * (dp - delta[:, at]))
            dv_ref[low:high, :] += times_wide(halves(weights), g_wide[at])
            dk_ref[low:high, :] += times_wide(ds, q_wide[at])
            dq_t = dq_t + tall_times(key_t[:, low:high], ds)
        dq_ref[at, :] += dq_t.T
    if first:
        dk_ref[...] = dk_ref[...] * (1.0 / (TEMPER * LOG2E))
        dv_ref[...] = dv_ref[...] * (1.0 / TEMPER)


def backward_of(second, heads, ins, before, earlier, micros):
    width = ins[0].shape[1]
    low, count = heads

    def rows(n, at=0):
        return pl.BlockSpec((n, HEAD), lambda h: (at, h + low))

    def of_head(x, n=None, at=0):
        return pl.BlockSpec((1, x.shape[1], n or x.shape[2]), lambda h: (h + low, 0, at))

    size, at_part = (REST, MOST // REST) if second else (MOST, 0)
    here = rows(size, at_part)
    seen = rows(SEG if second else MOST)
    shapes = [(SEG, width)] + [(SEG if second else MOST, width)] * 2
    return pl.pallas_call(
        functools.partial(backward_kernel, first=second * MOST),
        grid=(count,),
        in_specs=[here, seen, seen, rows(size), here, here]
        + [of_head(ins[6], size, at_part), of_head(ins[7]), of_head(ins[8])]
        + [rows(MOST)] * len(before)
        + [pl.BlockSpec(memory_space=pl.ANY)] * len(earlier),
        out_specs=[here, seen, seen],
        out_shape=[jax.ShapeDtypeStruct(shape, f32) for shape in shapes],
        input_output_aliases={len(ins) + len(before) + i: i for i in range(len(earlier))},
        compiler_params=pltpu.CompilerParams(vmem_limit_bytes=VMEM_LIMIT),
        cost_estimate=pl.CostEstimate(
            flops=LIGHT, bytes_accessed=micros * MICROSECOND or LIGHT, transcendentals=0
        ),
        name="backward",
    )(*ins, *before, *earlier)


def forward_of(heads, ins, earlier):
    width = ins[0].shape[1]
    low, count = heads
    column = pl.BlockSpec((SEG, HEAD), lambda h: (0, h + low))
    line = pl.BlockSpec((1, 1, SEG), lambda h: (h + low, 0, 0))
    return pl.pallas_call(
        forward_kernel,
        grid=(count,),
        in_specs=[column] * 3 + [pl.BlockSpec(memory_space=pl.ANY)] * len(earlier),
        out_specs=[column, line],
        out_shape=[
            jax.ShapeDtypeStruct((SEG, width), f32),
            jax.ShapeDtypeStruct((width // HEAD, 1, SEG), f32),
        ],
        input_output_aliases={len(ins) + i: i for i in range(len(earlier))},
        compiler_params=pltpu.CompilerParams(vmem_limit_bytes=VMEM_LIMIT),
        cost_estimate=pl.CostEstimate(flops=LIGHT, bytes_accessed=LIGHT, transcendentals=0),
        name="forward",
    )(*ins, *earlier)


def finish_kernel(k_ref, v_ref, dk_ref, dv_ref, state_ref, kg_ref, vg_ref):
    key = k_ref[...]
    state = state_ref[0, :HEAD, :]
    norm = state_ref[0, HEAD : HEAD + 1, :]
    lift_grad = mm(halves(v_ref[...]), halves(state.T), NN) + norm
    kg_ref[...] = dk_ref[...] + lift_grad * lifted_slope(key)
    vg_ref[...] = dv_ref[...] + mm(halves(lifted(key)), halves(state), NN)


def columns():
    return pl.BlockSpec((SEG, HEAD), lambda h: (0, h))


def state():
    return pl.BlockSpec((1, ROWS, HEAD), lambda h: (h, 0, 0))


def row(width):
    return pl.BlockSpec((1, 1, width), lambda h: (h, 0, 0))


def per_head(kernel, heads, ins, outs, name):
    width = heads * HEAD
    kinds = {
        "c": (columns(), jax.ShapeDtypeStruct((SEG, width), f32)),
        "s": (state(), jax.ShapeDtypeStruct((heads, ROWS, HEAD), f32)),
        "g": (row(HEAD), jax.ShapeDtypeStruct((heads, 1, HEAD), f32)),
        "t": (
            pl.BlockSpec((HEAD, SEG), lambda h: (h, 0)),
            jax.ShapeDtypeStruct((width, SEG), bf16),
        ),
        "l": (row(SEG), jax.ShapeDtypeStruct((heads, 1, SEG), f32)),
    }
    return pl.pallas_call(
        kernel,
        grid=(heads,),
        in_specs=[kinds[i][0] for i in ins],
        out_specs=[kinds[o][0] for o in outs],
        out_shape=[kinds[o][1] for o in outs],
        compiler_params=pltpu.CompilerParams(vmem_limit_bytes=VMEM_LIMIT),
        cost_estimate=pl.CostEstimate(
            flops=LIGHT, bytes_accessed=LIGHT, transcendentals=0
        ),
        name=name,
    )


def ring(n, step):
    return [(i, (i + step) % n) for i in range(n)]


def grid_sizes():
    heads = lax.axis_size("head")
    return heads, lax.axis_size("ctx") // (2 * heads)


def place():
    xs, zs = grid_sizes()
    at = lax.axis_index("ctx")
    return at // (2 * zs), (at // 2) % zs, at % 2


def core_swap(block):
    n = lax.axis_size("ctx")
    return lax.ppermute(block, "ctx", [(i, i ^ 1) for i in range(n)])


def moved(block, axis, to):
    xs, zs = grid_sizes()
    pairs = []
    for x in range(xs):
        for z in range(zs):
            x_to, z_to = (to(x), z) if axis == "x" else (x, to(z))
            if x_to is not None and z_to is not None:
                for c in range(2):
                    pairs.append(((x * zs + z) * 2 + c, (x_to * zs + z_to) * 2 + c))
    return lax.ppermute(block, "ctx", pairs)


def scan_of_four(block, axis, at, later, beside_first, beside_second):
    near = beside_first(moved(block, axis, lambda i: i ^ 1))
    pair = block + near
    other = beside_second(moved(pair, axis, lambda i: 3 - i))
    counts_near = (at % 2 == 0) if later else (at % 2 == 1)
    counts_other = (at < 2) if later else (at >= 2)
    return jnp.where(counts_near, near, 0.0) + jnp.where(counts_other, other, 0.0), pair + other


def scan_over_ctx(packed, later, work=None):
    xs, zs = grid_sizes()
    x, z, core = place()
    half = packed.shape[0] // 2
    first, second = packed[:half], packed[half:]
    is_first = core == 0
    mine = jnp.where(is_first, first, second)
    theirs = core_swap(jnp.where(is_first, second, first))
    chip = mine + theirs

    def beside_step(i):
        def tie(arrived):
            if work is None:
                return arrived
            done = work(i)
            arrived, *done[:] = lax.optimization_barrier((arrived, *done))
            return arrived

        return tie

    before_z, total_z = scan_of_four(chip, "z", z, later, beside_step(0), beside_step(1))
    before_x, total = scan_of_four(
        total_z, "x", x, later, beside_step(2), beside_step(3)
    )
    outside = before_z + before_x
    counts_other = is_first if later else jnp.logical_not(is_first)
    for_me = outside + jnp.where(counts_other, theirs, 0.0)
    for_other = outside + jnp.where(counts_other, 0.0, mine)
    row = lax.broadcasted_iota(jnp.int32, (1, ROWS, 1), 1)
    totals = jnp.where(row == ROWS - 1, total[:, HEAD + 1 : HEAD + 2, :], 0.0)
    for_me, for_other = for_me + totals, for_other + totals
    swapped = core_swap(for_other)
    low = jnp.where(is_first, for_me, swapped)
    high = jnp.where(is_first, swapped, for_me)
    return jnp.concatenate([low, high], axis=0)


def across(i):
    return 3 - i


def beside(i):
    return i ^ 1


def outgoing(piece, at, first, second):
    far = first(at)
    return jnp.stack([piece(far), piece(second(far))])


def half_scattered(piece, axis, at, first, second, sent=None):
    sent = outgoing(piece, at, first, second) if sent is None else sent
    came = moved(sent, axis, first)
    return piece(at) + came[0], piece(second(at)) + came[1]


def scattered(kept, passed, axis, second):
    return kept + moved(passed, axis, second)


def at_place(pieces, i):
    return lax.dynamic_index_in_dim(pieces, i, 0, keepdims=False)


def on_device(queries, keys, values, gate_logit, out_weight, out_grad):
    heads = gate_logit.shape[0]
    width = heads * HEAD
    hs = lax.axis_size("head")
    head = lax.axis_index("head")
    xs, zs = grid_sizes()
    x, z, core = place()
    rows, cols = out_grad.shape

    half = cols // 2

    def up(block):
        return lax.ppermute(block, "head", ring(hs, 1))

    def down(block):
        return lax.ppermute(block, "head", ring(hs, -1))

    left, right = up(out_grad), down(out_grad)

    gate = jax.nn.sigmoid(gate_logit)
    g = jnp.broadcast_to(gate[:, None, None], (heads, 1, HEAD))

    (packed,) = per_head(update_kernel, heads, "cc", "s", "update")(keys, values)
    forwards = []

    def forward(step):
        if step % 2 == 0:
            forwards[:] = forward_of((step, heads // 2), (queries, keys, values), forwards)
        return forwards

    before = scan_over_ctx(packed, False, forward)
    local_out, lse = forwards
    *mixed, memory_out, lqd = per_head(mix_kernel, heads, "ccsg", "ttcc", "mix")(
        queries, local_out, before, g
    )

    def block_at(distance):
        return (head + hs - distance) % hs

    own_at, left_at, far_at, right_at = (block_at(d) for d in range(4))
    add = functools.partial(round_of, out_weight=out_weight, mixed=mixed, core=core)

    def chip_piece(mine, came, start=0):
        return lambda i: at_place(mine, start + i) + at_place(came, start + i)

    mg, mine_own, send_own = add(None, [out_grad], [own_at])
    came_own = core_swap(send_own)
    own_parts = half_scattered(chip_piece(mine_own, came_own), "z", z, across, beside)
    left, right, *own_parts = lax.optimization_barrier((left, right, *own_parts))
    far_1 = up(left[:MOST, :half]), down(right[:MOST, half:])
    far_2 = up(left[MOST:, :half]), down(right[MOST:, half:])

    mg, mine_sides, send_sides = add(mg, [left, right], [left_at, right_at])
    *far_1, mine_sides, send_sides = lax.optimization_barrier((*far_1, mine_sides, send_sides))
    came_sides = core_swap(send_sides)
    far_places = [2 * far_at, 2 * far_at + 1]
    tail = functools.partial(
        tail_of, places=far_places, out_weight=out_weight, mixed=mixed, core=core,
        whole=(lqd, memory_out, local_out),
    )
    mg_1, *far_sums = tail(0, mg, far_1, before=())
    attended = queries, keys, values

    def backward_ins(part):
        return (*attended, part, local_out, memory_out, lse, before, g)

    sum_own = scattered(*own_parts, "z", beside)
    mg_1, came_sides = lax.optimization_barrier((mg_1, came_sides))
    left_parts = half_scattered(chip_piece(mine_sides, came_sides), "z", z, across, beside)
    right_parts = half_scattered(chip_piece(mine_sides, came_sides, zs), "z", z, beside, across)
    early = backward_of(0, (0, heads), backward_ins(mg_1), (), (), 0)
    *far_2, dq, dk, dv, left_kept, left_passed, right_kept, right_passed, sum_own = (
        lax.optimization_barrier((*far_2, *early, *left_parts, *right_parts, sum_own))
    )
    mg_2, back, mine_far, send_far = tail(1, mg, far_2, before=far_sums)
    sum_left = scattered(left_kept, left_passed, "z", beside)
    sum_right = scattered(right_kept, right_passed, "z", across)
    came_far = core_swap(send_far)
    far_parts = half_scattered(chip_piece(mine_far, came_far), "z", z, across, beside)

    pairs = [(0, heads // 2), (heads // 2, heads // 2)]
    held = {}

    def beside_scan(step):
        if step == 0:
            grads = backward_of(1, pairs[0], backward_ins(mg_2), (dk, dv), [dq], 6)
            held[0] = [*grads, sum_left, sum_right]
        elif step == 1:
            held[1] = list(far_parts)
        elif step == 2:
            grads = backward_of(1, pairs[1], backward_ins(mg_2), (dk, dv), held[0][:3], 6)
            held[2] = [*grads, scattered(*held[1], "z", beside)]
        else:
            held[3] = [outgoing(piece_x, x, across, beside)]
        return held[step]

    def piece_x(i):
        parts = jnp.stack([sum_own, held[0][3], held[2][3], held[0][4]])
        return at_place(parts, (head + hs - i) % hs)

    after = scan_over_ctx(back, True, beside_scan)
    x_parts = half_scattered(piece_x, "x", x, across, beside, held[3][0])
    weight_grad = scattered(*x_parts, "x", beside).T

    key_grad, value_grad = per_head(finish_kernel, heads, "ccccs", "cc", "finish")(
        keys, values, *held[2][1:3], after
    )
    dq = held[2][0]

    gate_sum = jnp.sum(after[:, ROWS - 1, :], axis=-1)
    gate_grad = gate_sum * gate * (1.0 - gate)
    return dq, key_grad, value_grad, weight_grad, gate_grad


def solution(mesh):
    in_specs = (
        P("ctx", "head"),
        P("ctx", "head"),
        P("ctx", "head"),
        P("head"),
        P("head", None),
        P("ctx", "head"),
    )
    out_specs = (P("ctx", "head"), P("ctx", "head"), P("ctx", "head"), P("ctx", "head"), P("head"))
    return jax.shard_map(
        on_device, mesh=mesh, in_specs=in_specs, out_specs=out_specs, check_vma=False
    )
```

```python
import functools
import math

import jax
import jax.numpy as jnp
from jax import lax
from jax.experimental import pallas as pl
from jax.experimental.pallas import tpu as pltpu
from jax.sharding import PartitionSpec as P

SEG = 1024
HEAD = 128
ROWS = 136
FORWARD_QB = 512
BACKWARD_QB = 256
MOST = SEG // 2
REST = SEG - MOST
STEP = 256
LIGHT = 2**16
VMEM_LIMIT = 60 * 2**20
MICROSECOND = 3_600_000

f32 = jnp.float32
bf16 = jnp.bfloat16
HIGH = lax.Precision.HIGH


def lifted(x):
    return jnp.where(x > 0, x + 1.0, jnp.exp(jnp.minimum(x, 0.0)))


def lifted_slope(x):
    return jnp.where(x > 0, 1.0, jnp.exp(jnp.minimum(x, 0.0)))


def halves(x):
    hi = x.astype(bf16)
    return hi, (x - hi.astype(f32)).astype(bf16)


def mm(a, b, contract):
    dims = ((contract[:1], contract[1:]), ((), ()))

    def one(x, y):
        return lax.dot_general(x, y, dims, preferred_element_type=f32)

    return one(a[0], b[0]) + (one(a[0], b[1]) + one(a[1], b[0]))


NN = (1, 0)
NT = (1, 1)
TN = (0, 0)


def dot(a, b, contract):
    return lax.dot_general(
        a, b, ((contract[:1], contract[1:]), ((), ())), preferred_element_type=f32
    )


def wide(pair):
    return jnp.concatenate(pair, axis=1)


def doubled(x):
    return jnp.concatenate([x, x], axis=1)


def scores_of(a_wide, b_hi_twice, b_lo):
    return dot(a_wide, b_hi_twice, NT) + dot(a_wide[:, :HEAD], b_lo, NT)


def times_wide(a, b_wide):
    both = dot(a[0], b_wide, NN)
    return both[:, :HEAD] + (both[:, HEAD:] + dot(a[1], b_wide[:, :HEAD], NN))


def tall_times(a_tall, b):
    both = dot(a_tall, b[0], NN)
    return both[:HEAD] + (both[HEAD:] + dot(a_tall[:HEAD], b[1], NN))


def update_kernel(k_ref, v_ref, out_ref):
    lk = lifted(k_ref[...])
    out_ref[0, :HEAD, :] = mm(halves(lk.T), halves(v_ref[...]), NN)
    out_ref[0, HEAD : HEAD + 1, :] = jnp.sum(lk, axis=0, keepdims=True)
    out_ref[0, HEAD + 1 :, :] = jnp.zeros((ROWS - HEAD - 1, HEAD), f32)


LOG2E = math.log2(math.e)
TEMPER = 1.0 / math.sqrt(HEAD)


def parts_of(qb, size):
    return ([(0, qb * size, False)] if qb else []) + [(qb * size, (qb + 1) * size, True)]


def causal(size):
    t = lax.broadcasted_iota(jnp.int32, (size, size), 0)
    return t <= lax.broadcasted_iota(jnp.int32, (size, size), 1)


def forward_kernel(q_ref, k_ref, v_ref, *refs):
    out_ref, lse_ref = refs[-2:]
    key = wide(halves(k_ref[...]))
    value_t = jnp.concatenate(halves(v_ref[...].T), axis=0)
    q_hi, q_lo = halves(q_ref[...] * (TEMPER * LOG2E))
    q_twice = doubled(q_hi)
    seen = causal(FORWARD_QB)
    for qb in range(SEG // FORWARD_QB):
        at = slice(qb * FORWARD_QB, (qb + 1) * FORWARD_QB)
        scores = []
        for low, high, own in parts_of(qb, FORWARD_QB):
            part = scores_of(key[low:high], q_twice[at], q_lo[at])
            scores.append(jnp.where(seen, part, -1e30) if own else part)
        top = functools.reduce(
            jnp.maximum, [jnp.max(part, axis=0, keepdims=True) for part in scores]
        )
        total, out_t = 0.0, 0.0
        for (low, high, _), part in zip(parts_of(qb, FORWARD_QB), scores):
            weights = jnp.exp2(part - top)
            total = total + jnp.sum(weights, axis=0, keepdims=True)
            out_t = out_t + tall_times(value_t[:, low:high], halves(weights))
        out_ref[at, :] = (out_t * (1.0 / total)).T
        lse_ref[0, :, at] = top + jnp.log2(total)


def mix_kernel(q_ref, local_ref, mem_ref, g_ref, hi_ref, lo_ref, memout_ref, lqd_ref):
    g = g_ref[0]
    lq = lifted(q_ref[...])
    norm = mem_ref[0, HEAD : HEAD + 1, :]
    denom = jnp.sum(lq * norm, axis=1, keepdims=True) + 1.0
    inverse = 1.0 / denom
    memory_out = mm(halves(lq), halves(mem_ref[0, :HEAD, :]), NN) * inverse
    memout_ref[...] = memory_out
    mixed = g * memory_out + (1.0 - g) * local_ref[...]
    hi_ref[...], lo_ref[...] = halves(mixed.T)
    lqd_ref[...] = lq * (inverse * g)


def add_weight_part(mixed, block, first, start, mine_ref, send_ref):
    part = mm(mixed, block, NN)
    groups = part.shape[1] // (2 * HEAD)
    for k in range(groups):
        even = part[:, 2 * k * HEAD : (2 * k + 1) * HEAD]
        odd = part[:, (2 * k + 1) * HEAD : (2 * k + 2) * HEAD]
        mine_ref[start + k] += jnp.where(first, even, odd)
        send_ref[start + k] += jnp.where(first, odd, even)


def block_kernel(at_ref, *refs, blocks, added, summed):
    refs = list(refs)

    def take(n):
        taken, refs[:] = refs[:n], refs[n:]
        return taken

    acc, block_refs, w_refs, mixed_refs = take(added), take(blocks), take(blocks), take(2)
    before, (out_ref,), by_core = take(summed), take(1), take(2)

    @pl.when(pl.program_id(0) == 0)
    def _():
        for n, w_ref in enumerate(w_refs):
            refs[2 * n][...], refs[2 * n + 1][...] = halves(w_ref[...])
        for n, ref in enumerate(by_core):
            ref[...] = before[n][...] if summed else jnp.zeros_like(ref)

    mixed = tuple(ref[...] for ref in mixed_refs)
    total = acc[0][...] if added else None
    start = 0
    for n, block_ref in enumerate(block_refs):
        block = halves(block_ref[...])
        product = mm(block, (refs[2 * n][...], refs[2 * n + 1][...]), NT)
        total = product if total is None else total + product
        add_weight_part(mixed, block, at_ref[blocks] == 0, start, *by_core)
        start += block_ref.shape[1] // (2 * HEAD)
    out_ref[...] = total


def tail_kernel(at_ref, *refs):
    acc_ref, a_ref, b_ref, wa_ref, wb_ref, lqd_ref, memout_ref, local_ref = refs[:8]
    mhi_ref, mlo_ref, *before = refs[8:-8]
    mg_ref, state_ref, mine_ref, send_ref, *w = refs[-8:]

    @pl.when(pl.program_id(0) == 0)
    def _():
        w[0][...], w[1][...] = halves(wa_ref[...])
        w[2][...], w[3][...] = halves(wb_ref[...])
        for n, ref in enumerate((state_ref, mine_ref, send_ref)):
            ref[...] = before[n][...] if before else jnp.zeros_like(ref)

    a, b = halves(a_ref[...]), halves(b_ref[...])
    mg = acc_ref[...] + mm(a, (w[0][...], w[1][...]), NT)
    mg = mg + mm(b, (w[2][...], w[3][...]), NT)
    mg_ref[...] = mg
    for h in range(state_ref.shape[0]):
        at = slice(h * HEAD, (h + 1) * HEAD)
        here, lqd, memory_out = mg[:, at], lqd_ref[:, at], memout_ref[:, at]
        state_ref[h, :HEAD, :] += mm(halves(lqd.T), halves(here), NN)
        r = jnp.sum(here * memory_out, axis=1, keepdims=True)
        state_ref[h, HEAD : HEAD + 1, :] -= jnp.sum(lqd * r, axis=0, keepdims=True)
        state_ref[h, HEAD + 1 : HEAD + 2, :] += jnp.sum(
            here * (memory_out - local_ref[:, at]), axis=0, keepdims=True
        )
    mixed, first = (mhi_ref[...], mlo_ref[...]), at_ref[2] == 0
    groups = a_ref.shape[1] // (2 * HEAD)
    add_weight_part(mixed, a, first, 0, mine_ref, send_ref)
    add_weight_part(mixed, b, first, groups, mine_ref, send_ref)


def rows_of(width, first=0):
    return pl.BlockSpec((STEP, width), lambda i, at: (i + first // STEP, 0))


def weight_specs(width, blocks):
    return [
        pl.BlockSpec(
            (width, block.shape[1]), lambda i, at, k=k: (0, at[k]), pipeline_mode=pl.Buffered(1)
        )
        for k, block in enumerate(blocks)
    ]


def tail_kernel(at_ref, *refs):
    acc_ref, a_ref, b_ref, wa_ref, wb_ref, lqd_ref, memout_ref, local_ref = refs[:8]
    mhi_ref, mlo_ref, *before = refs[8:-8]
    mg_ref, state_ref, mine_ref, send_ref, *w = refs[-8:]

    @pl.when(pl.program_id(0) == 0)
    def _():
        w[0][...], w[1][...] = halves(wa_ref[...])
        w[2][...], w[3][...] = halves(wb_ref[...])
        for n, ref in enumerate((state_ref, mine_ref, send_ref)):
            ref[...] = before[n][...] if before else jnp.zeros_like(ref)

    a, b = halves(a_ref[...]), halves(b_ref[...])
    mg = acc_ref[...] + mm(a, (w[0][...], w[1][...]), NT)
    mg = mg + mm(b, (w[2][...], w[3][...]), NT)
    mg_ref[...] = mg
    for h in range(state_ref.shape[0]):
        at = slice(h * HEAD, (h + 1) * HEAD)
        here, lqd, memory_out = mg[:, at], lqd_ref[:, at], memout_ref[:, at]
        state_ref[h, :HEAD, :] += mm(halves(lqd.T), halves(here), NN)
        r = jnp.sum(here * memory_out, axis=1, keepdims=True)
        state_ref[h, HEAD : HEAD + 1, :] -= jnp.sum(lqd * r, axis=0, keepdims=True)
        state_ref[h, HEAD + 1 : HEAD + 2, :] += jnp.sum(
            here * (memory_out - local_ref[:, at]), axis=0, keepdims=True
        )
    mixed, first = (mhi_ref[...], mlo_ref[...]), at_ref[2] == 0
    groups = a_ref.shape[1] // (2 * HEAD)
    add_weight_part(mixed, a, first, 0, mine_ref, send_ref)
    add_weight_part(mixed, b, first, groups, mine_ref, send_ref)


def rows_of(width, first=0):
    return pl.BlockSpec((STEP, width), lambda i, at: (i + first // STEP, 0))


def weight_specs(width, blocks):
    return [
        pl.BlockSpec(
            (width, block.shape[1]), lambda i, at, k=k: (0, at[k]), pipeline_mode=pl.Buffered(1)
        )
        for k, block in enumerate(blocks)
    ]


def tail_kernel(at_ref, *refs):
    acc_ref, a_ref, b_ref, wa_ref, wb_ref, lqd_ref, memout_ref, local_ref = refs[:8]
    mhi_ref, mlo_ref, *before = refs[8:-8]
    mg_ref, state_ref, mine_ref, send_ref, *w = refs[-8:]

    @pl.when(pl.program_id(0) == 0)
    def _():
        w[0][...], w[1][...] = halves(wa_ref[...])
        w[2][...], w[3][...] = halves(wb_ref[...])
        for n, ref in enumerate((state_ref, mine_ref, send_ref)):
            ref[...] = before[n][...] if before else jnp.zeros_like(ref)

    a, b = halves(a_ref[...]), halves(b_ref[...])
    mg = acc_ref[...] + mm(a, (w[0][...], w[1][...]), NT)
    mg = mg + mm(b, (w[2][...], w[3][...]), NT)
    mg_ref[...] = mg
    for h in range(state_ref.shape[0]):
        at = slice(h * HEAD, (h + 1) * HEAD)
        here, lqd, memory_out = mg[:, at], lqd_ref[:, at], memout_ref[:, at]
        state_ref[h, :HEAD, :] += mm(halves(lqd.T), halves(here), NN)
        r = jnp.sum(here * memory_out, axis=1, keepdims=True)
        state_ref[h, HEAD : HEAD + 1, :] -= jnp.sum(lqd * r, axis=0, keepdims=True)
        state_ref[h, HEAD + 1 : HEAD + 2, :] += jnp.sum(
            here * (memory_out - local_ref[:, at]), axis=0, keepdims=True
        )
    mixed, first = (mhi_ref[...], mlo_ref[...]), at_ref[2] == 0
    groups = a_ref.shape[1] // (2 * HEAD)
    add_weight_part(mixed, a, first, 0, mine_ref, send_ref)
    add_weight_part(mixed, b, first, groups, mine_ref, send_ref)


def rows_of(width, first=0):
    return pl.BlockSpec((STEP, width), lambda i, at: (i + first // STEP, 0))


def weight_specs(width, blocks):
    return [
        pl.BlockSpec(
            (width, block.shape[1]), lambda i, at, k=k: (0, at[k]), pipeline_mode=pl.Buffered(1)
        )
        for k, block in enumerate(blocks)
    ]


def tail_kernel(at_ref, *refs):
    acc_ref, a_ref, b_ref, wa_ref, wb_ref, lqd_ref, memout_ref, local_ref = refs[:8]
    mhi_ref, mlo_ref, *before = refs[8:-8]
    mg_ref, state_ref, mine_ref, send_ref, *w = refs[-8:]

    @pl.when(pl.program_id(0) == 0)
    def _():
        w[0][...], w[1][...] = halves(wa_ref[...])
        w[2][...], w[3][...] = halves(wb_ref[...])
        for n, ref in enumerate((state_ref, mine_ref, send_ref)):
            ref[...] = before[n][...] if before else jnp.zeros_like(ref)

    a, b = halves(a_ref[...]), halves(b_ref[...])
    mg = acc_ref[...] + mm(a, (w[0][...], w[1][...]), NT)
    mg = mg + mm(b, (w[2][...], w[3][...]), NT)
    mg_ref[...] = mg
    for h in range(state_ref.shape[0]):
        at = slice(h * HEAD, (h + 1) * HEAD)
        here, lqd, memory_out = mg[:, at], lqd_ref[:, at], memout_ref[:, at]
        state_ref[h, :HEAD, :] += mm(halves(lqd.T), halves(here), NN)
        r = jnp.sum(here * memory_out, axis=1, keepdims=True)
        state_ref[h, HEAD : HEAD + 1, :] -= jnp.sum(lqd * r, axis=0, keepdims=True)
        state_ref[h, HEAD + 1 : HEAD + 2, :] += jnp.sum(
            here * (memory_out - local_ref[:, at]), axis=0, keepdims=True
        )
    mixed, first = (mhi_ref[...], mlo_ref[...]), at_ref[2] == 0
    groups = a_ref.shape[1] // (2 * HEAD)
    add_weight_part(mixed, a, first, 0, mine_ref, send_ref)
    add_weight_part(mixed, b, first, groups, mine_ref, send_ref)


def rows_of(width, first=0):
    return pl.BlockSpec((STEP, width), lambda i, at: (i + first // STEP, 0))


def weight_specs(width, blocks):
    return [
        pl.BlockSpec(
            (width, block.shape[1]), lambda i, at, k=k: (0, at[k]), pipeline_mode=pl.Buffered(1)
        )
        for k, block in enumerate(blocks)
    ]


def round_of(acc, blocks, places, out_weight, mixed, core, first=0, before=(), micros=0):
    rows = blocks[0].shape[0]
    width = out_weight.shape[0]
    n = len(blocks)
    groups = sum(block.shape[1] for block in blocks) // (2 * HEAD)
    at = jnp.stack([*places, core]).astype(jnp.int32)
    acc = [] if acc is None else [acc]
    by_core = pl.BlockSpec((groups, width, HEAD), lambda i, at: (0, 0, 0))
    by_core_shape = jax.ShapeDtypeStruct((groups, width, HEAD), f32)
    return pl.pallas_call(
        functools.partial(block_kernel, blocks=n, added=len(acc), summed=len(before)),
        grid_spec=pltpu.PrefetchScalarGridSpec(
            num_scalar_prefetch=1,
            grid=(rows // STEP,),
            in_specs=[rows_of(width, first) for _ in acc]
            + [rows_of(block.shape[1]) for block in blocks]
            + weight_specs(width, blocks)
            + [pl.BlockSpec((width, STEP), lambda i, at: (0, i + first // STEP))] * 2
            + [by_core] * len(before),
            out_specs=[rows_of(width, first)] + [by_core] * 2,
            scratch_shapes=[
                pltpu.VMEM((width, block.shape[1]), bf16) for block in blocks for _ in range(2)
            ],
        ),
        out_shape=[jax.ShapeDtypeStruct((SEG, width), f32)] + [by_core_shape] * 2,
        input_output_aliases={1: 0} if acc else {},
        compiler_params=pltpu.CompilerParams(vmem_limit_bytes=VMEM_LIMIT),
        cost_estimate=pl.CostEstimate(flops=LIGHT, bytes_accessed=LIGHT, transcendentals=0),
        name="round",
    )(at, *acc, *blocks, *([out_weight] * n), *mixed, *before)


def tail_of(second, acc, blocks, places, out_weight, mixed, core, whole, before):
    rows, deep = blocks[0].shape
    width = out_weight.shape[0]
    first = second * MOST
    by_core = deep // HEAD, width, HEAD
    sums = [(width // HEAD, ROWS, HEAD), by_core, by_core]
    sum_specs = [pl.BlockSpec(shape, lambda i, at: (0, 0, 0)) for shape in sums]
    return pl.pallas_call(
        tail_kernel,
        grid_spec=pltpu.PrefetchScalarGridSpec(
            num_scalar_prefetch=1,
            grid=(rows // STEP,),
            in_specs=[rows_of(width, first)]
            + [rows_of(deep)] * 2
            + weight_specs(width, blocks)
            + [rows_of(width, first)] * 3
            + [pl.BlockSpec((width, STEP), lambda i, at: (0, i + first // STEP))] * 2
            + sum_specs[: len(before)],
            out_specs=[rows_of(width), *sum_specs],
            scratch_shapes=[pltpu.VMEM((width, deep), bf16) for _ in range(4)],
        ),
        out_shape=[jax.ShapeDtypeStruct(shape, f32) for shape in [(rows, width), *sums]],
        compiler_params=pltpu.CompilerParams(vmem_limit_bytes=VMEM_LIMIT),
        cost_estimate=pl.CostEstimate(flops=LIGHT, bytes_accessed=LIGHT, transcendentals=0),
        name="tail",
    )(
        jnp.stack([*places, core]).astype(jnp.int32),
        acc, *blocks, out_weight, out_weight, *whole, *mixed, *before,
    )


def backward_kernel(*refs, first):
    q_ref, k_ref, v_ref, mg_ref, local_ref, memout_ref, lse_ref, mem_ref, g_ref = refs[:9]
    dq_ref, dk_ref, dv_ref = refs[-3:]
    g = g_ref[0]
    q = q_ref[...]
    mg = mg_ref[...]
    local_grad = (1.0 - g) * TEMPER * mg
    key = halves(k_ref[...])
    key_t = jnp.concatenate([key[0].T, key[1].T], axis=0)
    key = wide(key)
    value = wide(halves(v_ref[...]))
    query = halves(q * (TEMPER * LOG2E))
    q_twice, q_wide = doubled(query[0]), wide(query)
    grad = halves(local_grad)
    g_twice, g_wide = doubled(grad[0]), wide(grad)
    delta = jnp.sum((local_grad * local_ref[...]).T, axis=0, keepdims=True)
    lq = lifted(q)
    norm = mem_ref[0, HEAD : HEAD + 1, :]
    inverse = 1.0 / (jnp.sum(lq * norm, axis=1, keepdims=True) + 1.0)
    r = jnp.sum(mg * memout_ref[...], axis=1, keepdims=True)
    lift_grad = mm(halves(mg), halves(mem_ref[0, :HEAD, :].T), NN) - r * norm
    dq_ref[...] = lift_grad * (inverse * g) * lifted_slope(q)
    for ref, before in zip((dk_ref, dv_ref), refs[9:11] if first else (None, None)):
        ref[first:, :] = jnp.zeros(q.shape, f32)
        if first:
            ref[:first, :] = before[...]
    seen = causal(BACKWARD_QB)
    for qb in range(q.shape[0] // BACKWARD_QB):
        at = slice(qb * BACKWARD_QB, (qb + 1) * BACKWARD_QB)
        dq_t = 0.0
        for low, high, own in parts_of(qb + first // BACKWARD_QB, BACKWARD_QB):
            scores = scores_of(key[low:high], q_twice[at], query[1][at])
            if own:
                scores = jnp.where(seen, scores, -1e30)
            weights = jnp.exp2(scores - lse_ref[0, :, at])
            dp = scores_of(value[low:high], g_twice[at], grad[1][at])
            ds = halves(weights * (dp - delta[:, at]))
            dv_ref[low:high, :] += times_wide(halves(weights), g_wide[at])
            dk_ref[low:high, :] += times_wide(ds, q_wide[at])
            dq_t = dq_t + tall_times(key_t[:, low:high], ds)
        dq_ref[at, :] += dq_t.T
    if first:
        dk_ref[...] = dk_ref[...] * (1.0 / (TEMPER * LOG2E))
        dv_ref[...] = dv_ref[...] * (1.0 / TEMPER)


def backward_of(second, heads, ins, before, earlier, micros):
    width = ins[0].shape[1]
    low, count = heads

    def rows(n, at=0):
        return pl.BlockSpec((n, HEAD), lambda h: (at, h + low))

    def of_head(x, n=None, at=0):
        return pl.BlockSpec((1, x.shape[1], n or x.shape[2]), lambda h: (h + low, 0, at))

    size, at_part = (REST, MOST // REST) if second else (MOST, 0)
    here = rows(size, at_part)
    seen = rows(SEG if second else MOST)
    shapes = [(SEG, width)] + [(SEG if second else MOST, width)] * 2
    return pl.pallas_call(
        functools.partial(backward_kernel, first=second * MOST),
        grid=(count,),
        in_specs=[here, seen, seen, rows(size), here, here]
        + [of_head(ins[6], size, at_part), of_head(ins[7]), of_head(ins[8])]
        + [rows(MOST)] * len(before)
        + [pl.BlockSpec(memory_space=pl.ANY)] * len(earlier),
        out_specs=[here, seen, seen],
        out_shape=[jax.ShapeDtypeStruct(shape, f32) for shape in shapes],
        input_output_aliases={len(ins) + len(before) + i: i for i in range(len(earlier))},
        compiler_params=pltpu.CompilerParams(vmem_limit_bytes=VMEM_LIMIT),
        cost_estimate=pl.CostEstimate(
            flops=LIGHT, bytes_accessed=micros * MICROSECOND or LIGHT, transcendentals=0
        ),
        name="backward",
    )(*ins, *before, *earlier)


def forward_of(heads, ins, earlier):
    width = ins[0].shape[1]
    low, count = heads
    column = pl.BlockSpec((SEG, HEAD), lambda h: (0, h + low))
    line = pl.BlockSpec((1, 1, SEG), lambda h: (h + low, 0, 0))
    return pl.pallas_call(
        forward_kernel,
        grid=(count,),
        in_specs=[column] * 3 + [pl.BlockSpec(memory_space=pl.ANY)] * len(earlier),
        out_specs=[column, line],
        out_shape=[
            jax.ShapeDtypeStruct((SEG, width), f32),
            jax.ShapeDtypeStruct((width // HEAD, 1, SEG), f32),
        ],
        input_output_aliases={len(ins) + i: i for i in range(len(earlier))},
        compiler_params=pltpu.CompilerParams(vmem_limit_bytes=VMEM_LIMIT),
        cost_estimate=pl.CostEstimate(flops=LIGHT, bytes_accessed=LIGHT, transcendentals=0),
        name="forward",
    )(*ins, *earlier)


def finish_kernel(k_ref, v_ref, dk_ref, dv_ref, state_ref, kg_ref, vg_ref):
    key = k_ref[...]
    state = state_ref[0, :HEAD, :]
    norm = state_ref[0, HEAD : HEAD + 1, :]
    lift_grad = mm(halves(v_ref[...]), halves(state.T), NN) + norm
    kg_ref[...] = dk_ref[...] + lift_grad * lifted_slope(key)
    vg_ref[...] = dv_ref[...] + mm(halves(lifted(key)), halves(state), NN)


def columns():
    return pl.BlockSpec((SEG, HEAD), lambda h: (0, h))


def state():
    return pl.BlockSpec((1, ROWS, HEAD), lambda h: (h, 0, 0))


def row(width):
    return pl.BlockSpec((1, 1, width), lambda h: (h, 0, 0))


def per_head(kernel, heads, ins, outs, name):
    width = heads * HEAD
    kinds = {
        "c": (columns(), jax.ShapeDtypeStruct((SEG, width), f32)),
        "s": (state(), jax.ShapeDtypeStruct((heads, ROWS, HEAD), f32)),
        "g": (row(HEAD), jax.ShapeDtypeStruct((heads, 1, HEAD), f32)),
        "t": (
            pl.BlockSpec((HEAD, SEG), lambda h: (h, 0)),
            jax.ShapeDtypeStruct((width, SEG), bf16),
        ),
        "l": (row(SEG), jax.ShapeDtypeStruct((heads, 1, SEG), f32)),
    }
    return pl.pallas_call(
        kernel,
        grid=(heads,),
        in_specs=[kinds[i][0] for i in ins],
        out_specs=[kinds[o][0] for o in outs],
        out_shape=[kinds[o][1] for o in outs],
        compiler_params=pltpu.CompilerParams(vmem_limit_bytes=VMEM_LIMIT),
        cost_estimate=pl.CostEstimate(
            flops=LIGHT, bytes_accessed=LIGHT, transcendentals=0
        ),
        name=name,
    )


def ring(n, step):
    return [(i, (i + step) % n) for i in range(n)]


def grid_sizes():
    heads = lax.axis_size("head")
    return heads, lax.axis_size("ctx") // (2 * heads)


def place():
    xs, zs = grid_sizes()
    at = lax.axis_index("ctx")
    return at // (2 * zs), (at // 2) % zs, at % 2


def core_swap(block):
    n = lax.axis_size("ctx")
    return lax.ppermute(block, "ctx", [(i, i ^ 1) for i in range(n)])


def moved(block, axis, to):
    xs, zs = grid_sizes()
    pairs = []
    for x in range(xs):
        for z in range(zs):
            x_to, z_to = (to(x), z) if axis == "x" else (x, to(z))
            if x_to is not None and z_to is not None:
                for c in range(2):
                    pairs.append(((x * zs + z) * 2 + c, (x_to * zs + z_to) * 2 + c))
    return lax.ppermute(block, "ctx", pairs)


def scan_of_four(block, axis, at, later, beside_first, beside_second):
    near = beside_first(block, moved(block, axis, lambda i: i ^ 1))
    pair = block + near
    other = beside_second(pair, moved(pair, axis, lambda i: 3 - i))
    counts_near = (at % 2 == 0) if later else (at % 2 == 1)
    counts_other = (at < 2) if later else (at >= 2)
    return jnp.where(counts_near, near, 0.0) + jnp.where(counts_other, other, 0.0), pair + other


def scan_over_ctx(packed, later, work=None):
    xs, zs = grid_sizes()
    x, z, core = place()
    half = packed.shape[0] // 2
    first, second = packed[:half], packed[half:]
    is_first = core == 0
    mine = jnp.where(is_first, first, second)
    theirs = core_swap(jnp.where(is_first, second, first))
    chip = mine + theirs

    def beside_step(i):
        def tie(block, arrived):
            if work is None:
                return arrived
            done = work(i, block)
            arrived, *done[:] = lax.optimization_barrier((arrived, *done))
            return arrived

        return tie

    before_z, total_z = scan_of_four(chip, "z", z, later, beside_step(0), beside_step(1))
    before_x, total = scan_of_four(
        total_z, "x", x, later, beside_step(2), beside_step(3)
    )
    outside = before_z + before_x
    counts_other = is_first if later else jnp.logical_not(is_first)
    for_me = outside + jnp.where(counts_other, theirs, 0.0)
    for_other = outside + jnp.where(counts_other, 0.0, mine)
    row = lax.broadcasted_iota(jnp.int32, (1, ROWS, 1), 1)
    totals = jnp.where(row == ROWS - 1, total[:, HEAD + 1 : HEAD + 2, :], 0.0)
    for_me, for_other = for_me + totals, for_other + totals
    swapped = core_swap(for_other)
    low = jnp.where(is_first, for_me, swapped)
    high = jnp.where(is_first, swapped, for_me)
    return jnp.concatenate([low, high], axis=0)


def across(i):
    return 3 - i


def beside(i):
    return i ^ 1


def outgoing(piece, at, first, second):
    far = first(at)
    return jnp.stack([piece(far), piece(second(far))])


def half_scattered(piece, axis, at, first, second, sent=None):
    sent = outgoing(piece, at, first, second) if sent is None else sent
    came = moved(sent, axis, first)
    return piece(at) + came[0], piece(second(at)) + came[1]


def scattered(kept, passed, axis, second):
    return kept + moved(passed, axis, second)


def at_place(pieces, i):
    return lax.dynamic_index_in_dim(pieces, i, 0, keepdims=False)


def on_device(queries, keys, values, gate_logit, out_weight, out_grad):
    heads = gate_logit.shape[0]
    width = heads * HEAD
    hs = lax.axis_size("head")
    head = lax.axis_index("head")
    xs, zs = grid_sizes()
    x, z, core = place()
    rows, cols = out_grad.shape

    half = cols // 2

    def up(block):
        return lax.ppermute(block, "head", ring(hs, 1))

    def down(block):
        return lax.ppermute(block, "head", ring(hs, -1))

    left, right = up(out_grad), down(out_grad)

    gate = jax.nn.sigmoid(gate_logit)
    g = jnp.broadcast_to(gate[:, None, None], (heads, 1, HEAD))

    (packed,) = per_head(update_kernel, heads, "cc", "s", "update")(keys, values)
    forwards = []

    def forward(step, block):
        if step % 2 == 0:
            forwards[:] = forward_of((step, heads // 2), (queries, keys, values), forwards)
        return forwards

    before = scan_over_ctx(packed, False, forward)
    local_out, lse = forwards
    *mixed, memory_out, lqd = per_head(mix_kernel, heads, "ccsg", "ttcc", "mix")(
        queries, local_out, before, g
    )

    def block_at(distance):
        return (head + hs - distance) % hs

    own_at, left_at, far_at, right_at = (block_at(d) for d in range(4))
    add = functools.partial(round_of, out_weight=out_weight, mixed=mixed, core=core)

    def chip_piece(mine, came, start=0):
        return lambda i: at_place(mine, start + i) + at_place(came, start + i)

    mg, mine_own, send_own = add(None, [out_grad], [own_at])
    came_own = core_swap(send_own)
    own_parts = half_scattered(chip_piece(mine_own, came_own), "z", z, across, beside)
    left, right, *own_parts = lax.optimization_barrier((left, right, *own_parts))
    far_1 = up(left[:MOST, :half]), down(right[:MOST, half:])
    far_2 = up(left[MOST:, :half]), down(right[MOST:, half:])

    mg, mine_sides, send_sides = add(mg, [left, right], [left_at, right_at])
    sum_own = scattered(*own_parts, "z", beside)
    *far_1, mine_sides, send_sides, sum_own = lax.optimization_barrier(
        (*far_1, mine_sides, send_sides, sum_own)
    )
    came_sides = core_swap(send_sides)
    far_places = [2 * far_at, 2 * far_at + 1]
    tail = functools.partial(
        tail_of, places=far_places, out_weight=out_weight, mixed=mixed, core=core,
        whole=(lqd, memory_out, local_out),
    )
    mg_1, *far_sums = tail(0, mg, far_1, before=())
    attended = queries, keys, values

    def backward_ins(part):
        return (*attended, part, local_out, memory_out, lse, before, g)

    mg_1, came_sides = lax.optimization_barrier((mg_1, came_sides))
    left_parts = half_scattered(chip_piece(mine_sides, came_sides), "z", z, across, beside)
    right_parts = half_scattered(chip_piece(mine_sides, came_sides, zs), "z", z, beside, across)
    early = backward_of(0, (0, heads), backward_ins(mg_1), (), (), 0)
    *far_2, dq, dk, dv, left_kept, left_passed, right_kept, right_passed = (
        lax.optimization_barrier((*far_2, *early, *left_parts, *right_parts))
    )
    mg_2, back, mine_far, send_far = tail(1, mg, far_2, before=far_sums)
    sum_left = scattered(left_kept, left_passed, "z", beside)
    sum_right = scattered(right_kept, right_passed, "z", across)
    back, send_far, sum_left, sum_right = lax.optimization_barrier(
        (back, send_far, sum_left, sum_right)
    )
    came_far = core_swap(send_far)
    far_parts = half_scattered(chip_piece(mine_far, came_far), "z", z, across, beside)

    pairs = [(0, heads // 2), (heads // 2, heads // 2)]
    held = {}

    def piece_x(i):
        parts = jnp.stack([sum_own, sum_left, held[1][0], sum_right])
        return at_place(parts, (head + hs - i) % hs)

    def beside_scan(step, block):
        if step == 0:
            part, _ = lax.optimization_barrier((mg_2, block))
            grads = backward_of(1, pairs[0], backward_ins(part), (dk, dv), [dq], 6)
            held[0] = [*grads, *far_parts]
        elif step == 1:
            held[1] = [scattered(*held[0][3:], "z", beside)]
        elif step == 2:
            sent = outgoing(piece_x, x, across, beside)
            held["sent"], part, _ = lax.optimization_barrier((sent, mg_2, block))
            held[2] = [*backward_of(1, pairs[1], backward_ins(part), (dk, dv), held[0][:3], 6)]
        else:
            held[3] = [*half_scattered(piece_x, "x", x, across, beside, held["sent"])]
        return held[step]

    after = scan_over_ctx(back, True, beside_scan)
    weight_grad = scattered(*held[3], "x", beside).T

    key_grad, value_grad = per_head(finish_kernel, heads, "ccccs", "cc", "finish")(
        keys, values, *held[2][1:3], after
    )
    dq = held[2][0]

    gate_sum = jnp.sum(after[:, ROWS - 1, :], axis=-1)
    gate_grad = gate_sum * gate * (1.0 - gate)
    return dq, key_grad, value_grad, weight_grad, gate_grad


def solution(mesh):
    in_specs = (
        P("ctx", "head"),
        P("ctx", "head"),
        P("ctx", "head"),
        P("head"),
        P("head", None),
        P("ctx", "head"),
    )
    out_specs = (P("ctx", "head"), P("ctx", "head"), P("ctx", "head"), P("ctx", "head"), P("head"))
    return jax.shard_map(
        on_device, mesh=mesh, in_specs=in_specs, out_specs=out_specs, check_vma=False
    )
```

```python
import functools
import math

import jax
import jax.numpy as jnp
from jax import lax
from jax.experimental import pallas as pl
from jax.experimental.pallas import tpu as pltpu
from jax.sharding import PartitionSpec as P

SEG = 1024
HEAD = 128
ROWS = 136
FORWARD_QB = 512
BACKWARD_QB = 256
MOST = SEG // 2
REST = SEG - MOST
STEP = 256
LIGHT = 2**16
VMEM_LIMIT = 60 * 2**20
MICROSECOND = 3_600_000

f32 = jnp.float32
bf16 = jnp.bfloat16
HIGH = lax.Precision.HIGH


def lifted(x):
    return jnp.where(x > 0, x + 1.0, jnp.exp(jnp.minimum(x, 0.0)))


def lifted_slope(x):
    return jnp.where(x > 0, 1.0, jnp.exp(jnp.minimum(x, 0.0)))


def halves(x):
    hi = x.astype(bf16)
    return hi, (x - hi.astype(f32)).astype(bf16)


def mm(a, b, contract):
    dims = ((contract[:1], contract[1:]), ((), ()))

    def one(x, y):
        return lax.dot_general(x, y, dims, preferred_element_type=f32)

    return one(a[0], b[0]) + (one(a[0], b[1]) + one(a[1], b[0]))


NN = (1, 0)
NT = (1, 1)
TN = (0, 0)


def dot(a, b, contract):
    return lax.dot_general(
        a, b, ((contract[:1], contract[1:]), ((), ())), preferred_element_type=f32
    )


def wide(pair):
    return jnp.concatenate(pair, axis=1)


def doubled(x):
    return jnp.concatenate([x, x], axis=1)


def scores_of(a_wide, b_hi_twice, b_lo):
    return dot(a_wide, b_hi_twice, NT) + dot(a_wide[:, :HEAD], b_lo, NT)


def times_wide(a, b_wide):
    both = dot(a[0], b_wide, NN)
    return both[:, :HEAD] + (both[:, HEAD:] + dot(a[1], b_wide[:, :HEAD], NN))


def tall_times(a_tall, b):
    both = dot(a_tall, b[0], NN)
    return both[:HEAD] + (both[HEAD:] + dot(a_tall[:HEAD], b[1], NN))


def update_kernel(k_ref, v_ref, out_ref):
    lk = lifted(k_ref[...])
    out_ref[0, :HEAD, :] = mm(halves(lk.T), halves(v_ref[...]), NN)
    out_ref[0, HEAD : HEAD + 1, :] = jnp.sum(lk, axis=0, keepdims=True)
    out_ref[0, HEAD + 1 :, :] = jnp.zeros((ROWS - HEAD - 1, HEAD), f32)


LOG2E = math.log2(math.e)
TEMPER = 1.0 / math.sqrt(HEAD)


def parts_of(qb, size):
    return ([(0, qb * size, False)] if qb else []) + [(qb * size, (qb + 1) * size, True)]


def causal(size):
    t = lax.broadcasted_iota(jnp.int32, (size, size), 0)
    return t <= lax.broadcasted_iota(jnp.int32, (size, size), 1)


def forward_kernel(q_ref, k_ref, v_ref, *refs):
    out_ref, lse_ref = refs[-2:]
    key = wide(halves(k_ref[...]))
    value_t = jnp.concatenate(halves(v_ref[...].T), axis=0)
    q_hi, q_lo = halves(q_ref[...] * (TEMPER * LOG2E))
    q_twice = doubled(q_hi)
    seen = causal(FORWARD_QB)
    for qb in range(SEG // FORWARD_QB):
        at = slice(qb * FORWARD_QB, (qb + 1) * FORWARD_QB)
        scores = []
        for low, high, own in parts_of(qb, FORWARD_QB):
            part = scores_of(key[low:high], q_twice[at], q_lo[at])
            scores.append(jnp.where(seen, part, -1e30) if own else part)
        top = functools.reduce(
            jnp.maximum, [jnp.max(part, axis=0, keepdims=True) for part in scores]
        )
        total, out_t = 0.0, 0.0
        for (low, high, _), part in zip(parts_of(qb, FORWARD_QB), scores):
            weights = jnp.exp2(part - top)
            total = total + jnp.sum(weights, axis=0, keepdims=True)
            out_t = out_t + tall_times(value_t[:, low:high], halves(weights))
        out_ref[at, :] = (out_t * (1.0 / total)).T
        lse_ref[0, :, at] = top + jnp.log2(total)


def mix_kernel(q_ref, local_ref, mem_ref, g_ref, hi_ref, lo_ref, memout_ref, lqd_ref):
    g = g_ref[0]
    lq = lifted(q_ref[...])
    norm = mem_ref[0, HEAD : HEAD + 1, :]
    denom = jnp.sum(lq * norm, axis=1, keepdims=True) + 1.0
    inverse = 1.0 / denom
    memory_out = mm(halves(lq), halves(mem_ref[0, :HEAD, :]), NN) * inverse
    memout_ref[...] = memory_out
    mixed = g * memory_out + (1.0 - g) * local_ref[...]
    hi_ref[...], lo_ref[...] = halves(mixed.T)
    lqd_ref[...] = lq * (inverse * g)


def add_weight_part(mixed, block, first, start, mine_ref, send_ref):
    part = mm(mixed, block, NN)
    groups = part.shape[1] // (2 * HEAD)
    for k in range(groups):
        even = part[:, 2 * k * HEAD : (2 * k + 1) * HEAD]
        odd = part[:, (2 * k + 1) * HEAD : (2 * k + 2) * HEAD]
        mine_ref[start + k] += jnp.where(first, even, odd)
        send_ref[start + k] += jnp.where(first, odd, even)


def block_kernel(at_ref, *refs, counts, added):
    acc, refs = refs[:added], refs[added:]
    block_refs = refs[: len(counts)]
    w_ref, mhi_ref, mlo_ref, out_ref, mine_ref, send_ref = refs[len(counts) :]
    j = pl.program_id(0)

    @pl.when(j == 0)
    def _():
        out_ref[...] = acc[0][...] if added else jnp.zeros_like(out_ref)

    def step(block_ref):
        block = halves(block_ref[...])
        out_ref[...] += mm(block, halves(w_ref[...]), NT)
        part = mm((mhi_ref[...], mlo_ref[...]), block, NN)
        first = at_ref[sum(counts)] == 0
        mine_ref[0] = jnp.where(first, part[:, :HEAD], part[:, HEAD:])
        send_ref[0] = jnp.where(first, part[:, HEAD:], part[:, :HEAD])

    start = 0
    for block_ref, count in zip(block_refs, counts):
        pl.when((j >= start) & (j < start + count))(functools.partial(step, block_ref))
        start += count


def rows_of(width, first=0):
    return pl.BlockSpec((STEP, width), lambda i, at: (i + first // STEP, 0))


def weight_specs(width, blocks):
    return [
        pl.BlockSpec(
            (width, block.shape[1]), lambda i, at, k=k: (0, at[k]), pipeline_mode=pl.Buffered(1)
        )
        for k, block in enumerate(blocks)
    ]


def round_of(acc, blocks, places, out_weight, mixed, core):
    rows = blocks[0].shape[0]
    width = out_weight.shape[0]
    group = 2 * HEAD
    counts = [block.shape[1] // group for block in blocks]
    steps = sum(counts)
    at = [place + k for place, count in zip(places, counts) for k in range(count)]
    at = jnp.stack([*at, core]).astype(jnp.int32)
    acc = [] if acc is None else [acc]
    whole = pl.BlockSpec((rows, width), lambda j, at: (0, 0))
    half = pl.BlockSpec((width, rows), lambda j, at: (0, 0), pipeline_mode=pl.Buffered(1))
    by_core = pl.BlockSpec((1, width, HEAD), lambda j, at: (j, 0, 0))
    by_core_shape = jax.ShapeDtypeStruct((steps, width, HEAD), f32)

    def columns_of(start, count):
        return pl.BlockSpec(
            (rows, group), lambda j, at: (0, jnp.clip(j - start, 0, count - 1))
        )

    return pl.pallas_call(
        functools.partial(block_kernel, counts=counts, added=len(acc)),
        grid_spec=pltpu.PrefetchScalarGridSpec(
            num_scalar_prefetch=1,
            grid=(steps,),
            in_specs=[whole for _ in acc]
            + [columns_of(sum(counts[:k]), count) for k, count in enumerate(counts)]
            + [pl.BlockSpec((width, group), lambda j, at: (0, at[j]))]
            + [half] * 2,
            out_specs=[whole] + [by_core] * 2,
        ),
        out_shape=[jax.ShapeDtypeStruct((rows, width), f32)] + [by_core_shape] * 2,
        input_output_aliases={1: 0} if acc else {},
        compiler_params=pltpu.CompilerParams(vmem_limit_bytes=VMEM_LIMIT),
        cost_estimate=pl.CostEstimate(flops=LIGHT, bytes_accessed=LIGHT, transcendentals=0),
        name="round",
    )(at, *acc, *blocks, out_weight, *mixed)


def tail_kernel(at_ref, *refs):
    acc_ref, a_ref, b_ref, wa_ref, wb_ref, lqd_ref, memout_ref, local_ref = refs[:8]
    mhi_ref, mlo_ref, *before = refs[8:-8]
    mg_ref, state_ref, mine_ref, send_ref, *w = refs[-8:]

    @pl.when(pl.program_id(0) == 0)
    def _():
        w[0][...], w[1][...] = halves(wa_ref[...])
        w[2][...], w[3][...] = halves(wb_ref[...])
        for n, ref in enumerate((state_ref, mine_ref, send_ref)):
            ref[...] = before[n][...] if before else jnp.zeros_like(ref)

    a, b = halves(a_ref[...]), halves(b_ref[...])
    mg = acc_ref[...] + mm(a, (w[0][...], w[1][...]), NT)
    mg = mg + mm(b, (w[2][...], w[3][...]), NT)
    mg_ref[...] = mg
    for h in range(state_ref.shape[0]):
        at = slice(h * HEAD, (h + 1) * HEAD)
        here, lqd, memory_out = mg[:, at], lqd_ref[:, at], memout_ref[:, at]
        state_ref[h, :HEAD, :] += mm(halves(lqd.T), halves(here), NN)
        r = jnp.sum(here * memory_out, axis=1, keepdims=True)
        state_ref[h, HEAD : HEAD + 1, :] -= jnp.sum(lqd * r, axis=0, keepdims=True)
        state_ref[h, HEAD + 1 : HEAD + 2, :] += jnp.sum(
            here * (memory_out - local_ref[:, at]), axis=0, keepdims=True
        )
    mixed, first = (mhi_ref[...], mlo_ref[...]), at_ref[2] == 0
    groups = a_ref.shape[1] // (2 * HEAD)
    add_weight_part(mixed, a, first, 0, mine_ref, send_ref)
    add_weight_part(mixed, b, first, groups, mine_ref, send_ref)


def tail_of(second, acc, blocks, places, out_weight, mixed, core, whole, before):
    rows, deep = blocks[0].shape
    width = out_weight.shape[0]
    first = second * MOST
    by_core = deep // HEAD, width, HEAD
    sums = [(width // HEAD, ROWS, HEAD), by_core, by_core]
    sum_specs = [pl.BlockSpec(shape, lambda i, at: (0, 0, 0)) for shape in sums]
    return pl.pallas_call(
        tail_kernel,
        grid_spec=pltpu.PrefetchScalarGridSpec(
            num_scalar_prefetch=1,
            grid=(rows // STEP,),
            in_specs=[rows_of(width, first)]
            + [rows_of(deep)] * 2
            + weight_specs(width, blocks)
            + [rows_of(width, first)] * 3
            + [pl.BlockSpec((width, STEP), lambda i, at: (0, i + first // STEP))] * 2
            + sum_specs[: len(before)],
            out_specs=[rows_of(width), *sum_specs],
            scratch_shapes=[pltpu.VMEM((width, deep), bf16) for _ in range(4)],
        ),
        out_shape=[jax.ShapeDtypeStruct(shape, f32) for shape in [(rows, width), *sums]],
        compiler_params=pltpu.CompilerParams(vmem_limit_bytes=VMEM_LIMIT),
        cost_estimate=pl.CostEstimate(flops=LIGHT, bytes_accessed=LIGHT, transcendentals=0),
        name="tail",
    )(
        jnp.stack([*places, core]).astype(jnp.int32),
        acc, *blocks, out_weight, out_weight, *whole, *mixed, *before,
    )


def backward_kernel(*refs, first):
    q_ref, k_ref, v_ref, mg_ref, local_ref, memout_ref, lse_ref, mem_ref, g_ref = refs[:9]
    dq_ref, dk_ref, dv_ref = refs[-3:]
    g = g_ref[0]
    q = q_ref[...]
    mg = mg_ref[...]
    local_grad = (1.0 - g) * TEMPER * mg
    key = halves(k_ref[...])
    key_t = jnp.concatenate([key[0].T, key[1].T], axis=0)
    key = wide(key)
    value = wide(halves(v_ref[...]))
    query = halves(q * (TEMPER * LOG2E))
    q_twice, q_wide = doubled(query[0]), wide(query)
    grad = halves(local_grad)
    g_twice, g_wide = doubled(grad[0]), wide(grad)
    delta = jnp.sum((local_grad * local_ref[...]).T, axis=0, keepdims=True)
    lq = lifted(q)
    norm = mem_ref[0, HEAD : HEAD + 1, :]
    inverse = 1.0 / (jnp.sum(lq * norm, axis=1, keepdims=True) + 1.0)
    r = jnp.sum(mg * memout_ref[...], axis=1, keepdims=True)
    lift_grad = mm(halves(mg), halves(mem_ref[0, :HEAD, :].T), NN) - r * norm
    dq_ref[...] = lift_grad * (inverse * g) * lifted_slope(q)
    for ref, before in zip((dk_ref, dv_ref), refs[9:11] if first else (None, None)):
        ref[first:, :] = jnp.zeros(q.shape, f32)
        if first:
            ref[:first, :] = before[...]
    seen = causal(BACKWARD_QB)
    for qb in range(q.shape[0] // BACKWARD_QB):
        at = slice(qb * BACKWARD_QB, (qb + 1) * BACKWARD_QB)
        dq_t = 0.0
        for low, high, own in parts_of(qb + first // BACKWARD_QB, BACKWARD_QB):
            scores = scores_of(key[low:high], q_twice[at], query[1][at])
            if own:
                scores = jnp.where(seen, scores, -1e30)
            weights = jnp.exp2(scores - lse_ref[0, :, at])
            dp = scores_of(value[low:high], g_twice[at], grad[1][at])
            ds = halves(weights * (dp - delta[:, at]))
            dv_ref[low:high, :] += times_wide(halves(weights), g_wide[at])
            dk_ref[low:high, :] += times_wide(ds, q_wide[at])
            dq_t = dq_t + tall_times(key_t[:, low:high], ds)
        dq_ref[at, :] += dq_t.T
    if first:
        dk_ref[...] = dk_ref[...] * (1.0 / (TEMPER * LOG2E))
        dv_ref[...] = dv_ref[...] * (1.0 / TEMPER)


def backward_of(second, heads, ins, before, earlier, micros):
    width = ins[0].shape[1]
    low, count = heads

    def rows(n, at=0):
        return pl.BlockSpec((n, HEAD), lambda h: (at, h + low))

    def of_head(x, n=None, at=0):
        return pl.BlockSpec((1, x.shape[1], n or x.shape[2]), lambda h: (h + low, 0, at))

    size, at_part = (REST, MOST // REST) if second else (MOST, 0)
    here = rows(size, at_part)
    seen = rows(SEG if second else MOST)
    shapes = [(SEG, width)] + [(SEG if second else MOST, width)] * 2
    return pl.pallas_call(
        functools.partial(backward_kernel, first=second * MOST),
        grid=(count,),
        in_specs=[here, seen, seen, rows(size), here, here]
        + [of_head(ins[6], size, at_part), of_head(ins[7]), of_head(ins[8])]
        + [rows(MOST)] * len(before)
        + [pl.BlockSpec(memory_space=pl.ANY)] * len(earlier),
        out_specs=[here, seen, seen],
        out_shape=[jax.ShapeDtypeStruct(shape, f32) for shape in shapes],
        input_output_aliases={len(ins) + len(before) + i: i for i in range(len(earlier))},
        compiler_params=pltpu.CompilerParams(vmem_limit_bytes=VMEM_LIMIT),
        cost_estimate=pl.CostEstimate(
            flops=LIGHT, bytes_accessed=micros * MICROSECOND or LIGHT, transcendentals=0
        ),
        name="backward",
    )(*ins, *before, *earlier)


def forward_of(heads, ins, earlier):
    width = ins[0].shape[1]
    low, count = heads
    column = pl.BlockSpec((SEG, HEAD), lambda h: (0, h + low))
    line = pl.BlockSpec((1, 1, SEG), lambda h: (h + low, 0, 0))
    return pl.pallas_call(
        forward_kernel,
        grid=(count,),
        in_specs=[column] * 3 + [pl.BlockSpec(memory_space=pl.ANY)] * len(earlier),
        out_specs=[column, line],
        out_shape=[
            jax.ShapeDtypeStruct((SEG, width), f32),
            jax.ShapeDtypeStruct((width // HEAD, 1, SEG), f32),
        ],
        input_output_aliases={len(ins) + i: i for i in range(len(earlier))},
        compiler_params=pltpu.CompilerParams(vmem_limit_bytes=VMEM_LIMIT),
        cost_estimate=pl.CostEstimate(flops=LIGHT, bytes_accessed=LIGHT, transcendentals=0),
        name="forward",
    )(*ins, *earlier)


def finish_kernel(k_ref, v_ref, dk_ref, dv_ref, state_ref, kg_ref, vg_ref):
    key = k_ref[...]
    state = state_ref[0, :HEAD, :]
    norm = state_ref[0, HEAD : HEAD + 1, :]
    lift_grad = mm(halves(v_ref[...]), halves(state.T), NN) + norm
    kg_ref[...] = dk_ref[...] + lift_grad * lifted_slope(key)
    vg_ref[...] = dv_ref[...] + mm(halves(lifted(key)), halves(state), NN)


def columns():
    return pl.BlockSpec((SEG, HEAD), lambda h: (0, h))


def state():
    return pl.BlockSpec((1, ROWS, HEAD), lambda h: (h, 0, 0))


def row(width):
    return pl.BlockSpec((1, 1, width), lambda h: (h, 0, 0))


def per_head(kernel, heads, ins, outs, name):
    width = heads * HEAD
    kinds = {
        "c": (columns(), jax.ShapeDtypeStruct((SEG, width), f32)),
        "s": (state(), jax.ShapeDtypeStruct((heads, ROWS, HEAD), f32)),
        "g": (row(HEAD), jax.ShapeDtypeStruct((heads, 1, HEAD), f32)),
        "t": (
            pl.BlockSpec((HEAD, SEG), lambda h: (h, 0)),
            jax.ShapeDtypeStruct((width, SEG), bf16),
        ),
        "l": (row(SEG), jax.ShapeDtypeStruct((heads, 1, SEG), f32)),
    }
    return pl.pallas_call(
        kernel,
        grid=(heads,),
        in_specs=[kinds[i][0] for i in ins],
        out_specs=[kinds[o][0] for o in outs],
        out_shape=[kinds[o][1] for o in outs],
        compiler_params=pltpu.CompilerParams(vmem_limit_bytes=VMEM_LIMIT),
        cost_estimate=pl.CostEstimate(
            flops=LIGHT, bytes_accessed=LIGHT, transcendentals=0
        ),
        name=name,
    )


def ring(n, step):
    return [(i, (i + step) % n) for i in range(n)]


def grid_sizes():
    heads = lax.axis_size("head")
    return heads, lax.axis_size("ctx") // (2 * heads)


def place():
    xs, zs = grid_sizes()
    at = lax.axis_index("ctx")
    return at // (2 * zs), (at // 2) % zs, at % 2


def core_swap(block):
    n = lax.axis_size("ctx")
    return lax.ppermute(block, "ctx", [(i, i ^ 1) for i in range(n)])


def moved(block, axis, to):
    xs, zs = grid_sizes()
    pairs = []
    for x in range(xs):
        for z in range(zs):
            x_to, z_to = (to(x), z) if axis == "x" else (x, to(z))
            if x_to is not None and z_to is not None:
                for c in range(2):
                    pairs.append(((x * zs + z) * 2 + c, (x_to * zs + z_to) * 2 + c))
    return lax.ppermute(block, "ctx", pairs)


def scan_of_four(block, axis, at, later, beside_first, beside_second):
    near = beside_first(block, moved(block, axis, lambda i: i ^ 1))
    pair = block + near
    other = beside_second(pair, moved(pair, axis, lambda i: 3 - i))
    counts_near = (at % 2 == 0) if later else (at % 2 == 1)
    counts_other = (at < 2) if later else (at >= 2)
    return jnp.where(counts_near, near, 0.0) + jnp.where(counts_other, other, 0.0), pair + other


def scan_over_ctx(packed, later, work=None):
    xs, zs = grid_sizes()
    x, z, core = place()
    half = packed.shape[0] // 2
    first, second = packed[:half], packed[half:]
    is_first = core == 0
    mine = jnp.where(is_first, first, second)
    theirs = core_swap(jnp.where(is_first, second, first))
    chip = mine + theirs

    def beside_step(i):
        def tie(block, arrived):
            if work is None:
                return arrived
            done = work(i, block)
            arrived, *done[:] = lax.optimization_barrier((arrived, *done))
            return arrived

        return tie

    before_z, total_z = scan_of_four(chip, "z", z, later, beside_step(0), beside_step(1))
    before_x, total = scan_of_four(
        total_z, "x", x, later, beside_step(2), beside_step(3)
    )
    outside = before_z + before_x
    counts_other = is_first if later else jnp.logical_not(is_first)
    for_me = outside + jnp.where(counts_other, theirs, 0.0)
    for_other = outside + jnp.where(counts_other, 0.0, mine)
    row = lax.broadcasted_iota(jnp.int32, (1, ROWS, 1), 1)
    totals = jnp.where(row == ROWS - 1, total[:, HEAD + 1 : HEAD + 2, :], 0.0)
    for_me, for_other = for_me + totals, for_other + totals
    swapped = core_swap(for_other)
    low = jnp.where(is_first, for_me, swapped)
    high = jnp.where(is_first, swapped, for_me)
    return jnp.concatenate([low, high], axis=0)


def across(i):
    return 3 - i


def beside(i):
    return i ^ 1


def outgoing(piece, at, first, second):
    far = first(at)
    return jnp.stack([piece(far), piece(second(far))])


def half_scattered(piece, axis, at, first, second, sent=None):
    sent = outgoing(piece, at, first, second) if sent is None else sent
    came = moved(sent, axis, first)
    return piece(at) + came[0], piece(second(at)) + came[1]


def scattered(kept, passed, axis, second):
    return kept + moved(passed, axis, second)


def at_place(pieces, i):
    return lax.dynamic_index_in_dim(pieces, i, 0, keepdims=False)


def on_device(queries, keys, values, gate_logit, out_weight, out_grad):
    heads = gate_logit.shape[0]
    width = heads * HEAD
    hs = lax.axis_size("head")
    head = lax.axis_index("head")
    xs, zs = grid_sizes()
    x, z, core = place()
    rows, cols = out_grad.shape

    half, group = cols // 2, 2 * HEAD

    def up(block):
        return lax.ppermute(block, "head", ring(hs, 1))

    def down(block):
        return lax.ppermute(block, "head", ring(hs, -1))

    left, right = up(out_grad[:, : cols - group]), down(out_grad[:, group:])
    left_rest, right_rest = up(out_grad[:, cols - group :]), down(out_grad[:, :group])
    left, right, *onward = lax.optimization_barrier(
        (
            left,
            right,
            left[:MOST, :half],
            right[:MOST, half - group :],
            left[MOST:, :half],
            right[MOST:, half - group :],
        )
    )
    far_1 = up(onward[0]), down(onward[1])
    far_2 = up(onward[2]), down(onward[3])

    gate = jax.nn.sigmoid(gate_logit)
    g = jnp.broadcast_to(gate[:, None, None], (heads, 1, HEAD))

    (packed,) = per_head(update_kernel, heads, "cc", "s", "update")(keys, values)
    forwards = []

    def forward(step, block):
        if step % 2 == 0:
            forwards[:] = forward_of((step, heads // 2), (queries, keys, values), forwards)
        return forwards

    before = scan_over_ctx(packed, False, forward)
    local_out, lse = forwards
    *mixed, memory_out, lqd = per_head(mix_kernel, heads, "ccsg", "ttcc", "mix")(
        queries, local_out, before, g
    )

    def block_at(distance):
        return (head + hs - distance) % hs

    own_at, left_at, far_at, right_at = (block_at(d) for d in range(4))
    add = functools.partial(round_of, out_weight=out_weight, mixed=mixed, core=core)

    def chip_piece(mine, came, start=0):
        return lambda i: at_place(mine, start + i) + at_place(came, start + i)

    mg, mine_own, send_own = add(None, [out_grad], [zs * own_at])
    mg, mine_most, send_most = add(mg, [left, right], [zs * left_at, zs * right_at + 1])
    left_rest, right_rest, mine_own, send_own, mine_most, send_most = lax.optimization_barrier(
        (left_rest, right_rest, mine_own, send_own, mine_most, send_most)
    )
    came_own, came_most = core_swap(send_own), core_swap(send_most)
    mg, mine_rest, send_rest = add(
        mg, [left_rest, right_rest], [zs * left_at + zs - 1, zs * right_at]
    )
    own_parts = half_scattered(chip_piece(mine_own, came_own), "z", z, across, beside)
    *far_1, own_kept, own_passed, came_most, mine_rest, send_rest = lax.optimization_barrier(
        (*far_1, *own_parts, came_most, mine_rest, send_rest)
    )
    came_rest = core_swap(send_rest)
    far_places = [2 * far_at, 2 * far_at + 1]
    tail = functools.partial(
        tail_of, places=far_places, out_weight=out_weight, mixed=mixed, core=core,
        whole=(lqd, memory_out, local_out),
    )
    mg_1, *far_sums = tail(0, mg, far_1, before=())
    attended = queries, keys, values

    def backward_ins(part):
        return (*attended, part, local_out, memory_out, lse, before, g)

    mg_1, came_rest = lax.optimization_barrier((mg_1, came_rest))
    most, rest = chip_piece(mine_most, came_most), chip_piece(mine_rest, came_rest)

    def piece_left(i):
        return jnp.where(i < zs - 1, most(jnp.minimum(i, zs - 2)), rest(0))

    def piece_right(i):
        return jnp.where(i > 0, most(jnp.maximum(i, 1) + zs - 2), rest(1))

    left_parts = half_scattered(piece_left, "z", z, across, beside)
    right_parts = half_scattered(piece_right, "z", z, beside, across)
    early = backward_of(0, (0, heads), backward_ins(mg_1), (), (), 0)
    *far_2, dq, dk, dv, left_kept, left_passed, right_kept, right_passed = (
        lax.optimization_barrier((*far_2, *early, *left_parts, *right_parts))
    )
    mg_2, back, mine_far, send_far = tail(1, mg, far_2, before=far_sums)
    sum_own = scattered(own_kept, own_passed, "z", beside)
    sum_left = scattered(left_kept, left_passed, "z", beside)
    sum_right = scattered(right_kept, right_passed, "z", across)
    back, send_far, sum_own, sum_left, sum_right = lax.optimization_barrier(
        (back, send_far, sum_own, sum_left, sum_right)
    )
    came_far = core_swap(send_far)
    far_parts = half_scattered(chip_piece(mine_far, came_far), "z", z, across, beside)

    pairs = [(0, heads // 2), (heads // 2, heads // 2)]
    held = {}

    def piece_x(i):
        parts = jnp.stack([sum_own, sum_left, held[1][0], sum_right])
        return at_place(parts, (head + hs - i) % hs)

    def beside_scan(step, block):
        if step == 0:
            part, _ = lax.optimization_barrier((mg_2, block))
            grads = backward_of(1, pairs[0], backward_ins(part), (dk, dv), [dq], 6)
            held[0] = [*grads, *far_parts]
        elif step == 1:
            held[1] = [scattered(*held[0][3:], "z", beside)]
        elif step == 2:
            sent = outgoing(piece_x, x, across, beside)
            held["sent"], part, _ = lax.optimization_barrier((sent, mg_2, block))
            held[2] = [*backward_of(1, pairs[1], backward_ins(part), (dk, dv), held[0][:3], 6)]
        else:
            held[3] = [*half_scattered(piece_x, "x", x, across, beside, held["sent"])]
        return held[step]

    after = scan_over_ctx(back, True, beside_scan)
    weight_grad = scattered(*held[3], "x", beside).T

    key_grad, value_grad = per_head(finish_kernel, heads, "ccccs", "cc", "finish")(
        keys, values, *held[2][1:3], after
    )
    dq = held[2][0]

    gate_sum = jnp.sum(after[:, ROWS - 1, :], axis=-1)
    gate_grad = gate_sum * gate * (1.0 - gate)
    return dq, key_grad, value_grad, weight_grad, gate_grad


def solution(mesh):
    in_specs = (
        P("ctx", "head"),
        P("ctx", "head"),
        P("ctx", "head"),
        P("head"),
        P("head", None),
        P("ctx", "head"),
    )
    out_specs = (P("ctx", "head"), P("ctx", "head"), P("ctx", "head"), P("ctx", "head"), P("head"))
    return jax.shard_map(
        on_device, mesh=mesh, in_specs=in_specs, out_specs=out_specs, check_vma=False
    )
```

```python
import functools
import math

import jax
import jax.numpy as jnp
from jax import lax
from jax.experimental import pallas as pl
from jax.experimental.pallas import tpu as pltpu
from jax.sharding import PartitionSpec as P

SEG = 1024
HEAD = 128
ROWS = 136
FORWARD_QB = 512
BACKWARD_QB = 256
MOST = SEG // 2
REST = SEG - MOST
STEP = 512
LIGHT = 2**16
VMEM_LIMIT = 60 * 2**20
MICROSECOND = 3_600_000

f32 = jnp.float32
bf16 = jnp.bfloat16
HIGH = lax.Precision.HIGH


def lifted(x):
    return jnp.where(x > 0, x + 1.0, jnp.exp(jnp.minimum(x, 0.0)))


def lifted_slope(x):
    return jnp.where(x > 0, 1.0, jnp.exp(jnp.minimum(x, 0.0)))


def halves(x):
    hi = x.astype(bf16)
    return hi, (x - hi.astype(f32)).astype(bf16)


def mm(a, b, contract):
    dims = ((contract[:1], contract[1:]), ((), ()))

    def one(x, y):
        return lax.dot_general(x, y, dims, preferred_element_type=f32)

    return one(a[0], b[0]) + (one(a[0], b[1]) + one(a[1], b[0]))


NN = (1, 0)
NT = (1, 1)
TN = (0, 0)


def dot(a, b, contract):
    return lax.dot_general(
        a, b, ((contract[:1], contract[1:]), ((), ())), preferred_element_type=f32
    )


def wide(pair):
    return jnp.concatenate(pair, axis=1)


def doubled(x):
    return jnp.concatenate([x, x], axis=1)


def scores_of(a_wide, b_hi_twice, b_lo):
    return dot(a_wide, b_hi_twice, NT) + dot(a_wide[:, :HEAD], b_lo, NT)


def times_wide(a, b_wide):
    both = dot(a[0], b_wide, NN)
    return both[:, :HEAD] + (both[:, HEAD:] + dot(a[1], b_wide[:, :HEAD], NN))


def tall_times(a_tall, b):
    both = dot(a_tall, b[0], NN)
    return both[:HEAD] + (both[HEAD:] + dot(a_tall[:HEAD], b[1], NN))


def update_kernel(k_ref, v_ref, out_ref):
    lk = lifted(k_ref[...])
    out_ref[0, :HEAD, :] = mm(halves(lk.T), halves(v_ref[...]), NN)
    out_ref[0, HEAD : HEAD + 1, :] = jnp.sum(lk, axis=0, keepdims=True)
    out_ref[0, HEAD + 1 :, :] = jnp.zeros((ROWS - HEAD - 1, HEAD), f32)


LOG2E = math.log2(math.e)
TEMPER = 1.0 / math.sqrt(HEAD)


def parts_of(qb, size):
    return ([(0, qb * size, False)] if qb else []) + [(qb * size, (qb + 1) * size, True)]


def causal(size):
    t = lax.broadcasted_iota(jnp.int32, (size, size), 0)
    return t <= lax.broadcasted_iota(jnp.int32, (size, size), 1)


def forward_kernel(q_ref, k_ref, v_ref, *refs):
    out_ref, lse_ref = refs[-2:]
    key = wide(halves(k_ref[...]))
    value_t = jnp.concatenate(halves(v_ref[...].T), axis=0)
    q_hi, q_lo = halves(q_ref[...] * (TEMPER * LOG2E))
    q_twice = doubled(q_hi)
    seen = causal(FORWARD_QB)
    for qb in range(SEG // FORWARD_QB):
        at = slice(qb * FORWARD_QB, (qb + 1) * FORWARD_QB)
        scores = []
        for low, high, own in parts_of(qb, FORWARD_QB):
            part = scores_of(key[low:high], q_twice[at], q_lo[at])
            scores.append(jnp.where(seen, part, -1e30) if own else part)
        top = functools.reduce(
            jnp.maximum, [jnp.max(part, axis=0, keepdims=True) for part in scores]
        )
        total, out_t = 0.0, 0.0
        for (low, high, _), part in zip(parts_of(qb, FORWARD_QB), scores):
            weights = jnp.exp2(part - top)
            total = total + jnp.sum(weights, axis=0, keepdims=True)
            out_t = out_t + tall_times(value_t[:, low:high], halves(weights))
        out_ref[at, :] = (out_t * (1.0 / total)).T
        lse_ref[0, :, at] = top + jnp.log2(total)


def mix_kernel(q_ref, local_ref, mem_ref, g_ref, hi_ref, lo_ref, memout_ref, lqd_ref):
    g = g_ref[0]
    lq = lifted(q_ref[...])
    norm = mem_ref[0, HEAD : HEAD + 1, :]
    denom = jnp.sum(lq * norm, axis=1, keepdims=True) + 1.0
    inverse = 1.0 / denom
    memory_out = mm(halves(lq), halves(mem_ref[0, :HEAD, :]), NN) * inverse
    memout_ref[...] = memory_out
    mixed = g * memory_out + (1.0 - g) * local_ref[...]
    hi_ref[...], lo_ref[...] = halves(mixed.T)
    lqd_ref[...] = lq * (inverse * g)


def add_weight_part(mixed, block, first, start, mine_ref, send_ref):
    part = mm(mixed, block, NN)
    groups = part.shape[1] // (2 * HEAD)
    for k in range(groups):
        even = part[:, 2 * k * HEAD : (2 * k + 1) * HEAD]
        odd = part[:, (2 * k + 1) * HEAD : (2 * k + 2) * HEAD]
        mine_ref[start + k] += jnp.where(first, even, odd)
        send_ref[start + k] += jnp.where(first, odd, even)


def block_kernel(at_ref, *refs, counts, added):
    acc, refs = refs[:added], refs[added:]
    block_refs = refs[: len(counts)]
    w_ref, mhi_ref, mlo_ref, out_ref, mine_ref, send_ref = refs[len(counts) :]
    j = pl.program_id(0)

    @pl.when(j == 0)
    def _():
        out_ref[...] = acc[0][...] if added else jnp.zeros_like(out_ref)

    def step(block_ref):
        block = halves(block_ref[...])
        out_ref[...] += mm(block, halves(w_ref[...]), NT)
        part = mm((mhi_ref[...], mlo_ref[...]), block, NN)
        first = at_ref[sum(counts)] == 0
        mine_ref[0] = jnp.where(first, part[:, :HEAD], part[:, HEAD:])
        send_ref[0] = jnp.where(first, part[:, HEAD:], part[:, :HEAD])

    start = 0
    for block_ref, count in zip(block_refs, counts):
        pl.when((j >= start) & (j < start + count))(functools.partial(step, block_ref))
        start += count


def onward_kernel(*refs):
    for source, target in zip(refs[:4], refs[4:]):
        target[...] = source[...]


def onward_of(left, right):
    rows, half, step = MOST, left.shape[1] // 2, MOST // 2

    def rows_from(first, column):
        return pl.BlockSpec((step, half), lambda i: (i + first // step, column))

    return pl.pallas_call(
        onward_kernel,
        grid=(rows // step,),
        in_specs=[rows_from(0, 0), rows_from(0, 1), rows_from(MOST, 0), rows_from(MOST, 1)],
        out_specs=[rows_from(0, 0)] * 4,
        out_shape=[jax.ShapeDtypeStruct((rows, half), f32)] * 4,
        compiler_params=pltpu.CompilerParams(vmem_limit_bytes=VMEM_LIMIT),
        cost_estimate=pl.CostEstimate(flops=LIGHT, bytes_accessed=LIGHT, transcendentals=0),
        name="onward",
    )(left, right, left, right)


def rows_of(width, first=0):
    return pl.BlockSpec((STEP, width), lambda i, at: (i + first // STEP, 0))


def weight_specs(width, blocks):
    return [
        pl.BlockSpec(
            (width, block.shape[1]), lambda i, at, k=k: (0, at[k]), pipeline_mode=pl.Buffered(1)
        )
        for k, block in enumerate(blocks)
    ]


def round_of(acc, blocks, places, out_weight, mixed, core):
    rows = blocks[0].shape[0]
    width = out_weight.shape[0]
    group = 2 * HEAD
    counts = [block.shape[1] // group for block in blocks]
    steps = sum(counts)
    at = [place + k for place, count in zip(places, counts) for k in range(count)]
    at = jnp.stack([*at, core]).astype(jnp.int32)
    acc = [] if acc is None else [acc]
    whole = pl.BlockSpec((rows, width), lambda j, at: (0, 0))
    half = pl.BlockSpec((width, rows), lambda j, at: (0, 0), pipeline_mode=pl.Buffered(1))
    by_core = pl.BlockSpec((1, width, HEAD), lambda j, at: (j, 0, 0))
    by_core_shape = jax.ShapeDtypeStruct((steps, width, HEAD), f32)

    def columns_of(start, count):
        return pl.BlockSpec(
            (rows, group), lambda j, at: (0, jnp.clip(j - start, 0, count - 1))
        )

    return pl.pallas_call(
        functools.partial(block_kernel, counts=counts, added=len(acc)),
        grid_spec=pltpu.PrefetchScalarGridSpec(
            num_scalar_prefetch=1,
            grid=(steps,),
            in_specs=[whole for _ in acc]
            + [columns_of(sum(counts[:k]), count) for k, count in enumerate(counts)]
            + [pl.BlockSpec((width, group), lambda j, at: (0, at[j]))]
            + [half] * 2,
            out_specs=[whole] + [by_core] * 2,
        ),
        out_shape=[jax.ShapeDtypeStruct((rows, width), f32)] + [by_core_shape] * 2,
        input_output_aliases={1: 0} if acc else {},
        compiler_params=pltpu.CompilerParams(vmem_limit_bytes=VMEM_LIMIT),
        cost_estimate=pl.CostEstimate(flops=LIGHT, bytes_accessed=LIGHT, transcendentals=0),
        name="round",
    )(at, *acc, *blocks, out_weight, *mixed)


def tail_kernel(at_ref, *refs):
    acc_ref, a_ref, b_ref, wa_ref, wb_ref, lqd_ref, memout_ref, local_ref = refs[:8]
    mhi_ref, mlo_ref, *before = refs[8:-8]
    mg_ref, state_ref, mine_ref, send_ref, *w = refs[-8:]

    @pl.when(pl.program_id(0) == 0)
    def _():
        w[0][...], w[1][...] = halves(wa_ref[...])
        w[2][...], w[3][...] = halves(wb_ref[...])
        for n, ref in enumerate((state_ref, mine_ref, send_ref)):
            ref[...] = before[n][...] if before else jnp.zeros_like(ref)

    a, b = halves(a_ref[...]), halves(b_ref[...])
    mg = acc_ref[...] + mm(a, (w[0][...], w[1][...]), NT)
    mg = mg + mm(b, (w[2][...], w[3][...]), NT)
    mg_ref[...] = mg
    for h in range(state_ref.shape[0]):
        at = slice(h * HEAD, (h + 1) * HEAD)
        here, lqd, memory_out = mg[:, at], lqd_ref[:, at], memout_ref[:, at]
        state_ref[h, :HEAD, :] += mm(halves(lqd.T), halves(here), NN)
        r = jnp.sum(here * memory_out, axis=1, keepdims=True)
        state_ref[h, HEAD : HEAD + 1, :] -= jnp.sum(lqd * r, axis=0, keepdims=True)
        state_ref[h, HEAD + 1 : HEAD + 2, :] += jnp.sum(
            here * (memory_out - local_ref[:, at]), axis=0, keepdims=True
        )
    mixed, first = (mhi_ref[...], mlo_ref[...]), at_ref[2] == 0
    groups = a_ref.shape[1] // (2 * HEAD)
    add_weight_part(mixed, a, first, 0, mine_ref, send_ref)
    add_weight_part(mixed, b, first, groups, mine_ref, send_ref)


def tail_of(second, acc, blocks, places, out_weight, mixed, core, whole, before):
    rows, deep = blocks[0].shape
    width = out_weight.shape[0]
    first = second * MOST
    by_core = deep // HEAD, width, HEAD
    sums = [(width // HEAD, ROWS, HEAD), by_core, by_core]
    sum_specs = [pl.BlockSpec(shape, lambda i, at: (0, 0, 0)) for shape in sums]
    return pl.pallas_call(
        tail_kernel,
        grid_spec=pltpu.PrefetchScalarGridSpec(
            num_scalar_prefetch=1,
            grid=(rows // STEP,),
            in_specs=[rows_of(width, first)]
            + [rows_of(deep)] * 2
            + weight_specs(width, blocks)
            + [rows_of(width, first)] * 3
            + [pl.BlockSpec((width, STEP), lambda i, at: (0, i + first // STEP))] * 2
            + sum_specs[: len(before)],
            out_specs=[rows_of(width), *sum_specs],
            scratch_shapes=[pltpu.VMEM((width, deep), bf16) for _ in range(4)],
        ),
        out_shape=[jax.ShapeDtypeStruct(shape, f32) for shape in [(rows, width), *sums]],
        compiler_params=pltpu.CompilerParams(vmem_limit_bytes=VMEM_LIMIT),
        cost_estimate=pl.CostEstimate(flops=LIGHT, bytes_accessed=LIGHT, transcendentals=0),
        name="tail",
    )(
        jnp.stack([*places, core]).astype(jnp.int32),
        acc, *blocks, out_weight, out_weight, *whole, *mixed, *before,
    )


def backward_kernel(*refs, first):
    q_ref, k_ref, v_ref, mg_ref, local_ref, memout_ref, lse_ref, mem_ref, g_ref = refs[:9]
    dq_ref, dk_ref, dv_ref = refs[-3:]
    g = g_ref[0]
    q = q_ref[...]
    mg = mg_ref[...]
    local_grad = (1.0 - g) * TEMPER * mg
    key = halves(k_ref[...])
    key_t = jnp.concatenate([key[0].T, key[1].T], axis=0)
    key = wide(key)
    value = wide(halves(v_ref[...]))
    query = halves(q * (TEMPER * LOG2E))
    q_twice, q_wide = doubled(query[0]), wide(query)
    grad = halves(local_grad)
    g_twice, g_wide = doubled(grad[0]), wide(grad)
    delta = jnp.sum((local_grad * local_ref[...]).T, axis=0, keepdims=True)
    lq = lifted(q)
    norm = mem_ref[0, HEAD : HEAD + 1, :]
    inverse = 1.0 / (jnp.sum(lq * norm, axis=1, keepdims=True) + 1.0)
    r = jnp.sum(mg * memout_ref[...], axis=1, keepdims=True)
    lift_grad = mm(halves(mg), halves(mem_ref[0, :HEAD, :].T), NN) - r * norm
    dq_ref[...] = lift_grad * (inverse * g) * lifted_slope(q)
    for ref, before in zip((dk_ref, dv_ref), refs[9:11] if first else (None, None)):
        ref[first:, :] = jnp.zeros(q.shape, f32)
        if first:
            ref[:first, :] = before[...]
    seen = causal(BACKWARD_QB)
    for qb in range(q.shape[0] // BACKWARD_QB):
        at = slice(qb * BACKWARD_QB, (qb + 1) * BACKWARD_QB)
        dq_t = 0.0
        for low, high, own in parts_of(qb + first // BACKWARD_QB, BACKWARD_QB):
            scores = scores_of(key[low:high], q_twice[at], query[1][at])
            if own:
                scores = jnp.where(seen, scores, -1e30)
            weights = jnp.exp2(scores - lse_ref[0, :, at])
            dp = scores_of(value[low:high], g_twice[at], grad[1][at])
            ds = halves(weights * (dp - delta[:, at]))
            dv_ref[low:high, :] += times_wide(halves(weights), g_wide[at])
            dk_ref[low:high, :] += times_wide(ds, q_wide[at])
            dq_t = dq_t + tall_times(key_t[:, low:high], ds)
        dq_ref[at, :] += dq_t.T
    if first:
        dk_ref[...] = dk_ref[...] * (1.0 / (TEMPER * LOG2E))
        dv_ref[...] = dv_ref[...] * (1.0 / TEMPER)


def backward_of(second, heads, ins, before, earlier, micros):
    width = ins[0].shape[1]
    low, count = heads

    def rows(n, at=0):
        return pl.BlockSpec((n, HEAD), lambda h: (at, h + low))

    def of_head(x, n=None, at=0):
        return pl.BlockSpec((1, x.shape[1], n or x.shape[2]), lambda h: (h + low, 0, at))

    size, at_part = (REST, MOST // REST) if second else (MOST, 0)
    here = rows(size, at_part)
    seen = rows(SEG if second else MOST)
    shapes = [(SEG, width)] + [(SEG if second else MOST, width)] * 2
    return pl.pallas_call(
        functools.partial(backward_kernel, first=second * MOST),
        grid=(count,),
        in_specs=[here, seen, seen, rows(size), here, here]
        + [of_head(ins[6], size, at_part), of_head(ins[7]), of_head(ins[8])]
        + [rows(MOST)] * len(before)
        + [pl.BlockSpec(memory_space=pl.ANY)] * len(earlier),
        out_specs=[here, seen, seen],
        out_shape=[jax.ShapeDtypeStruct(shape, f32) for shape in shapes],
        input_output_aliases={len(ins) + len(before) + i: i for i in range(len(earlier))},
        compiler_params=pltpu.CompilerParams(vmem_limit_bytes=VMEM_LIMIT),
        cost_estimate=pl.CostEstimate(
            flops=LIGHT, bytes_accessed=micros * MICROSECOND or LIGHT, transcendentals=0
        ),
        name="backward",
    )(*ins, *before, *earlier)


def forward_of(heads, ins, earlier):
    width = ins[0].shape[1]
    low, count = heads
    column = pl.BlockSpec((SEG, HEAD), lambda h: (0, h + low))
    line = pl.BlockSpec((1, 1, SEG), lambda h: (h + low, 0, 0))
    return pl.pallas_call(
        forward_kernel,
        grid=(count,),
        in_specs=[column] * 3 + [pl.BlockSpec(memory_space=pl.ANY)] * len(earlier),
        out_specs=[column, line],
        out_shape=[
            jax.ShapeDtypeStruct((SEG, width), f32),
            jax.ShapeDtypeStruct((width // HEAD, 1, SEG), f32),
        ],
        input_output_aliases={len(ins) + i: i for i in range(len(earlier))},
        compiler_params=pltpu.CompilerParams(vmem_limit_bytes=VMEM_LIMIT),
        cost_estimate=pl.CostEstimate(flops=LIGHT, bytes_accessed=LIGHT, transcendentals=0),
        name="forward",
    )(*ins, *earlier)


def finish_kernel(k_ref, v_ref, dk_ref, dv_ref, state_ref, kg_ref, vg_ref):
    key = k_ref[...]
    state = state_ref[0, :HEAD, :]
    norm = state_ref[0, HEAD : HEAD + 1, :]
    lift_grad = mm(halves(v_ref[...]), halves(state.T), NN) + norm
    kg_ref[...] = dk_ref[...] + lift_grad * lifted_slope(key)
    vg_ref[...] = dv_ref[...] + mm(halves(lifted(key)), halves(state), NN)


def columns():
    return pl.BlockSpec((SEG, HEAD), lambda h: (0, h))


def state():
    return pl.BlockSpec((1, ROWS, HEAD), lambda h: (h, 0, 0))


def row(width):
    return pl.BlockSpec((1, 1, width), lambda h: (h, 0, 0))


def per_head(kernel, heads, ins, outs, name):
    width = heads * HEAD
    kinds = {
        "c": (columns(), jax.ShapeDtypeStruct((SEG, width), f32)),
        "s": (state(), jax.ShapeDtypeStruct((heads, ROWS, HEAD), f32)),
        "g": (row(HEAD), jax.ShapeDtypeStruct((heads, 1, HEAD), f32)),
        "t": (
            pl.BlockSpec((HEAD, SEG), lambda h: (h, 0)),
            jax.ShapeDtypeStruct((width, SEG), bf16),
        ),
        "l": (row(SEG), jax.ShapeDtypeStruct((heads, 1, SEG), f32)),
    }
    return pl.pallas_call(
        kernel,
        grid=(heads,),
        in_specs=[kinds[i][0] for i in ins],
        out_specs=[kinds[o][0] for o in outs],
        out_shape=[kinds[o][1] for o in outs],
        compiler_params=pltpu.CompilerParams(vmem_limit_bytes=VMEM_LIMIT),
        cost_estimate=pl.CostEstimate(
            flops=LIGHT, bytes_accessed=LIGHT, transcendentals=0
        ),
        name=name,
    )


def ring(n, step):
    return [(i, (i + step) % n) for i in range(n)]


def grid_sizes():
    heads = lax.axis_size("head")
    return heads, lax.axis_size("ctx") // (2 * heads)


def place():
    xs, zs = grid_sizes()
    at = lax.axis_index("ctx")
    return at // (2 * zs), (at // 2) % zs, at % 2


def core_swap(block):
    n = lax.axis_size("ctx")
    return lax.ppermute(block, "ctx", [(i, i ^ 1) for i in range(n)])


def moved(block, axis, to):
    xs, zs = grid_sizes()
    pairs = []
    for x in range(xs):
        for z in range(zs):
            x_to, z_to = (to(x), z) if axis == "x" else (x, to(z))
            if x_to is not None and z_to is not None:
                for c in range(2):
                    pairs.append(((x * zs + z) * 2 + c, (x_to * zs + z_to) * 2 + c))
    return lax.ppermute(block, "ctx", pairs)


def scan_of_four(block, axis, at, later, beside_first, beside_second):
    near = beside_first(block, moved(block, axis, lambda i: i ^ 1))
    pair = block + near
    other = beside_second(pair, moved(pair, axis, lambda i: 3 - i))
    counts_near = (at % 2 == 0) if later else (at % 2 == 1)
    counts_other = (at < 2) if later else (at >= 2)
    return jnp.where(counts_near, near, 0.0) + jnp.where(counts_other, other, 0.0), pair + other


def scan_over_ctx(packed, later, work=None):
    xs, zs = grid_sizes()
    x, z, core = place()
    half = packed.shape[0] // 2
    first, second = packed[:half], packed[half:]
    is_first = core == 0
    mine = jnp.where(is_first, first, second)
    theirs = core_swap(jnp.where(is_first, second, first))
    chip = mine + theirs

    def beside_step(i):
        def tie(block, arrived):
            if work is None:
                return arrived
            done = work(i, block)
            arrived, *done[:] = lax.optimization_barrier((arrived, *done))
            return arrived

        return tie

    before_z, total_z = scan_of_four(chip, "z", z, later, beside_step(0), beside_step(1))
    before_x, total = scan_of_four(
        total_z, "x", x, later, beside_step(2), beside_step(3)
    )
    outside = before_z + before_x
    counts_other = is_first if later else jnp.logical_not(is_first)
    for_me = outside + jnp.where(counts_other, theirs, 0.0)
    for_other = outside + jnp.where(counts_other, 0.0, mine)
    row = lax.broadcasted_iota(jnp.int32, (1, ROWS, 1), 1)
    totals = jnp.where(row == ROWS - 1, total[:, HEAD + 1 : HEAD + 2, :], 0.0)
    for_me, for_other = for_me + totals, for_other + totals
    swapped = core_swap(for_other)
    low = jnp.where(is_first, for_me, swapped)
    high = jnp.where(is_first, swapped, for_me)
    return jnp.concatenate([low, high], axis=0)


def across(i):
    return 3 - i


def beside(i):
    return i ^ 1


def outgoing(piece, at, first, second):
    far = first(at)
    return jnp.stack([piece(far), piece(second(far))])


def half_scattered(piece, axis, at, first, second, sent=None):
    sent = outgoing(piece, at, first, second) if sent is None else sent
    came = moved(sent, axis, first)
    return piece(at) + came[0], piece(second(at)) + came[1]


def scattered(kept, passed, axis, second):
    return kept + moved(passed, axis, second)


def at_place(pieces, i):
    return lax.dynamic_index_in_dim(pieces, i, 0, keepdims=False)


def on_device(queries, keys, values, gate_logit, out_weight, out_grad):
    heads = gate_logit.shape[0]
    width = heads * HEAD
    hs = lax.axis_size("head")
    head = lax.axis_index("head")
    xs, zs = grid_sizes()
    x, z, core = place()
    rows, cols = out_grad.shape


    def up(block):
        return lax.ppermute(block, "head", ring(hs, 1))

    def down(block):
        return lax.ppermute(block, "head", ring(hs, -1))

    left, right = up(out_grad), down(out_grad)

    gate = jax.nn.sigmoid(gate_logit)
    g = jnp.broadcast_to(gate[:, None, None], (heads, 1, HEAD))

    (packed,) = per_head(update_kernel, heads, "cc", "s", "update")(keys, values)
    forwards = []

    def forward(step, block):
        if step % 2 == 0:
            forwards[:] = forward_of((step, heads // 2), (queries, keys, values), forwards)
        return forwards

    before = scan_over_ctx(packed, False, forward)
    local_out, lse = forwards
    *mixed, memory_out, lqd = per_head(mix_kernel, heads, "ccsg", "ttcc", "mix")(
        queries, local_out, before, g
    )

    def block_at(distance):
        return (head + hs - distance) % hs

    own_at, left_at, far_at, right_at = (block_at(d) for d in range(4))
    add = functools.partial(round_of, out_weight=out_weight, mixed=mixed, core=core)

    def chip_piece(mine, came, start=0):
        return lambda i: at_place(mine, start + i) + at_place(came, start + i)

    mg, mine_own, send_own = add(None, [out_grad], [zs * own_at])
    came_own = core_swap(send_own)
    own_parts = half_scattered(chip_piece(mine_own, came_own), "z", z, across, beside)
    left, right, *own_parts = lax.optimization_barrier((left, right, *own_parts))
    onward = onward_of(left, right)
    far_1 = up(onward[0]), down(onward[1])
    far_2 = up(onward[2]), down(onward[3])

    mg, mine_sides, send_sides = add(mg, [left, right], [zs * left_at, zs * right_at])
    sum_own = scattered(*own_parts, "z", beside)
    *far_1, mine_sides, send_sides, sum_own = lax.optimization_barrier(
        (*far_1, mine_sides, send_sides, sum_own)
    )
    came_sides = core_swap(send_sides)
    far_places = [2 * far_at, 2 * far_at + 1]
    tail = functools.partial(
        tail_of, places=far_places, out_weight=out_weight, mixed=mixed, core=core,
        whole=(lqd, memory_out, local_out),
    )
    mg_1, *far_sums = tail(0, mg, far_1, before=())
    attended = queries, keys, values

    def backward_ins(part):
        return (*attended, part, local_out, memory_out, lse, before, g)

    mg_1, came_sides = lax.optimization_barrier((mg_1, came_sides))
    left_parts = half_scattered(chip_piece(mine_sides, came_sides), "z", z, across, beside)
    right_parts = half_scattered(chip_piece(mine_sides, came_sides, zs), "z", z, beside, across)
    early = backward_of(0, (0, heads), backward_ins(mg_1), (), (), 0)
    *far_2, dq, dk, dv, left_kept, left_passed, right_kept, right_passed = (
        lax.optimization_barrier((*far_2, *early, *left_parts, *right_parts))
    )
    mg_2, back, mine_far, send_far = tail(1, mg, far_2, before=far_sums)
    sum_left = scattered(left_kept, left_passed, "z", beside)
    sum_right = scattered(right_kept, right_passed, "z", across)
    back, send_far, sum_left, sum_right = lax.optimization_barrier(
        (back, send_far, sum_left, sum_right)
    )
    came_far = core_swap(send_far)
    far_parts = half_scattered(chip_piece(mine_far, came_far), "z", z, across, beside)

    shares = [(0, heads // 2), (heads // 2, heads // 4), (3 * heads // 4, heads // 4)]
    held = {}

    def piece_x(i):
        parts = jnp.stack([sum_own, sum_left, held[1][3], sum_right])
        return at_place(parts, (head + hs - i) % hs)

    def beside_scan(step, block):
        if step < 3:
            tied = [mg_2, block]
            if step == 2:
                tied.append(outgoing(piece_x, x, across, beside))
            part, _, *sent = lax.optimization_barrier(tied)
            earlier = [dq] if step == 0 else held[step - 1][:3]
            held[step] = [
                *backward_of(1, shares[step], backward_ins(part), (dk, dv), earlier, 5)
            ]
            if step == 0:
                held[step] += far_parts
            elif step == 1:
                held[step].append(scattered(*held[0][3:], "z", beside))
            else:
                held["sent"] = sent[0]
        else:
            held[step] = [*half_scattered(piece_x, "x", x, across, beside, held["sent"])]
        return held[step]

    after = scan_over_ctx(back, True, beside_scan)
    weight_grad = scattered(*held[3], "x", beside).T

    key_grad, value_grad = per_head(finish_kernel, heads, "ccccs", "cc", "finish")(
        keys, values, *held[2][1:3], after
    )
    dq = held[2][0]

    gate_sum = jnp.sum(after[:, ROWS - 1, :], axis=-1)
    gate_grad = gate_sum * gate * (1.0 - gate)
    return dq, key_grad, value_grad, weight_grad, gate_grad


def solution(mesh):
    in_specs = (
        P("ctx", "head"),
        P("ctx", "head"),
        P("ctx", "head"),
        P("head"),
        P("head", None),
        P("ctx", "head"),
    )
    out_specs = (P("ctx", "head"), P("ctx", "head"), P("ctx", "head"), P("ctx", "head"), P("head"))
    return jax.shard_map(
        on_device, mesh=mesh, in_specs=in_specs, out_specs=out_specs, check_vma=False
    )
```

```python
import functools
import math

import jax
import jax.numpy as jnp
from jax import lax
from jax.experimental import pallas as pl
from jax.experimental.pallas import tpu as pltpu
from jax.sharding import PartitionSpec as P

SEG = 1024
HEAD = 128
ROWS = 136
FORWARD_QB = 512
BACKWARD_QB = 256
MOST = SEG // 2
REST = SEG - MOST
STEP = 256
LIGHT = 2**16
VMEM_LIMIT = 60 * 2**20
MICROSECOND = 3_600_000

f32 = jnp.float32
bf16 = jnp.bfloat16
HIGH = lax.Precision.HIGH


def lifted(x):
    return jnp.where(x > 0, x + 1.0, jnp.exp(jnp.minimum(x, 0.0)))


def lifted_slope(x):
    return jnp.where(x > 0, 1.0, jnp.exp(jnp.minimum(x, 0.0)))


def halves(x):
    hi = x.astype(bf16)
    return hi, (x - hi.astype(f32)).astype(bf16)


def mm(a, b, contract):
    dims = ((contract[:1], contract[1:]), ((), ()))

    def one(x, y):
        return lax.dot_general(x, y, dims, preferred_element_type=f32)

    return one(a[0], b[0]) + (one(a[0], b[1]) + one(a[1], b[0]))


NN = (1, 0)
NT = (1, 1)
TN = (0, 0)


def dot(a, b, contract):
    return lax.dot_general(
        a, b, ((contract[:1], contract[1:]), ((), ())), preferred_element_type=f32
    )


def wide(pair):
    return jnp.concatenate(pair, axis=1)


def doubled(x):
    return jnp.concatenate([x, x], axis=1)


def scores_of(a_wide, b_hi_twice, b_lo):
    return dot(a_wide, b_hi_twice, NT) + dot(a_wide[:, :HEAD], b_lo, NT)


def times_wide(a, b_wide):
    both = dot(a[0], b_wide, NN)
    return both[:, :HEAD] + (both[:, HEAD:] + dot(a[1], b_wide[:, :HEAD], NN))


def tall_times(a_tall, b):
    both = dot(a_tall, b[0], NN)
    return both[:HEAD] + (both[HEAD:] + dot(a_tall[:HEAD], b[1], NN))


def update_kernel(k_ref, v_ref, out_ref):
    lk = lifted(k_ref[...])
    out_ref[0, :HEAD, :] = mm(halves(lk.T), halves(v_ref[...]), NN)
    out_ref[0, HEAD : HEAD + 1, :] = jnp.sum(lk, axis=0, keepdims=True)
    out_ref[0, HEAD + 1 :, :] = jnp.zeros((ROWS - HEAD - 1, HEAD), f32)


LOG2E = math.log2(math.e)
TEMPER = 1.0 / math.sqrt(HEAD)


def parts_of(qb, size):
    return ([(0, qb * size, False)] if qb else []) + [(qb * size, (qb + 1) * size, True)]


def causal(size):
    t = lax.broadcasted_iota(jnp.int32, (size, size), 0)
    return t <= lax.broadcasted_iota(jnp.int32, (size, size), 1)


def forward_kernel(q_ref, k_ref, v_ref, *refs):
    out_ref, lse_ref = refs[-2:]
    key = wide(halves(k_ref[...]))
    value_t = jnp.concatenate(halves(v_ref[...].T), axis=0)
    q_hi, q_lo = halves(q_ref[...] * (TEMPER * LOG2E))
    q_twice = doubled(q_hi)
    seen = causal(FORWARD_QB)
    for qb in range(SEG // FORWARD_QB):
        at = slice(qb * FORWARD_QB, (qb + 1) * FORWARD_QB)
        scores = []
        for low, high, own in parts_of(qb, FORWARD_QB):
            part = scores_of(key[low:high], q_twice[at], q_lo[at])
            scores.append(jnp.where(seen, part, -1e30) if own else part)
        top = functools.reduce(
            jnp.maximum, [jnp.max(part, axis=0, keepdims=True) for part in scores]
        )
        total, out_t = 0.0, 0.0
        for (low, high, _), part in zip(parts_of(qb, FORWARD_QB), scores):
            weights = jnp.exp2(part - top)
            total = total + jnp.sum(weights, axis=0, keepdims=True)
            out_t = out_t + tall_times(value_t[:, low:high], halves(weights))
        out_ref[at, :] = (out_t * (1.0 / total)).T
        lse_ref[0, :, at] = top + jnp.log2(total)


def mix_kernel(q_ref, local_ref, mem_ref, g_ref, hi_ref, lo_ref, memout_ref, lqd_ref):
    g = g_ref[0]
    lq = lifted(q_ref[...])
    norm = mem_ref[0, HEAD : HEAD + 1, :]
    denom = jnp.sum(lq * norm, axis=1, keepdims=True) + 1.0
    inverse = 1.0 / denom
    memory_out = mm(halves(lq), halves(mem_ref[0, :HEAD, :]), NN) * inverse
    memout_ref[...] = memory_out
    mixed = g * memory_out + (1.0 - g) * local_ref[...]
    hi_ref[...], lo_ref[...] = halves(mixed.T)
    lqd_ref[...] = lq * (inverse * g)


def add_weight_part(mixed, block, first, start, mine_ref, send_ref):
    part = mm(mixed, block, NN)
    groups = part.shape[1] // (2 * HEAD)
    for k in range(groups):
        even = part[:, 2 * k * HEAD : (2 * k + 1) * HEAD]
        odd = part[:, (2 * k + 1) * HEAD : (2 * k + 2) * HEAD]
        mine_ref[start + k] += jnp.where(first, even, odd)
        send_ref[start + k] += jnp.where(first, odd, even)


def block_kernel(at_ref, *refs, blocks, added, summed):
    refs = list(refs)

    def take(n):
        taken, refs[:] = refs[:n], refs[n:]
        return taken

    acc, block_refs, w_refs, mixed_refs = take(added), take(blocks), take(blocks), take(2)
    before, (out_ref,), by_core = take(summed), take(1), take(2)

    @pl.when(pl.program_id(0) == 0)
    def _():
        for n, w_ref in enumerate(w_refs):
            refs[2 * n][...], refs[2 * n + 1][...] = halves(w_ref[...])
        for n, ref in enumerate(by_core):
            ref[...] = before[n][...] if summed else jnp.zeros_like(ref)

    mixed = tuple(ref[...] for ref in mixed_refs)
    total = acc[0][...] if added else None
    start = 0
    for n, block_ref in enumerate(block_refs):
        block = halves(block_ref[...])
        product = mm(block, (refs[2 * n][...], refs[2 * n + 1][...]), NT)
        total = product if total is None else total + product
        add_weight_part(mixed, block, at_ref[blocks] == 0, start, *by_core)
        start += block_ref.shape[1] // (2 * HEAD)
    out_ref[...] = total


def tail_kernel(at_ref, *refs):
    acc_ref, a_ref, b_ref, wa_ref, wb_ref, lqd_ref, memout_ref, local_ref = refs[:8]
    mhi_ref, mlo_ref, *before = refs[8:-8]
    mg_ref, state_ref, mine_ref, send_ref, *w = refs[-8:]

    @pl.when(pl.program_id(0) == 0)
    def _():
        w[0][...], w[1][...] = halves(wa_ref[...])
        w[2][...], w[3][...] = halves(wb_ref[...])
        for n, ref in enumerate((state_ref, mine_ref, send_ref)):
            ref[...] = before[n][...] if before else jnp.zeros_like(ref)

    a, b = halves(a_ref[...]), halves(b_ref[...])
    mg = acc_ref[...] + mm(a, (w[0][...], w[1][...]), NT)
    mg = mg + mm(b, (w[2][...], w[3][...]), NT)
    mg_ref[...] = mg
    for h in range(state_ref.shape[0]):
        at = slice(h * HEAD, (h + 1) * HEAD)
        here, lqd, memory_out = mg[:, at], lqd_ref[:, at], memout_ref[:, at]
        state_ref[h, :HEAD, :] += mm(halves(lqd.T), halves(here), NN)
        r = jnp.sum(here * memory_out, axis=1, keepdims=True)
        state_ref[h, HEAD : HEAD + 1, :] -= jnp.sum(lqd * r, axis=0, keepdims=True)
        state_ref[h, HEAD + 1 : HEAD + 2, :] += jnp.sum(
            here * (memory_out - local_ref[:, at]), axis=0, keepdims=True
        )
    mixed, first = (mhi_ref[...], mlo_ref[...]), at_ref[2] == 0
    groups = a_ref.shape[1] // (2 * HEAD)
    add_weight_part(mixed, a, first, 0, mine_ref, send_ref)
    add_weight_part(mixed, b, first, groups, mine_ref, send_ref)


def rows_of(width, first=0):
    return pl.BlockSpec((STEP, width), lambda i, at: (i + first // STEP, 0))


def weight_specs(width, blocks):
    return [
        pl.BlockSpec(
            (width, block.shape[1]), lambda i, at, k=k: (0, at[k]), pipeline_mode=pl.Buffered(1)
        )
        for k, block in enumerate(blocks)
    ]


def tail_kernel(at_ref, *refs):
    acc_ref, a_ref, b_ref, wa_ref, wb_ref, lqd_ref, memout_ref, local_ref = refs[:8]
    mhi_ref, mlo_ref, *before = refs[8:-8]
    mg_ref, state_ref, mine_ref, send_ref, *w = refs[-8:]

    @pl.when(pl.program_id(0) == 0)
    def _():
        w[0][...], w[1][...] = halves(wa_ref[...])
        w[2][...], w[3][...] = halves(wb_ref[...])
        for n, ref in enumerate((state_ref, mine_ref, send_ref)):
            ref[...] = before[n][...] if before else jnp.zeros_like(ref)

    a, b = halves(a_ref[...]), halves(b_ref[...])
    mg = acc_ref[...] + mm(a, (w[0][...], w[1][...]), NT)
    mg = mg + mm(b, (w[2][...], w[3][...]), NT)
    mg_ref[...] = mg
    for h in range(state_ref.shape[0]):
        at = slice(h * HEAD, (h + 1) * HEAD)
        here, lqd, memory_out = mg[:, at], lqd_ref[:, at], memout_ref[:, at]
        state_ref[h, :HEAD, :] += mm(halves(lqd.T), halves(here), NN)
        r = jnp.sum(here * memory_out, axis=1, keepdims=True)
        state_ref[h, HEAD : HEAD + 1, :] -= jnp.sum(lqd * r, axis=0, keepdims=True)
        state_ref[h, HEAD + 1 : HEAD + 2, :] += jnp.sum(
            here * (memory_out - local_ref[:, at]), axis=0, keepdims=True
        )
    mixed, first = (mhi_ref[...], mlo_ref[...]), at_ref[2] == 0
    groups = a_ref.shape[1] // (2 * HEAD)
    add_weight_part(mixed, a, first, 0, mine_ref, send_ref)
    add_weight_part(mixed, b, first, groups, mine_ref, send_ref)


def rows_of(width, first=0):
    return pl.BlockSpec((STEP, width), lambda i, at: (i + first // STEP, 0))


def weight_specs(width, blocks):
    return [
        pl.BlockSpec(
            (width, block.shape[1]), lambda i, at, k=k: (0, at[k]), pipeline_mode=pl.Buffered(1)
        )
        for k, block in enumerate(blocks)
    ]


def tail_kernel(at_ref, *refs):
    acc_ref, a_ref, b_ref, wa_ref, wb_ref, lqd_ref, memout_ref, local_ref = refs[:8]
    mhi_ref, mlo_ref, *before = refs[8:-8]
    mg_ref, state_ref, mine_ref, send_ref, *w = refs[-8:]

    @pl.when(pl.program_id(0) == 0)
    def _():
        w[0][...], w[1][...] = halves(wa_ref[...])
        w[2][...], w[3][...] = halves(wb_ref[...])
        for n, ref in enumerate((state_ref, mine_ref, send_ref)):
            ref[...] = before[n][...] if before else jnp.zeros_like(ref)

    a, b = halves(a_ref[...]), halves(b_ref[...])
    mg = acc_ref[...] + mm(a, (w[0][...], w[1][...]), NT)
    mg = mg + mm(b, (w[2][...], w[3][...]), NT)
    mg_ref[...] = mg
    for h in range(state_ref.shape[0]):
        at = slice(h * HEAD, (h + 1) * HEAD)
        here, lqd, memory_out = mg[:, at], lqd_ref[:, at], memout_ref[:, at]
        state_ref[h, :HEAD, :] += mm(halves(lqd.T), halves(here), NN)
        r = jnp.sum(here * memory_out, axis=1, keepdims=True)
        state_ref[h, HEAD : HEAD + 1, :] -= jnp.sum(lqd * r, axis=0, keepdims=True)
        state_ref[h, HEAD + 1 : HEAD + 2, :] += jnp.sum(
            here * (memory_out - local_ref[:, at]), axis=0, keepdims=True
        )
    mixed, first = (mhi_ref[...], mlo_ref[...]), at_ref[2] == 0
    groups = a_ref.shape[1] // (2 * HEAD)
    add_weight_part(mixed, a, first, 0, mine_ref, send_ref)
    add_weight_part(mixed, b, first, groups, mine_ref, send_ref)


def rows_of(width, first=0):
    return pl.BlockSpec((STEP, width), lambda i, at: (i + first // STEP, 0))


def weight_specs(width, blocks):
    return [
        pl.BlockSpec(
            (width, block.shape[1]), lambda i, at, k=k: (0, at[k]), pipeline_mode=pl.Buffered(1)
        )
        for k, block in enumerate(blocks)
    ]


def tail_kernel(at_ref, *refs):
    acc_ref, a_ref, b_ref, wa_ref, wb_ref, lqd_ref, memout_ref, local_ref = refs[:8]
    mhi_ref, mlo_ref, *before = refs[8:-8]
    mg_ref, state_ref, mine_ref, send_ref, *w = refs[-8:]

    @pl.when(pl.program_id(0) == 0)
    def _():
        w[0][...], w[1][...] = halves(wa_ref[...])
        w[2][...], w[3][...] = halves(wb_ref[...])
        for n, ref in enumerate((state_ref, mine_ref, send_ref)):
            ref[...] = before[n][...] if before else jnp.zeros_like(ref)

    a, b = halves(a_ref[...]), halves(b_ref[...])
    mg = acc_ref[...] + mm(a, (w[0][...], w[1][...]), NT)
    mg = mg + mm(b, (w[2][...], w[3][...]), NT)
    mg_ref[...] = mg
    for h in range(state_ref.shape[0]):
        at = slice(h * HEAD, (h + 1) * HEAD)
        here, lqd, memory_out = mg[:, at], lqd_ref[:, at], memout_ref[:, at]
        state_ref[h, :HEAD, :] += mm(halves(lqd.T), halves(here), NN)
        r = jnp.sum(here * memory_out, axis=1, keepdims=True)
        state_ref[h, HEAD : HEAD + 1, :] -= jnp.sum(lqd * r, axis=0, keepdims=True)
        state_ref[h, HEAD + 1 : HEAD + 2, :] += jnp.sum(
            here * (memory_out - local_ref[:, at]), axis=0, keepdims=True
        )
    mixed, first = (mhi_ref[...], mlo_ref[...]), at_ref[2] == 0
    groups = a_ref.shape[1] // (2 * HEAD)
    add_weight_part(mixed, a, first, 0, mine_ref, send_ref)
    add_weight_part(mixed, b, first, groups, mine_ref, send_ref)


def rows_of(width, first=0):
    return pl.BlockSpec((STEP, width), lambda i, at: (i + first // STEP, 0))


def weight_specs(width, blocks):
    return [
        pl.BlockSpec(
            (width, block.shape[1]), lambda i, at, k=k: (0, at[k]), pipeline_mode=pl.Buffered(1)
        )
        for k, block in enumerate(blocks)
    ]


def onward_kernel(*refs):
    for source, target in zip(refs[:4], refs[4:]):
        target[...] = source[...]


def onward_of(left, right):
    rows, half, step = MOST, left.shape[1] // 2, MOST // 2

    def rows_from(first, column):
        return pl.BlockSpec((step, half), lambda i: (i + first // step, column))

    return pl.pallas_call(
        onward_kernel,
        grid=(rows // step,),
        in_specs=[rows_from(0, 0), rows_from(0, 1), rows_from(MOST, 0), rows_from(MOST, 1)],
        out_specs=[rows_from(0, 0)] * 4,
        out_shape=[jax.ShapeDtypeStruct((rows, half), f32)] * 4,
        compiler_params=pltpu.CompilerParams(vmem_limit_bytes=VMEM_LIMIT),
        cost_estimate=pl.CostEstimate(flops=LIGHT, bytes_accessed=LIGHT, transcendentals=0),
        name="onward",
    )(left, right, left, right)


def round_of(acc, blocks, places, out_weight, mixed, core, first=0, before=(), micros=0):
    rows = blocks[0].shape[0]
    width = out_weight.shape[0]
    n = len(blocks)
    groups = sum(block.shape[1] for block in blocks) // (2 * HEAD)
    at = jnp.stack([*places, core]).astype(jnp.int32)
    acc = [] if acc is None else [acc]
    by_core = pl.BlockSpec((groups, width, HEAD), lambda i, at: (0, 0, 0))
    by_core_shape = jax.ShapeDtypeStruct((groups, width, HEAD), f32)
    return pl.pallas_call(
        functools.partial(block_kernel, blocks=n, added=len(acc), summed=len(before)),
        grid_spec=pltpu.PrefetchScalarGridSpec(
            num_scalar_prefetch=1,
            grid=(rows // STEP,),
            in_specs=[rows_of(width, first) for _ in acc]
            + [rows_of(block.shape[1]) for block in blocks]
            + weight_specs(width, blocks)
            + [pl.BlockSpec((width, STEP), lambda i, at: (0, i + first // STEP))] * 2
            + [by_core] * len(before),
            out_specs=[rows_of(width, first)] + [by_core] * 2,
            scratch_shapes=[
                pltpu.VMEM((width, block.shape[1]), bf16) for block in blocks for _ in range(2)
            ],
        ),
        out_shape=[jax.ShapeDtypeStruct((SEG, width), f32)] + [by_core_shape] * 2,
        input_output_aliases={1: 0} if acc else {},
        compiler_params=pltpu.CompilerParams(vmem_limit_bytes=VMEM_LIMIT),
        cost_estimate=pl.CostEstimate(flops=LIGHT, bytes_accessed=LIGHT, transcendentals=0),
        name="round",
    )(at, *acc, *blocks, *([out_weight] * n), *mixed, *before)


def tail_of(second, acc, blocks, places, out_weight, mixed, core, whole, before):
    rows, deep = blocks[0].shape
    width = out_weight.shape[0]
    first = second * MOST
    by_core = deep // HEAD, width, HEAD
    sums = [(width // HEAD, ROWS, HEAD), by_core, by_core]
    sum_specs = [pl.BlockSpec(shape, lambda i, at: (0, 0, 0)) for shape in sums]
    return pl.pallas_call(
        tail_kernel,
        grid_spec=pltpu.PrefetchScalarGridSpec(
            num_scalar_prefetch=1,
            grid=(rows // STEP,),
            in_specs=[rows_of(width, first)]
            + [rows_of(deep)] * 2
            + weight_specs(width, blocks)
            + [rows_of(width, first)] * 3
            + [pl.BlockSpec((width, STEP), lambda i, at: (0, i + first // STEP))] * 2
            + sum_specs[: len(before)],
            out_specs=[rows_of(width), *sum_specs],
            scratch_shapes=[pltpu.VMEM((width, deep), bf16) for _ in range(4)],
        ),
        out_shape=[jax.ShapeDtypeStruct(shape, f32) for shape in [(rows, width), *sums]],
        compiler_params=pltpu.CompilerParams(vmem_limit_bytes=VMEM_LIMIT),
        cost_estimate=pl.CostEstimate(flops=LIGHT, bytes_accessed=LIGHT, transcendentals=0),
        name="tail",
    )(
        jnp.stack([*places, core]).astype(jnp.int32),
        acc, *blocks, out_weight, out_weight, *whole, *mixed, *before,
    )


def backward_kernel(*refs, first):
    q_ref, k_ref, v_ref, mg_ref, local_ref, memout_ref, lse_ref, mem_ref, g_ref = refs[:9]
    dq_ref, dk_ref, dv_ref = refs[-3:]
    g = g_ref[0]
    q = q_ref[...]
    mg = mg_ref[...]
    local_grad = (1.0 - g) * TEMPER * mg
    key = halves(k_ref[...])
    key_t = jnp.concatenate([key[0].T, key[1].T], axis=0)
    key = wide(key)
    value = wide(halves(v_ref[...]))
    query = halves(q * (TEMPER * LOG2E))
    q_twice, q_wide = doubled(query[0]), wide(query)
    grad = halves(local_grad)
    g_twice, g_wide = doubled(grad[0]), wide(grad)
    delta = jnp.sum((local_grad * local_ref[...]).T, axis=0, keepdims=True)
    lq = lifted(q)
    norm = mem_ref[0, HEAD : HEAD + 1, :]
    inverse = 1.0 / (jnp.sum(lq * norm, axis=1, keepdims=True) + 1.0)
    r = jnp.sum(mg * memout_ref[...], axis=1, keepdims=True)
    lift_grad = mm(halves(mg), halves(mem_ref[0, :HEAD, :].T), NN) - r * norm
    dq_ref[...] = lift_grad * (inverse * g) * lifted_slope(q)
    for ref, before in zip((dk_ref, dv_ref), refs[9:11] if first else (None, None)):
        ref[first:, :] = jnp.zeros(q.shape, f32)
        if first:
            ref[:first, :] = before[...]
    seen = causal(BACKWARD_QB)
    for qb in range(q.shape[0] // BACKWARD_QB):
        at = slice(qb * BACKWARD_QB, (qb + 1) * BACKWARD_QB)
        dq_t = 0.0
        for low, high, own in parts_of(qb + first // BACKWARD_QB, BACKWARD_QB):
            scores = scores_of(key[low:high], q_twice[at], query[1][at])
            if own:
                scores = jnp.where(seen, scores, -1e30)
            weights = jnp.exp2(scores - lse_ref[0, :, at])
            dp = scores_of(value[low:high], g_twice[at], grad[1][at])
            ds = halves(weights * (dp - delta[:, at]))
            dv_ref[low:high, :] += times_wide(halves(weights), g_wide[at])
            dk_ref[low:high, :] += times_wide(ds, q_wide[at])
            dq_t = dq_t + tall_times(key_t[:, low:high], ds)
        dq_ref[at, :] += dq_t.T
    if first:
        dk_ref[...] = dk_ref[...] * (1.0 / (TEMPER * LOG2E))
        dv_ref[...] = dv_ref[...] * (1.0 / TEMPER)


def backward_of(second, heads, ins, before, earlier, micros):
    width = ins[0].shape[1]
    low, count = heads

    def rows(n, at=0):
        return pl.BlockSpec((n, HEAD), lambda h: (at, h + low))

    def of_head(x, n=None, at=0):
        return pl.BlockSpec((1, x.shape[1], n or x.shape[2]), lambda h: (h + low, 0, at))

    size, at_part = (REST, MOST // REST) if second else (MOST, 0)
    here = rows(size, at_part)
    seen = rows(SEG if second else MOST)
    shapes = [(SEG, width)] + [(SEG if second else MOST, width)] * 2
    return pl.pallas_call(
        functools.partial(backward_kernel, first=second * MOST),
        grid=(count,),
        in_specs=[here, seen, seen, rows(size), here, here]
        + [of_head(ins[6], size, at_part), of_head(ins[7]), of_head(ins[8])]
        + [rows(MOST)] * len(before)
        + [pl.BlockSpec(memory_space=pl.ANY)] * len(earlier),
        out_specs=[here, seen, seen],
        out_shape=[jax.ShapeDtypeStruct(shape, f32) for shape in shapes],
        input_output_aliases={len(ins) + len(before) + i: i for i in range(len(earlier))},
        compiler_params=pltpu.CompilerParams(vmem_limit_bytes=VMEM_LIMIT),
        cost_estimate=pl.CostEstimate(
            flops=LIGHT, bytes_accessed=micros * MICROSECOND or LIGHT, transcendentals=0
        ),
        name="backward",
    )(*ins, *before, *earlier)


def forward_of(heads, ins, earlier):
    width = ins[0].shape[1]
    low, count = heads
    column = pl.BlockSpec((SEG, HEAD), lambda h: (0, h + low))
    line = pl.BlockSpec((1, 1, SEG), lambda h: (h + low, 0, 0))
    return pl.pallas_call(
        forward_kernel,
        grid=(count,),
        in_specs=[column] * 3 + [pl.BlockSpec(memory_space=pl.ANY)] * len(earlier),
        out_specs=[column, line],
        out_shape=[
            jax.ShapeDtypeStruct((SEG, width), f32),
            jax.ShapeDtypeStruct((width // HEAD, 1, SEG), f32),
        ],
        input_output_aliases={len(ins) + i: i for i in range(len(earlier))},
        compiler_params=pltpu.CompilerParams(vmem_limit_bytes=VMEM_LIMIT),
        cost_estimate=pl.CostEstimate(flops=LIGHT, bytes_accessed=LIGHT, transcendentals=0),
        name="forward",
    )(*ins, *earlier)


def finish_kernel(k_ref, v_ref, dk_ref, dv_ref, state_ref, kg_ref, vg_ref):
    key = k_ref[...]
    state = state_ref[0, :HEAD, :]
    norm = state_ref[0, HEAD : HEAD + 1, :]
    lift_grad = mm(halves(v_ref[...]), halves(state.T), NN) + norm
    kg_ref[...] = dk_ref[...] + lift_grad * lifted_slope(key)
    vg_ref[...] = dv_ref[...] + mm(halves(lifted(key)), halves(state), NN)


def columns():
    return pl.BlockSpec((SEG, HEAD), lambda h: (0, h))


def state():
    return pl.BlockSpec((1, ROWS, HEAD), lambda h: (h, 0, 0))


def row(width):
    return pl.BlockSpec((1, 1, width), lambda h: (h, 0, 0))


def per_head(kernel, heads, ins, outs, name):
    width = heads * HEAD
    kinds = {
        "c": (columns(), jax.ShapeDtypeStruct((SEG, width), f32)),
        "s": (state(), jax.ShapeDtypeStruct((heads, ROWS, HEAD), f32)),
        "g": (row(HEAD), jax.ShapeDtypeStruct((heads, 1, HEAD), f32)),
        "t": (
            pl.BlockSpec((HEAD, SEG), lambda h: (h, 0)),
            jax.ShapeDtypeStruct((width, SEG), bf16),
        ),
        "l": (row(SEG), jax.ShapeDtypeStruct((heads, 1, SEG), f32)),
    }
    return pl.pallas_call(
        kernel,
        grid=(heads,),
        in_specs=[kinds[i][0] for i in ins],
        out_specs=[kinds[o][0] for o in outs],
        out_shape=[kinds[o][1] for o in outs],
        compiler_params=pltpu.CompilerParams(vmem_limit_bytes=VMEM_LIMIT),
        cost_estimate=pl.CostEstimate(
            flops=LIGHT, bytes_accessed=LIGHT, transcendentals=0
        ),
        name=name,
    )


def ring(n, step):
    return [(i, (i + step) % n) for i in range(n)]


def grid_sizes():
    heads = lax.axis_size("head")
    return heads, lax.axis_size("ctx") // (2 * heads)


def place():
    xs, zs = grid_sizes()
    at = lax.axis_index("ctx")
    return at // (2 * zs), (at // 2) % zs, at % 2


def core_swap(block):
    n = lax.axis_size("ctx")
    return lax.ppermute(block, "ctx", [(i, i ^ 1) for i in range(n)])


def moved(block, axis, to):
    xs, zs = grid_sizes()
    pairs = []
    for x in range(xs):
        for z in range(zs):
            x_to, z_to = (to(x), z) if axis == "x" else (x, to(z))
            if x_to is not None and z_to is not None:
                for c in range(2):
                    pairs.append(((x * zs + z) * 2 + c, (x_to * zs + z_to) * 2 + c))
    return lax.ppermute(block, "ctx", pairs)


def scan_of_four(block, axis, at, later, beside_first, beside_second):
    near = beside_first(block, moved(block, axis, lambda i: i ^ 1))
    pair = block + near
    other = beside_second(pair, moved(pair, axis, lambda i: 3 - i))
    counts_near = (at % 2 == 0) if later else (at % 2 == 1)
    counts_other = (at < 2) if later else (at >= 2)
    return jnp.where(counts_near, near, 0.0) + jnp.where(counts_other, other, 0.0), pair + other


def scan_over_ctx(packed, later, work=None):
    xs, zs = grid_sizes()
    x, z, core = place()
    half = packed.shape[0] // 2
    first, second = packed[:half], packed[half:]
    is_first = core == 0
    mine = jnp.where(is_first, first, second)
    theirs = core_swap(jnp.where(is_first, second, first))
    chip = mine + theirs

    def beside_step(i):
        def tie(block, arrived):
            if work is None:
                return arrived
            done = work(i, block)
            arrived, *done[:] = lax.optimization_barrier((arrived, *done))
            return arrived

        return tie

    before_z, total_z = scan_of_four(chip, "z", z, later, beside_step(0), beside_step(1))
    before_x, total = scan_of_four(
        total_z, "x", x, later, beside_step(2), beside_step(3)
    )
    outside = before_z + before_x
    counts_other = is_first if later else jnp.logical_not(is_first)
    for_me = outside + jnp.where(counts_other, theirs, 0.0)
    for_other = outside + jnp.where(counts_other, 0.0, mine)
    row = lax.broadcasted_iota(jnp.int32, (1, ROWS, 1), 1)
    totals = jnp.where(row == ROWS - 1, total[:, HEAD + 1 : HEAD + 2, :], 0.0)
    for_me, for_other = for_me + totals, for_other + totals
    swapped = core_swap(for_other)
    low = jnp.where(is_first, for_me, swapped)
    high = jnp.where(is_first, swapped, for_me)
    return jnp.concatenate([low, high], axis=0)


def across(i):
    return 3 - i


def beside(i):
    return i ^ 1


def outgoing(piece, at, first, second):
    far = first(at)
    return jnp.stack([piece(far), piece(second(far))])


def half_scattered(piece, axis, at, first, second, sent=None):
    sent = outgoing(piece, at, first, second) if sent is None else sent
    came = moved(sent, axis, first)
    return piece(at) + came[0], piece(second(at)) + came[1]


def scattered(kept, passed, axis, second):
    return kept + moved(passed, axis, second)


def at_place(pieces, i):
    return lax.dynamic_index_in_dim(pieces, i, 0, keepdims=False)


def on_device(queries, keys, values, gate_logit, out_weight, out_grad):
    heads = gate_logit.shape[0]
    width = heads * HEAD
    hs = lax.axis_size("head")
    head = lax.axis_index("head")
    xs, zs = grid_sizes()
    x, z, core = place()
    rows, cols = out_grad.shape


    def up(block):
        return lax.ppermute(block, "head", ring(hs, 1))

    def down(block):
        return lax.ppermute(block, "head", ring(hs, -1))

    left, right = up(out_grad), down(out_grad)

    gate = jax.nn.sigmoid(gate_logit)
    g = jnp.broadcast_to(gate[:, None, None], (heads, 1, HEAD))

    (packed,) = per_head(update_kernel, heads, "cc", "s", "update")(keys, values)
    forwards = []

    def forward(step, block):
        if step % 2 == 0:
            forwards[:] = forward_of((step, heads // 2), (queries, keys, values), forwards)
        return forwards

    before = scan_over_ctx(packed, False, forward)
    local_out, lse = forwards
    *mixed, memory_out, lqd = per_head(mix_kernel, heads, "ccsg", "ttcc", "mix")(
        queries, local_out, before, g
    )

    def block_at(distance):
        return (head + hs - distance) % hs

    own_at, left_at, far_at, right_at = (block_at(d) for d in range(4))
    add = functools.partial(round_of, out_weight=out_weight, mixed=mixed, core=core)

    def chip_piece(mine, came, start=0):
        return lambda i: at_place(mine, start + i) + at_place(came, start + i)

    mg, mine_own, send_own = add(None, [out_grad], [own_at])
    came_own = core_swap(send_own)
    own_parts = half_scattered(chip_piece(mine_own, came_own), "z", z, across, beside)
    left, right, *own_parts = lax.optimization_barrier((left, right, *own_parts))
    onward = onward_of(left, right)
    far_1 = up(onward[0]), down(onward[1])
    far_2 = up(onward[2]), down(onward[3])

    mg, mine_sides, send_sides = add(mg, [left, right], [left_at, right_at])
    sum_own = scattered(*own_parts, "z", beside)
    *far_1, mine_sides, send_sides, sum_own = lax.optimization_barrier(
        (*far_1, mine_sides, send_sides, sum_own)
    )
    came_sides = core_swap(send_sides)
    far_places = [2 * far_at, 2 * far_at + 1]
    tail = functools.partial(
        tail_of, places=far_places, out_weight=out_weight, mixed=mixed, core=core,
        whole=(lqd, memory_out, local_out),
    )
    mg_1, *far_sums = tail(0, mg, far_1, before=())
    attended = queries, keys, values

    def backward_ins(part):
        return (*attended, part, local_out, memory_out, lse, before, g)

    mg_1, came_sides = lax.optimization_barrier((mg_1, came_sides))
    left_parts = half_scattered(chip_piece(mine_sides, came_sides), "z", z, across, beside)
    right_parts = half_scattered(chip_piece(mine_sides, came_sides, zs), "z", z, beside, across)
    early = backward_of(0, (0, heads), backward_ins(mg_1), (), (), 0)
    *far_2, dq, dk, dv, left_kept, left_passed, right_kept, right_passed = (
        lax.optimization_barrier((*far_2, *early, *left_parts, *right_parts))
    )
    mg_2, back, mine_far, send_far = tail(1, mg, far_2, before=far_sums)
    sum_left = scattered(left_kept, left_passed, "z", beside)
    sum_right = scattered(right_kept, right_passed, "z", across)
    back, send_far, sum_left, sum_right = lax.optimization_barrier(
        (back, send_far, sum_left, sum_right)
    )
    came_far = core_swap(send_far)

    pairs = [(0, heads // 2), (heads // 2, heads // 2)]
    held = {}

    def piece_x(i):
        parts = jnp.stack([sum_own, sum_left, held[1][0], sum_right])
        return at_place(parts, (head + hs - i) % hs)

    def beside_scan(step, block):
        if step == 0:
            part, came, _ = lax.optimization_barrier((mg_2, came_far, block))
            far_piece = chip_piece(mine_far, came)
            sent = outgoing(far_piece, z, across, beside)
            sent, part = lax.optimization_barrier((sent, part))
            grads = backward_of(1, pairs[0], backward_ins(part), (dk, dv), [dq], 6)
            held[0] = [*grads, *half_scattered(far_piece, "z", z, across, beside, sent)]
        elif step == 1:
            held[1] = [scattered(*held[0][3:], "z", beside)]
        elif step == 2:
            sent = outgoing(piece_x, x, across, beside)
            held["sent"], part, _ = lax.optimization_barrier((sent, mg_2, block))
            held[2] = [*backward_of(1, pairs[1], backward_ins(part), (dk, dv), held[0][:3], 6)]
        else:
            held[3] = [*half_scattered(piece_x, "x", x, across, beside, held["sent"])]
        return held[step]

    after = scan_over_ctx(back, True, beside_scan)
    weight_grad = scattered(*held[3], "x", beside).T

    key_grad, value_grad = per_head(finish_kernel, heads, "ccccs", "cc", "finish")(
        keys, values, *held[2][1:3], after
    )
    dq = held[2][0]

    gate_sum = jnp.sum(after[:, ROWS - 1, :], axis=-1)
    gate_grad = gate_sum * gate * (1.0 - gate)
    return dq, key_grad, value_grad, weight_grad, gate_grad


def solution(mesh):
    in_specs = (
        P("ctx", "head"),
        P("ctx", "head"),
        P("ctx", "head"),
        P("head"),
        P("head", None),
        P("ctx", "head"),
    )
    out_specs = (P("ctx", "head"), P("ctx", "head"), P("ctx", "head"), P("ctx", "head"), P("head"))
    return jax.shard_map(
        on_device, mesh=mesh, in_specs=in_specs, out_specs=out_specs, check_vma=False
    )
```

```python
import functools
import math

import jax
import jax.numpy as jnp
from jax import lax
from jax.experimental import pallas as pl
from jax.experimental.pallas import tpu as pltpu
from jax.sharding import PartitionSpec as P

SEG = 1024
HEAD = 128
ROWS = 136
FORWARD_QB = 512
BACKWARD_QB = 256
MOST = SEG // 2
REST = SEG - MOST
STEP = 256
LIGHT = 2**16
VMEM_LIMIT = 60 * 2**20
MICROSECOND = 3_600_000

f32 = jnp.float32
bf16 = jnp.bfloat16
HIGH = lax.Precision.HIGH


def lifted(x):
    return jnp.where(x > 0, x + 1.0, jnp.exp(jnp.minimum(x, 0.0)))


def lifted_slope(x):
    return jnp.where(x > 0, 1.0, jnp.exp(jnp.minimum(x, 0.0)))


def halves(x):
    hi = x.astype(bf16)
    return hi, (x - hi.astype(f32)).astype(bf16)


def mm(a, b, contract):
    dims = ((contract[:1], contract[1:]), ((), ()))

    def one(x, y):
        return lax.dot_general(x, y, dims, preferred_element_type=f32)

    return one(a[0], b[0]) + (one(a[0], b[1]) + one(a[1], b[0]))


NN = (1, 0)
NT = (1, 1)
TN = (0, 0)


def dot(a, b, contract):
    return lax.dot_general(
        a, b, ((contract[:1], contract[1:]), ((), ())), preferred_element_type=f32
    )


def wide(pair):
    return jnp.concatenate(pair, axis=1)


def doubled(x):
    return jnp.concatenate([x, x], axis=1)


def scores_of(a_wide, b_hi_twice, b_lo):
    return dot(a_wide, b_hi_twice, NT) + dot(a_wide[:, :HEAD], b_lo, NT)


def times_wide(a, b_wide):
    both = dot(a[0], b_wide, NN)
    return both[:, :HEAD] + (both[:, HEAD:] + dot(a[1], b_wide[:, :HEAD], NN))


def tall_times(a_tall, b):
    both = dot(a_tall, b[0], NN)
    return both[:HEAD] + (both[HEAD:] + dot(a_tall[:HEAD], b[1], NN))


def update_kernel(k_ref, v_ref, out_ref):
    lk = lifted(k_ref[...])
    out_ref[0, :HEAD, :] = mm(halves(lk.T), halves(v_ref[...]), NN)
    out_ref[0, HEAD : HEAD + 1, :] = jnp.sum(lk, axis=0, keepdims=True)
    out_ref[0, HEAD + 1 :, :] = jnp.zeros((ROWS - HEAD - 1, HEAD), f32)


LOG2E = math.log2(math.e)
TEMPER = 1.0 / math.sqrt(HEAD)


def parts_of(qb, size):
    return ([(0, qb * size, False)] if qb else []) + [(qb * size, (qb + 1) * size, True)]


def causal(size):
    t = lax.broadcasted_iota(jnp.int32, (size, size), 0)
    return t <= lax.broadcasted_iota(jnp.int32, (size, size), 1)


def forward_kernel(q_ref, k_ref, v_ref, *refs):
    out_ref, lse_ref = refs[-2:]
    key = wide(halves(k_ref[...]))
    value_t = jnp.concatenate(halves(v_ref[...].T), axis=0)
    q_hi, q_lo = halves(q_ref[...] * (TEMPER * LOG2E))
    q_twice = doubled(q_hi)
    seen = causal(FORWARD_QB)
    for qb in range(SEG // FORWARD_QB):
        at = slice(qb * FORWARD_QB, (qb + 1) * FORWARD_QB)
        scores = []
        for low, high, own in parts_of(qb, FORWARD_QB):
            part = scores_of(key[low:high], q_twice[at], q_lo[at])
            scores.append(jnp.where(seen, part, -1e30) if own else part)
        top = functools.reduce(
            jnp.maximum, [jnp.max(part, axis=0, keepdims=True) for part in scores]
        )
        total, out_t = 0.0, 0.0
        for (low, high, _), part in zip(parts_of(qb, FORWARD_QB), scores):
            weights = jnp.exp2(part - top)
            total = total + jnp.sum(weights, axis=0, keepdims=True)
            out_t = out_t + tall_times(value_t[:, low:high], halves(weights))
        out_ref[at, :] = (out_t * (1.0 / total)).T
        lse_ref[0, :, at] = top + jnp.log2(total)


def mix_kernel(q_ref, local_ref, mem_ref, g_ref, hi_ref, lo_ref, memout_ref, lqd_ref):
    g = g_ref[0]
    lq = lifted(q_ref[...])
    norm = mem_ref[0, HEAD : HEAD + 1, :]
    denom = jnp.sum(lq * norm, axis=1, keepdims=True) + 1.0
    inverse = 1.0 / denom
    memory_out = mm(halves(lq), halves(mem_ref[0, :HEAD, :]), NN) * inverse
    memout_ref[...] = memory_out
    mixed = g * memory_out + (1.0 - g) * local_ref[...]
    hi_ref[...], lo_ref[...] = halves(mixed.T)
    lqd_ref[...] = lq * (inverse * g)


def add_weight_part(mixed, block, first, start, mine_ref, send_ref):
    part = mm(mixed, block, NN)
    groups = part.shape[1] // (2 * HEAD)
    for k in range(groups):
        even = part[:, 2 * k * HEAD : (2 * k + 1) * HEAD]
        odd = part[:, (2 * k + 1) * HEAD : (2 * k + 2) * HEAD]
        mine_ref[start + k] += jnp.where(first, even, odd)
        send_ref[start + k] += jnp.where(first, odd, even)


def block_kernel(at_ref, *refs, blocks, added, summed):
    refs = list(refs)

    def take(n):
        taken, refs[:] = refs[:n], refs[n:]
        return taken

    acc, block_refs, w_refs, mixed_refs = take(added), take(blocks), take(blocks), take(2)
    before, (out_ref,), by_core = take(summed), take(1), take(2)

    @pl.when(pl.program_id(0) == 0)
    def _():
        for n, w_ref in enumerate(w_refs):
            refs[2 * n][...], refs[2 * n + 1][...] = halves(w_ref[...])
        for n, ref in enumerate(by_core):
            ref[...] = before[n][...] if summed else jnp.zeros_like(ref)

    mixed = tuple(ref[...] for ref in mixed_refs)
    total = acc[0][...] if added else None
    start = 0
    for n, block_ref in enumerate(block_refs):
        block = halves(block_ref[...])
        product = mm(block, (refs[2 * n][...], refs[2 * n + 1][...]), NT)
        total = product if total is None else total + product
        add_weight_part(mixed, block, at_ref[blocks] == 0, start, *by_core)
        start += block_ref.shape[1] // (2 * HEAD)
    out_ref[...] = total


def tail_kernel(at_ref, *refs):
    acc_ref, a_ref, b_ref, wa_ref, wb_ref, lqd_ref, memout_ref, local_ref = refs[:8]
    mhi_ref, mlo_ref, *before = refs[8:-8]
    mg_ref, state_ref, mine_ref, send_ref, *w = refs[-8:]

    @pl.when(pl.program_id(0) == 0)
    def _():
        w[0][...], w[1][...] = halves(wa_ref[...])
        w[2][...], w[3][...] = halves(wb_ref[...])
        for n, ref in enumerate((state_ref, mine_ref, send_ref)):
            ref[...] = before[n][...] if before else jnp.zeros_like(ref)

    a, b = halves(a_ref[...]), halves(b_ref[...])
    mg = acc_ref[...] + mm(a, (w[0][...], w[1][...]), NT)
    mg = mg + mm(b, (w[2][...], w[3][...]), NT)
    mg_ref[...] = mg
    for h in range(state_ref.shape[0]):
        at = slice(h * HEAD, (h + 1) * HEAD)
        here, lqd, memory_out = mg[:, at], lqd_ref[:, at], memout_ref[:, at]
        state_ref[h, :HEAD, :] += mm(halves(lqd.T), halves(here), NN)
        r = jnp.sum(here * memory_out, axis=1, keepdims=True)
        state_ref[h, HEAD : HEAD + 1, :] -= jnp.sum(lqd * r, axis=0, keepdims=True)
        state_ref[h, HEAD + 1 : HEAD + 2, :] += jnp.sum(
            here * (memory_out - local_ref[:, at]), axis=0, keepdims=True
        )
    mixed, first = (mhi_ref[...], mlo_ref[...]), at_ref[2] == 0
    groups = a_ref.shape[1] // (2 * HEAD)
    add_weight_part(mixed, a, first, 0, mine_ref, send_ref)
    add_weight_part(mixed, b, first, groups, mine_ref, send_ref)


def rows_of(width, first=0):
    return pl.BlockSpec((STEP, width), lambda i, at: (i + first // STEP, 0))


def weight_specs(width, blocks):
    return [
        pl.BlockSpec(
            (width, block.shape[1]), lambda i, at, k=k: (0, at[k]), pipeline_mode=pl.Buffered(1)
        )
        for k, block in enumerate(blocks)
    ]


def tail_kernel(at_ref, *refs):
    acc_ref, a_ref, b_ref, wa_ref, wb_ref, lqd_ref, memout_ref, local_ref = refs[:8]
    mhi_ref, mlo_ref, *before = refs[8:-8]
    mg_ref, state_ref, mine_ref, send_ref, *w = refs[-8:]

    @pl.when(pl.program_id(0) == 0)
    def _():
        w[0][...], w[1][...] = halves(wa_ref[...])
        w[2][...], w[3][...] = halves(wb_ref[...])
        for n, ref in enumerate((state_ref, mine_ref, send_ref)):
            ref[...] = before[n][...] if before else jnp.zeros_like(ref)

    a, b = halves(a_ref[...]), halves(b_ref[...])
    mg = acc_ref[...] + mm(a, (w[0][...], w[1][...]), NT)
    mg = mg + mm(b, (w[2][...], w[3][...]), NT)
    mg_ref[...] = mg
    for h in range(state_ref.shape[0]):
        at = slice(h * HEAD, (h + 1) * HEAD)
        here, lqd, memory_out = mg[:, at], lqd_ref[:, at], memout_ref[:, at]
        state_ref[h, :HEAD, :] += mm(halves(lqd.T), halves(here), NN)
        r = jnp.sum(here * memory_out, axis=1, keepdims=True)
        state_ref[h, HEAD : HEAD + 1, :] -= jnp.sum(lqd * r, axis=0, keepdims=True)
        state_ref[h, HEAD + 1 : HEAD + 2, :] += jnp.sum(
            here * (memory_out - local_ref[:, at]), axis=0, keepdims=True
        )
    mixed, first = (mhi_ref[...], mlo_ref[...]), at_ref[2] == 0
    groups = a_ref.shape[1] // (2 * HEAD)
    add_weight_part(mixed, a, first, 0, mine_ref, send_ref)
    add_weight_part(mixed, b, first, groups, mine_ref, send_ref)


def rows_of(width, first=0):
    return pl.BlockSpec((STEP, width), lambda i, at: (i + first // STEP, 0))


def weight_specs(width, blocks):
    return [
        pl.BlockSpec(
            (width, block.shape[1]), lambda i, at, k=k: (0, at[k]), pipeline_mode=pl.Buffered(1)
        )
        for k, block in enumerate(blocks)
    ]


def tail_kernel(at_ref, *refs):
    acc_ref, a_ref, b_ref, wa_ref, wb_ref, lqd_ref, memout_ref, local_ref = refs[:8]
    mhi_ref, mlo_ref, *before = refs[8:-8]
    mg_ref, state_ref, mine_ref, send_ref, *w = refs[-8:]

    @pl.when(pl.program_id(0) == 0)
    def _():
        w[0][...], w[1][...] = halves(wa_ref[...])
        w[2][...], w[3][...] = halves(wb_ref[...])
        for n, ref in enumerate((state_ref, mine_ref, send_ref)):
            ref[...] = before[n][...] if before else jnp.zeros_like(ref)

    a, b = halves(a_ref[...]), halves(b_ref[...])
    mg = acc_ref[...] + mm(a, (w[0][...], w[1][...]), NT)
    mg = mg + mm(b, (w[2][...], w[3][...]), NT)
    mg_ref[...] = mg
    for h in range(state_ref.shape[0]):
        at = slice(h * HEAD, (h + 1) * HEAD)
        here, lqd, memory_out = mg[:, at], lqd_ref[:, at], memout_ref[:, at]
        state_ref[h, :HEAD, :] += mm(halves(lqd.T), halves(here), NN)
        r = jnp.sum(here * memory_out, axis=1, keepdims=True)
        state_ref[h, HEAD : HEAD + 1, :] -= jnp.sum(lqd * r, axis=0, keepdims=True)
        state_ref[h, HEAD + 1 : HEAD + 2, :] += jnp.sum(
            here * (memory_out - local_ref[:, at]), axis=0, keepdims=True
        )
    mixed, first = (mhi_ref[...], mlo_ref[...]), at_ref[2] == 0
    groups = a_ref.shape[1] // (2 * HEAD)
    add_weight_part(mixed, a, first, 0, mine_ref, send_ref)
    add_weight_part(mixed, b, first, groups, mine_ref, send_ref)


def rows_of(width, first=0):
    return pl.BlockSpec((STEP, width), lambda i, at: (i + first // STEP, 0))


def weight_specs(width, blocks):
    return [
        pl.BlockSpec(
            (width, block.shape[1]), lambda i, at, k=k: (0, at[k]), pipeline_mode=pl.Buffered(1)
        )
        for k, block in enumerate(blocks)
    ]


def tail_kernel(at_ref, *refs):
    acc_ref, a_ref, b_ref, wa_ref, wb_ref, lqd_ref, memout_ref, local_ref = refs[:8]
    mhi_ref, mlo_ref, *before = refs[8:-8]
    mg_ref, state_ref, mine_ref, send_ref, *w = refs[-8:]

    @pl.when(pl.program_id(0) == 0)
    def _():
        w[0][...], w[1][...] = halves(wa_ref[...])
        w[2][...], w[3][...] = halves(wb_ref[...])
        for n, ref in enumerate((state_ref, mine_ref, send_ref)):
            ref[...] = before[n][...] if before else jnp.zeros_like(ref)

    a, b = halves(a_ref[...]), halves(b_ref[...])
    mg = acc_ref[...] + mm(a, (w[0][...], w[1][...]), NT)
    mg = mg + mm(b, (w[2][...], w[3][...]), NT)
    mg_ref[...] = mg
    for h in range(state_ref.shape[0]):
        at = slice(h * HEAD, (h + 1) * HEAD)
        here, lqd, memory_out = mg[:, at], lqd_ref[:, at], memout_ref[:, at]
        state_ref[h, :HEAD, :] += mm(halves(lqd.T), halves(here), NN)
        r = jnp.sum(here * memory_out, axis=1, keepdims=True)
        state_ref[h, HEAD : HEAD + 1, :] -= jnp.sum(lqd * r, axis=0, keepdims=True)
        state_ref[h, HEAD + 1 : HEAD + 2, :] += jnp.sum(
            here * (memory_out - local_ref[:, at]), axis=0, keepdims=True
        )
    mixed, first = (mhi_ref[...], mlo_ref[...]), at_ref[2] == 0
    groups = a_ref.shape[1] // (2 * HEAD)
    add_weight_part(mixed, a, first, 0, mine_ref, send_ref)
    add_weight_part(mixed, b, first, groups, mine_ref, send_ref)


def rows_of(width, first=0):
    return pl.BlockSpec((STEP, width), lambda i, at: (i + first // STEP, 0))


def weight_specs(width, blocks):
    return [
        pl.BlockSpec(
            (width, block.shape[1]), lambda i, at, k=k: (0, at[k]), pipeline_mode=pl.Buffered(1)
        )
        for k, block in enumerate(blocks)
    ]


def onward_kernel(*refs):
    for source, target in zip(refs[:2], refs[2:]):
        target[...] = source[...]


def onward_of(block, column):
    rows, half, step = MOST, block.shape[1] // 2, MOST // 2

    def rows_from(first, column):
        return pl.BlockSpec((step, half), lambda i: (i + first // step, column))

    return pl.pallas_call(
        onward_kernel,
        grid=(rows // step,),
        in_specs=[rows_from(0, column), rows_from(MOST, column)],
        out_specs=[rows_from(0, 0)] * 2,
        out_shape=[jax.ShapeDtypeStruct((rows, half), f32)] * 2,
        compiler_params=pltpu.CompilerParams(vmem_limit_bytes=VMEM_LIMIT),
        cost_estimate=pl.CostEstimate(flops=LIGHT, bytes_accessed=LIGHT, transcendentals=0),
        name="onward",
    )(block, block)


def round_of(acc, blocks, places, out_weight, mixed, core, first=0, before=(), micros=0):
    rows = blocks[0].shape[0]
    width = out_weight.shape[0]
    n = len(blocks)
    groups = sum(block.shape[1] for block in blocks) // (2 * HEAD)
    at = jnp.stack([*places, core]).astype(jnp.int32)
    acc = [] if acc is None else [acc]
    by_core = pl.BlockSpec((groups, width, HEAD), lambda i, at: (0, 0, 0))
    by_core_shape = jax.ShapeDtypeStruct((groups, width, HEAD), f32)
    return pl.pallas_call(
        functools.partial(block_kernel, blocks=n, added=len(acc), summed=len(before)),
        grid_spec=pltpu.PrefetchScalarGridSpec(
            num_scalar_prefetch=1,
            grid=(rows // STEP,),
            in_specs=[rows_of(width, first) for _ in acc]
            + [rows_of(block.shape[1]) for block in blocks]
            + weight_specs(width, blocks)
            + [pl.BlockSpec((width, STEP), lambda i, at: (0, i + first // STEP))] * 2
            + [by_core] * len(before),
            out_specs=[rows_of(width, first)] + [by_core] * 2,
            scratch_shapes=[
                pltpu.VMEM((width, block.shape[1]), bf16) for block in blocks for _ in range(2)
            ],
        ),
        out_shape=[jax.ShapeDtypeStruct((SEG, width), f32)] + [by_core_shape] * 2,
        input_output_aliases={1: 0} if acc else {},
        compiler_params=pltpu.CompilerParams(vmem_limit_bytes=VMEM_LIMIT),
        cost_estimate=pl.CostEstimate(flops=LIGHT, bytes_accessed=LIGHT, transcendentals=0),
        name="round",
    )(at, *acc, *blocks, *([out_weight] * n), *mixed, *before)


def tail_of(second, acc, blocks, places, out_weight, mixed, core, whole, before):
    rows, deep = blocks[0].shape
    width = out_weight.shape[0]
    first = second * MOST
    by_core = deep // HEAD, width, HEAD
    sums = [(width // HEAD, ROWS, HEAD), by_core, by_core]
    sum_specs = [pl.BlockSpec(shape, lambda i, at: (0, 0, 0)) for shape in sums]
    return pl.pallas_call(
        tail_kernel,
        grid_spec=pltpu.PrefetchScalarGridSpec(
            num_scalar_prefetch=1,
            grid=(rows // STEP,),
            in_specs=[rows_of(width, first)]
            + [rows_of(deep)] * 2
            + weight_specs(width, blocks)
            + [rows_of(width, first)] * 3
            + [pl.BlockSpec((width, STEP), lambda i, at: (0, i + first // STEP))] * 2
            + sum_specs[: len(before)],
            out_specs=[rows_of(width), *sum_specs],
            scratch_shapes=[pltpu.VMEM((width, deep), bf16) for _ in range(4)],
        ),
        out_shape=[jax.ShapeDtypeStruct(shape, f32) for shape in [(rows, width), *sums]],
        compiler_params=pltpu.CompilerParams(vmem_limit_bytes=VMEM_LIMIT),
        cost_estimate=pl.CostEstimate(flops=LIGHT, bytes_accessed=LIGHT, transcendentals=0),
        name="tail",
    )(
        jnp.stack([*places, core]).astype(jnp.int32),
        acc, *blocks, out_weight, out_weight, *whole, *mixed, *before,
    )


def backward_kernel(*refs, first):
    q_ref, k_ref, v_ref, mg_ref, local_ref, memout_ref, lse_ref, mem_ref, g_ref = refs[:9]
    dq_ref, dk_ref, dv_ref = refs[-3:]
    g = g_ref[0]
    q = q_ref[...]
    mg = mg_ref[...]
    local_grad = (1.0 - g) * TEMPER * mg
    key = halves(k_ref[...])
    key_t = jnp.concatenate([key[0].T, key[1].T], axis=0)
    key = wide(key)
    value = wide(halves(v_ref[...]))
    query = halves(q * (TEMPER * LOG2E))
    q_twice, q_wide = doubled(query[0]), wide(query)
    grad = halves(local_grad)
    g_twice, g_wide = doubled(grad[0]), wide(grad)
    delta = jnp.sum((local_grad * local_ref[...]).T, axis=0, keepdims=True)
    lq = lifted(q)
    norm = mem_ref[0, HEAD : HEAD + 1, :]
    inverse = 1.0 / (jnp.sum(lq * norm, axis=1, keepdims=True) + 1.0)
    r = jnp.sum(mg * memout_ref[...], axis=1, keepdims=True)
    lift_grad = mm(halves(mg), halves(mem_ref[0, :HEAD, :].T), NN) - r * norm
    dq_ref[...] = lift_grad * (inverse * g) * lifted_slope(q)
    for ref, before in zip((dk_ref, dv_ref), refs[9:11] if first else (None, None)):
        ref[first:, :] = jnp.zeros(q.shape, f32)
        if first:
            ref[:first, :] = before[...]
    seen = causal(BACKWARD_QB)
    for qb in range(q.shape[0] // BACKWARD_QB):
        at = slice(qb * BACKWARD_QB, (qb + 1) * BACKWARD_QB)
        dq_t = 0.0
        for low, high, own in parts_of(qb + first // BACKWARD_QB, BACKWARD_QB):
            scores = scores_of(key[low:high], q_twice[at], query[1][at])
            if own:
                scores = jnp.where(seen, scores, -1e30)
            weights = jnp.exp2(scores - lse_ref[0, :, at])
            dp = scores_of(value[low:high], g_twice[at], grad[1][at])
            ds = halves(weights * (dp - delta[:, at]))
            dv_ref[low:high, :] += times_wide(halves(weights), g_wide[at])
            dk_ref[low:high, :] += times_wide(ds, q_wide[at])
            dq_t = dq_t + tall_times(key_t[:, low:high], ds)
        dq_ref[at, :] += dq_t.T
    if first:
        dk_ref[...] = dk_ref[...] * (1.0 / (TEMPER * LOG2E))
        dv_ref[...] = dv_ref[...] * (1.0 / TEMPER)


def backward_of(second, heads, ins, before, earlier, micros):
    width = ins[0].shape[1]
    low, count = heads

    def rows(n, at=0):
        return pl.BlockSpec((n, HEAD), lambda h: (at, h + low))

    def of_head(x, n=None, at=0):
        return pl.BlockSpec((1, x.shape[1], n or x.shape[2]), lambda h: (h + low, 0, at))

    size, at_part = (REST, MOST // REST) if second else (MOST, 0)
    here = rows(size, at_part)
    seen = rows(SEG if second else MOST)
    shapes = [(SEG, width)] + [(SEG if second else MOST, width)] * 2
    return pl.pallas_call(
        functools.partial(backward_kernel, first=second * MOST),
        grid=(count,),
        in_specs=[here, seen, seen, rows(size), here, here]
        + [of_head(ins[6], size, at_part), of_head(ins[7]), of_head(ins[8])]
        + [rows(MOST)] * len(before)
        + [pl.BlockSpec(memory_space=pl.ANY)] * len(earlier),
        out_specs=[here, seen, seen],
        out_shape=[jax.ShapeDtypeStruct(shape, f32) for shape in shapes],
        input_output_aliases={len(ins) + len(before) + i: i for i in range(len(earlier))},
        compiler_params=pltpu.CompilerParams(vmem_limit_bytes=VMEM_LIMIT),
        cost_estimate=pl.CostEstimate(
            flops=LIGHT, bytes_accessed=micros * MICROSECOND or LIGHT, transcendentals=0
        ),
        name="backward",
    )(*ins, *before, *earlier)


def forward_of(heads, ins, earlier):
    width = ins[0].shape[1]
    low, count = heads
    column = pl.BlockSpec((SEG, HEAD), lambda h: (0, h + low))
    line = pl.BlockSpec((1, 1, SEG), lambda h: (h + low, 0, 0))
    return pl.pallas_call(
        forward_kernel,
        grid=(count,),
        in_specs=[column] * 3 + [pl.BlockSpec(memory_space=pl.ANY)] * len(earlier),
        out_specs=[column, line],
        out_shape=[
            jax.ShapeDtypeStruct((SEG, width), f32),
            jax.ShapeDtypeStruct((width // HEAD, 1, SEG), f32),
        ],
        input_output_aliases={len(ins) + i: i for i in range(len(earlier))},
        compiler_params=pltpu.CompilerParams(vmem_limit_bytes=VMEM_LIMIT),
        cost_estimate=pl.CostEstimate(flops=LIGHT, bytes_accessed=LIGHT, transcendentals=0),
        name="forward",
    )(*ins, *earlier)


def finish_kernel(k_ref, v_ref, dk_ref, dv_ref, state_ref, kg_ref, vg_ref):
    key = k_ref[...]
    state = state_ref[0, :HEAD, :]
    norm = state_ref[0, HEAD : HEAD + 1, :]
    lift_grad = mm(halves(v_ref[...]), halves(state.T), NN) + norm
    kg_ref[...] = dk_ref[...] + lift_grad * lifted_slope(key)
    vg_ref[...] = dv_ref[...] + mm(halves(lifted(key)), halves(state), NN)


def columns():
    return pl.BlockSpec((SEG, HEAD), lambda h: (0, h))


def state():
    return pl.BlockSpec((1, ROWS, HEAD), lambda h: (h, 0, 0))


def row(width):
    return pl.BlockSpec((1, 1, width), lambda h: (h, 0, 0))


def per_head(kernel, heads, ins, outs, name):
    width = heads * HEAD
    kinds = {
        "c": (columns(), jax.ShapeDtypeStruct((SEG, width), f32)),
        "s": (state(), jax.ShapeDtypeStruct((heads, ROWS, HEAD), f32)),
        "g": (row(HEAD), jax.ShapeDtypeStruct((heads, 1, HEAD), f32)),
        "t": (
            pl.BlockSpec((HEAD, SEG), lambda h: (h, 0)),
            jax.ShapeDtypeStruct((width, SEG), bf16),
        ),
        "l": (row(SEG), jax.ShapeDtypeStruct((heads, 1, SEG), f32)),
    }
    return pl.pallas_call(
        kernel,
        grid=(heads,),
        in_specs=[kinds[i][0] for i in ins],
        out_specs=[kinds[o][0] for o in outs],
        out_shape=[kinds[o][1] for o in outs],
        compiler_params=pltpu.CompilerParams(vmem_limit_bytes=VMEM_LIMIT),
        cost_estimate=pl.CostEstimate(
            flops=LIGHT, bytes_accessed=LIGHT, transcendentals=0
        ),
        name=name,
    )


def ring(n, step):
    return [(i, (i + step) % n) for i in range(n)]


def grid_sizes():
    heads = lax.axis_size("head")
    return heads, lax.axis_size("ctx") // (2 * heads)


def place():
    xs, zs = grid_sizes()
    at = lax.axis_index("ctx")
    return at // (2 * zs), (at // 2) % zs, at % 2


def core_swap(block):
    n = lax.axis_size("ctx")
    return lax.ppermute(block, "ctx", [(i, i ^ 1) for i in range(n)])


def moved(block, axis, to):
    xs, zs = grid_sizes()
    pairs = []
    for x in range(xs):
        for z in range(zs):
            x_to, z_to = (to(x), z) if axis == "x" else (x, to(z))
            if x_to is not None and z_to is not None:
                for c in range(2):
                    pairs.append(((x * zs + z) * 2 + c, (x_to * zs + z_to) * 2 + c))
    return lax.ppermute(block, "ctx", pairs)


def scan_of_four(block, axis, at, later, beside_first, beside_second):
    near = beside_first(block, moved(block, axis, lambda i: i ^ 1))
    pair = block + near
    other = beside_second(pair, moved(pair, axis, lambda i: 3 - i))
    counts_near = (at % 2 == 0) if later else (at % 2 == 1)
    counts_other = (at < 2) if later else (at >= 2)
    return jnp.where(counts_near, near, 0.0) + jnp.where(counts_other, other, 0.0), pair + other


def scan_over_ctx(packed, later, work=None):
    xs, zs = grid_sizes()
    x, z, core = place()
    half = packed.shape[0] // 2
    first, second = packed[:half], packed[half:]
    is_first = core == 0
    mine = jnp.where(is_first, first, second)
    theirs = core_swap(jnp.where(is_first, second, first))
    chip = mine + theirs

    def beside_step(i):
        def tie(block, arrived):
            if work is None:
                return arrived
            done = work(i, block)
            arrived, *done[:] = lax.optimization_barrier((arrived, *done))
            return arrived

        return tie

    before_z, total_z = scan_of_four(chip, "z", z, later, beside_step(0), beside_step(1))
    before_x, total = scan_of_four(
        total_z, "x", x, later, beside_step(2), beside_step(3)
    )
    outside = before_z + before_x
    counts_other = is_first if later else jnp.logical_not(is_first)
    for_me = outside + jnp.where(counts_other, theirs, 0.0)
    for_other = outside + jnp.where(counts_other, 0.0, mine)
    row = lax.broadcasted_iota(jnp.int32, (1, ROWS, 1), 1)
    totals = jnp.where(row == ROWS - 1, total[:, HEAD + 1 : HEAD + 2, :], 0.0)
    for_me, for_other = for_me + totals, for_other + totals
    swapped = core_swap(for_other)
    low = jnp.where(is_first, for_me, swapped)
    high = jnp.where(is_first, swapped, for_me)
    return jnp.concatenate([low, high], axis=0)


def across(i):
    return 3 - i


def beside(i):
    return i ^ 1


def outgoing(piece, at, first, second):
    far = first(at)
    return jnp.stack([piece(far), piece(second(far))])


def half_scattered(piece, axis, at, first, second, sent=None):
    sent = outgoing(piece, at, first, second) if sent is None else sent
    came = moved(sent, axis, first)
    return piece(at) + came[0], piece(second(at)) + came[1]


def scattered(kept, passed, axis, second):
    return kept + moved(passed, axis, second)


def at_place(pieces, i):
    return lax.dynamic_index_in_dim(pieces, i, 0, keepdims=False)


def on_device(queries, keys, values, gate_logit, out_weight, out_grad):
    heads = gate_logit.shape[0]
    width = heads * HEAD
    hs = lax.axis_size("head")
    head = lax.axis_index("head")
    xs, zs = grid_sizes()
    x, z, core = place()
    rows, cols = out_grad.shape


    def up(block):
        return lax.ppermute(block, "head", ring(hs, 1))

    def down(block):
        return lax.ppermute(block, "head", ring(hs, -1))

    left, right = up(out_grad), down(out_grad)

    gate = jax.nn.sigmoid(gate_logit)
    g = jnp.broadcast_to(gate[:, None, None], (heads, 1, HEAD))

    (packed,) = per_head(update_kernel, heads, "cc", "s", "update")(keys, values)
    forwards = []

    def forward(step, block):
        if step % 2 == 0:
            forwards[:] = forward_of((step, heads // 2), (queries, keys, values), forwards)
        return forwards

    before = scan_over_ctx(packed, False, forward)
    local_out, lse = forwards
    *mixed, memory_out, lqd = per_head(mix_kernel, heads, "ccsg", "ttcc", "mix")(
        queries, local_out, before, g
    )

    def block_at(distance):
        return (head + hs - distance) % hs

    own_at, left_at, far_at, right_at = (block_at(d) for d in range(4))
    add = functools.partial(round_of, out_weight=out_weight, mixed=mixed, core=core)

    def chip_piece(mine, came, start=0):
        return lambda i: at_place(mine, start + i) + at_place(came, start + i)

    mg, mine_own, send_own = add(None, [out_grad], [own_at])
    came_own = core_swap(send_own)
    own_parts = half_scattered(chip_piece(mine_own, came_own), "z", z, across, beside)
    left, right, *own_parts = lax.optimization_barrier((left, right, *own_parts))
    left_on, right_on = onward_of(left, 0), onward_of(right, 1)
    far_1 = up(left_on[0]), down(right_on[0])
    far_2 = up(left_on[1]), down(right_on[1])

    mg, mine_sides, send_sides = add(mg, [left, right], [left_at, right_at])
    sum_own = scattered(*own_parts, "z", beside)
    *far_1, mine_sides, send_sides, sum_own = lax.optimization_barrier(
        (*far_1, mine_sides, send_sides, sum_own)
    )
    came_sides = core_swap(send_sides)
    far_places = [2 * far_at, 2 * far_at + 1]
    tail = functools.partial(
        tail_of, places=far_places, out_weight=out_weight, mixed=mixed, core=core,
        whole=(lqd, memory_out, local_out),
    )
    mg_1, *far_sums = tail(0, mg, far_1, before=())
    attended = queries, keys, values

    def backward_ins(part):
        return (*attended, part, local_out, memory_out, lse, before, g)

    mg_1, came_sides = lax.optimization_barrier((mg_1, came_sides))
    left_parts = half_scattered(chip_piece(mine_sides, came_sides), "z", z, across, beside)
    right_parts = half_scattered(chip_piece(mine_sides, came_sides, zs), "z", z, beside, across)
    early = backward_of(0, (0, heads), backward_ins(mg_1), (), (), 0)
    *far_2, dq, dk, dv, left_kept, left_passed, right_kept, right_passed = (
        lax.optimization_barrier((*far_2, *early, *left_parts, *right_parts))
    )
    mg_2, back, mine_far, send_far = tail(1, mg, far_2, before=far_sums)
    sum_left = scattered(left_kept, left_passed, "z", beside)
    sum_right = scattered(right_kept, right_passed, "z", across)
    back, send_far, sum_left, sum_right = lax.optimization_barrier(
        (back, send_far, sum_left, sum_right)
    )
    came_far = core_swap(send_far)

    pairs = [(0, heads // 2), (heads // 2, heads // 2)]
    held = {}

    def piece_x(i):
        parts = jnp.stack([sum_own, sum_left, held[1][0], sum_right])
        return at_place(parts, (head + hs - i) % hs)

    def beside_scan(step, block):
        if step == 0:
            part, came, _ = lax.optimization_barrier((mg_2, came_far, block))
            far_piece = chip_piece(mine_far, came)
            sent = outgoing(far_piece, z, across, beside)
            sent, part = lax.optimization_barrier((sent, part))
            grads = backward_of(1, pairs[0], backward_ins(part), (dk, dv), [dq], 6)
            held[0] = [*grads, *half_scattered(far_piece, "z", z, across, beside, sent)]
        elif step == 1:
            held[1] = [scattered(*held[0][3:], "z", beside)]
        elif step == 2:
            sent = outgoing(piece_x, x, across, beside)
            held["sent"], part, _ = lax.optimization_barrier((sent, mg_2, block))
            held[2] = [*backward_of(1, pairs[1], backward_ins(part), (dk, dv), held[0][:3], 6)]
        else:
            held[3] = [*half_scattered(piece_x, "x", x, across, beside, held["sent"])]
        return held[step]

    after = scan_over_ctx(back, True, beside_scan)
    weight_grad = scattered(*held[3], "x", beside).T

    key_grad, value_grad = per_head(finish_kernel, heads, "ccccs", "cc", "finish")(
        keys, values, *held[2][1:3], after
    )
    dq = held[2][0]

    gate_sum = jnp.sum(after[:, ROWS - 1, :], axis=-1)
    gate_grad = gate_sum * gate * (1.0 - gate)
    return dq, key_grad, value_grad, weight_grad, gate_grad


def solution(mesh):
    in_specs = (
        P("ctx", "head"),
        P("ctx", "head"),
        P("ctx", "head"),
        P("head"),
        P("head", None),
        P("ctx", "head"),
    )
    out_specs = (P("ctx", "head"), P("ctx", "head"), P("ctx", "head"), P("ctx", "head"), P("head"))
    return jax.shard_map(
        on_device, mesh=mesh, in_specs=in_specs, out_specs=out_specs, check_vma=False
    )
```
